32 devices in a mesh: ctx: 4 (over x, core), fsdp: 8 (over z, y).
Axes of the slice: x: 2, y: 2, z: 4, core: 2. Of those that a mesh axis runs over, the one named last changes fastest.
Arguments:
- hidden_in: bfloat16 [8, 1024, 1024], P('fsdp', 'ctx'), may hold values from -6 to 6
- positions: int32 [8, 1024], P('fsdp', 'ctx'), may hold values from 0 to 1023, as said below
- out_grad: bfloat16 [8, 1024, 1024], P('fsdp', 'ctx'), may hold values from -6 to 6
- attn_gain: bfloat16 [1024], P('fsdp'), may hold values from 0.5 to 1.5
- attn_shift: bfloat16 [1024], P('fsdp'), may hold values from -4 to 4
- in_weight: bfloat16 [1024, 3072], P('fsdp'), may hold values from -0.25 to 0.25
- in_bias: bfloat16 [3072], P('fsdp'), may hold values from -4 to 4
- proj_weight: bfloat16 [1024, 1024], P('fsdp'), may hold values from -1 to 1
- proj_bias: bfloat16 [1024], P('fsdp'), may hold values from -4 to 4
- mlp_gain: bfloat16 [1024], P('fsdp'), may hold values from 0.5 to 1.5
- mlp_shift: bfloat16 [1024], P('fsdp'), may hold values from -4 to 4
- up_weight: bfloat16 [1024, 4096], P('fsdp'), may hold values from -0.1875 to 0.1875
- up_bias: bfloat16 [4096], P('fsdp'), may hold values from -4 to 4
- down_weight: bfloat16 [4096, 1024], P('fsdp'), may hold values from -0.125 to 0.125
- down_bias: bfloat16 [1024], P('fsdp'), may hold values from -4 to 4
Outputs:
- block_out: bfloat16 [8, 1024, 1024], P('fsdp', 'ctx')
- input_grad: float32 [8, 1024, 1024], P('fsdp', 'ctx')
- attn_gain_grad: float32 [1024], P('fsdp')
- attn_shift_grad: float32 [1024], P('fsdp')
- in_weight_grad: float32 [1024, 3072], P('fsdp')
- in_bias_grad: float32 [3072], P('fsdp')
- proj_weight_grad: float32 [1024, 1024], P('fsdp')
- proj_bias_grad: float32 [1024], P('fsdp')
- mlp_gain_grad: float32 [1024], P('fsdp')
- mlp_shift_grad: float32 [1024], P('fsdp')
- up_weight_grad: float32 [1024, 4096], P('fsdp')
- up_bias_grad: float32 [4096], P('fsdp')
- down_weight_grad: float32 [4096, 1024], P('fsdp')
- down_bias_grad: float32 [1024], P('fsdp')
The draws below stay inside these ranges and needn't reach their ends.
Inputs may be any that keep to these rules, and one draw needn't show every extreme that they name: Row s lists the positions in sequence s of the tokens stored along it: a permutation of 0 to 1023 made of runs of 128 consecutive positions that start at multiples of 128. The 256 entries held by one index of ctx are two such runs, blocks b and 7 - b for some b, in either order.
All inputs are finite; a program needn't handle non-finite values.
Results may differ from the reference program's by a relative error of at most 0.017.
Values may be sent and summed in bfloat16 or wider, within the bound.
A program may use at most 192 MiB of HBM per device.

```python
import jax
import jax.numpy as jnp
from jax import lax

D = 1024
HEADS = 16
HEAD_DIM = 64
ROT = 16
FF = 4096
BLK = 128
SEQ = 1024
NSEQ = 8


def draw_positions(key, part):
    key = jax.random.fold_in(key, 7)
    block_count = SEQ // BLK
    pair_count = block_count // 2
    order_key, flip_key = jax.random.split(key)
    orders = jax.vmap(lambda row_key: jax.random.permutation(row_key, pair_count))(jax.random.split(order_key, NSEQ))
    flip_bits = jax.random.randint(flip_key, (NSEQ, pair_count), 0, 2)
    leading = jnp.where(flip_bits == 0, orders, block_count - 1 - orders)
    second = block_count - 1 - leading
    blocks = jnp.stack([leading, second], axis=-1).reshape(NSEQ, block_count)
    offsets = jnp.arange(BLK, dtype=jnp.int32)
    return (blocks[:, :, None] * BLK + offsets[None, None, :]).reshape(NSEQ, SEQ).astype(jnp.int32)


def shard_levels(key, extent, pieces, low, high):
    factor_of, own = 1.0, jax.random.fold_in(key, 6)
    for axis_at, blocks in pieces:
        steps = jnp.exp(jax.random.uniform(jax.random.fold_in(own, axis_at), (blocks,), jnp.float32, low / len(pieces), high / len(pieces)))
        factor_of = factor_of * jnp.repeat(steps, extent[axis_at] // blocks).reshape([-1 if axis == axis_at else 1 for axis in range(len(extent))])
    return factor_of


def noise(stream_key, extent, scale, reach, pieces=(), kind=jnp.bfloat16):
    array = jax.random.normal(stream_key, extent, jnp.float32) * scale
    if len(pieces) > 0:
        array = shard_levels(stream_key, extent, pieces, -0.22, 0.18) * array
    return jnp.clip(array, min=-reach, max=reach).astype(kind)


def setup_inputs(seed: int = 0) -> dict:
    keys = jax.random.split(jax.random.key(seed), 16)
    hidden_in = noise(keys[0], (NSEQ, SEQ, D), 1.0, 6.0, ((0, 8), (1, 4)))
    positions = draw_positions(jax.random.fold_in(keys[15], 71), 0)
    out_grad = noise(keys[2], (NSEQ, SEQ, D), 1.0, 6.0, ((0, 8), (1, 4)))
    attn_gain = jnp.clip(1.0 + 0.1 * jax.random.normal(keys[3], (D,), jnp.float32), 0.5, 1.5).astype(jnp.bfloat16)
    attn_shift = noise(keys[4], (D,), 0.3, 4.0, ((0, 8),))
    in_weight = noise(keys[5], (D, 3 * D), (D // 2) ** -0.5, 0.25, ((0, 8),))
    in_bias = noise(keys[6], (3 * D,), 0.3, 4.0, ((0, 8),))
    proj_weight = noise(keys[7], (D, D), (max(D // 32, 1)) ** -0.5, 1.0, ((0, 8),))
    proj_bias = noise(keys[8], (D,), 0.3, 4.0, ((0, 8),))
    mlp_gain = jnp.clip(1.0 + 0.1 * jax.random.normal(keys[9], (D,), jnp.float32), 0.5, 1.5).astype(jnp.bfloat16)
    mlp_shift = noise(keys[10], (D,), 0.3, 4.0, ((0, 8),))
    up_weight = noise(keys[11], (D, FF), D ** -0.5, 0.1875, ((0, 8),))
    up_bias = noise(keys[12], (FF,), 0.3, 4.0, ((0, 8),))
    down_weight = noise(keys[13], (FF, D), (FF // 2) ** -0.5, 0.125, ((0, 8),))
    down_bias = noise(keys[14], (D,), 0.3, 4.0, ((0, 8),))
    return {"hidden_in": hidden_in, "positions": positions, "out_grad": out_grad, "attn_gain": attn_gain, "attn_shift": attn_shift, "in_weight": in_weight, "in_bias": in_bias, "proj_weight": proj_weight, "proj_bias": proj_bias, "mlp_gain": mlp_gain, "mlp_shift": mlp_shift, "up_weight": up_weight, "up_bias": up_bias, "down_weight": down_weight, "down_bias": down_bias}


exact_mode = lax.Precision.HIGHEST

@jax.custom_vjp
def low(v):
    return lax.optimization_barrier(v.astype(jnp.bfloat16)).astype(jnp.float32)

@jax.custom_vjp
def low_back(v):
    return v

def low_keep(v):
    return (low(v), None)

def low_pass(kept, grad):
    return (grad,)

def back_keep(v):
    return (v, None)

def back_low(kept, grad):
    return (low(grad),)
low.defvjp(low_keep, low_pass)
low_back.defvjp(back_keep, back_low)

def layer_norm(states, scaling, offset):
    center = states - lax.optimization_barrier(jnp.mean(states, axis=-1, keepdims=True))
    spread = lax.optimization_barrier(jnp.mean(center * center, axis=-1, keepdims=True))
    return center * lax.rsqrt(spread + 1e-05) * scaling + offset

def rotary_tables(places, rot_dims):
    halves = rot_dims // 2
    frequency = jnp.power(10000.0, -2.0 * jnp.arange(halves, dtype=jnp.float32) / rot_dims)
    angles = places.astype(jnp.float32)[:, None] * frequency[None, :]
    return (jnp.cos(angles)[:, None, :], jnp.sin(angles)[:, None, :])

def rotate(states, cosine, sine_part, rot_dims):
    halves = rot_dims // 2
    leading = states[..., :halves]
    trailing = states[..., halves:rot_dims]
    return jnp.concatenate([leading * cosine - trailing * sine_part, trailing * cosine + leading * sine_part, states[..., rot_dims:]], axis=-1)

def one_sequence(params, states, places):
    attn_gain, attn_shift, in_weight, in_bias, proj_weight, proj_bias, mlp_gain, mlp_shift, up_weight, up_bias, down_weight, down_bias = params
    model_width = states.shape[-1]
    length = states.shape[0]
    normed = low(layer_norm(states, attn_gain, attn_shift))
    joined = low_back(jnp.dot(normed, in_weight, precision=exact_mode) + in_bias)
    cosine, sine_part = rotary_tables(places, ROT)
    query = low(rotate(joined[:, :model_width].reshape(length, HEADS, HEAD_DIM), cosine, sine_part, ROT))
    key_heads = low(rotate(joined[:, model_width:2 * model_width].reshape(length, HEADS, HEAD_DIM), cosine, sine_part, ROT))
    value_heads = low(joined[:, 2 * model_width:].reshape(length, HEADS, HEAD_DIM))
    scores = low_back(jnp.einsum('qhd,khd->hqk', query, key_heads, precision=exact_mode) * HEAD_DIM ** (-0.5))
    allowed = places[None, :] <= places[:, None]
    scores = jnp.where(allowed[None], scores, -1e+30)
    row_max = lax.optimization_barrier(jnp.max(scores, axis=-1, keepdims=True))
    unnormed = jnp.exp(scores - row_max)
    probability = low(unnormed / lax.optimization_barrier(jnp.sum(unnormed, axis=-1, keepdims=True)))
    attended = low(low_back(jnp.einsum('hqk,khd->qhd', probability, value_heads, precision=exact_mode).reshape(length, model_width)))
    branch_attn = jnp.dot(attended, proj_weight, precision=exact_mode) + proj_bias
    normed_mlp = low(layer_norm(states, mlp_gain, mlp_shift))
    lifted = low_back(jnp.dot(normed_mlp, up_weight, precision=exact_mode) + up_bias)
    activated = low(jax.nn.gelu(lifted, approximate=False))
    branch_mlp = jnp.dot(activated, down_weight, precision=exact_mode) + down_bias
    return states + branch_attn + branch_mlp

def reference(hidden_in, positions, out_grad, attn_gain, attn_shift, in_weight, in_bias, proj_weight, proj_bias, mlp_gain, mlp_shift, up_weight, up_bias, down_weight, down_bias):
    params = tuple((weight_part.astype(jnp.float32) for weight_part in (attn_gain, attn_shift, in_weight, in_bias, proj_weight, proj_bias, mlp_gain, mlp_shift, up_weight, up_bias, down_weight, down_bias)))
    states = hidden_in.astype(jnp.float32)
    cotangent = out_grad.astype(jnp.float32)

    def forward(weights, inputs):

        def per_sequence(sequence_pair):
            return jax.checkpoint(one_sequence)(weights, sequence_pair[0], sequence_pair[1])
        return lax.map(per_sequence, (inputs, positions))
    outputs, pullback = jax.vjp(forward, params, states)
    param_grads, input_grad = pullback(cotangent)
    return (outputs.astype(jnp.bfloat16), input_grad, param_grads[0], param_grads[1], param_grads[2], param_grads[3], param_grads[4], param_grads[5], param_grads[6], param_grads[7], param_grads[8], param_grads[9], param_grads[10], param_grads[11])
```

```python
import math

import jax
import jax.numpy as jnp
import numpy as np
from jax import lax
from jax.experimental import pallas as pl
from jax.experimental.pallas import tpu as pltpu
from jax.sharding import PartitionSpec as P

HEADS = 16
HEAD_DIM = 64
ROT = 16
BLK = 128
EPS = 1e-05
MESH = pl.DeviceIdType.MESH
BF = jnp.bfloat16
F32 = jnp.float32
IN, PROJ, UP, DOWN, VEC = range(5)
VROWS = 16
BOTH1 = (((1,), (1,)), ((), ()))
BOTH0 = (((0,), (0,)), ((), ()))


def dot(a, b):
    return jnp.dot(a, b, preferred_element_type=F32)


def dot11(a, b):
    return lax.dot_general(a, b, BOTH1, preferred_element_type=F32)


def dot00(a, b):
    return lax.dot_general(a, b, BOTH0, preferred_element_type=F32)


def mult(value, of):
    return pl.multiple_of(value, of)


def both(*conds):
    out = conds[0]
    for cond in conds[1:]:
        out = jnp.logical_and(out, cond)
    return out


class Sizes:
    def __init__(self, tokens, width, hidden, nctx, nshard):
        self.T = tokens
        self.N = tokens * nctx
        self.D = width
        self.H = hidden // nctx
        self.G = width // nctx
        self.nctx = nctx
        self.F = nshard
        self.A = nctx
        self.B = nshard // nctx
        self.R = width // nshard
        self.hc = hidden // nshard // nctx
        self.packed = self.R % 128 == 0 and self.hc % 128 == 0
        self.rows = (self.R, self.R, self.R, self.hc, VROWS)
        self.cols = (3 * self.G, width, self.H, width, 128)
        self.units = (self.F, self.B, self.F, self.F, self.F)
        self.types = (BF, BF, BF, BF, F32)
        self.kinds = (IN, PROJ, UP, DOWN) + ((VEC,) if self.packed else ())
        self.NY = 1 if self.B == 2 else self.B + 1


def scratch_plan(s):
    N, D, G, H = s.N, s.D, s.G, s.H
    vm = pltpu.VMEM
    dma = pltpu.SemaphoreType.DMA
    plan = dict(
        Xs=vm((N, D), BF),
        Gs=vm((N, D), BF),
        Bs=vm((s.nctx * 8, D), jnp.int32),
        cos_st=vm((N, 128), F32),
        sin_st=vm((N, 128), F32),
        nb=vm((N, D), BF),
        A1=vm((N, D), BF),
        A2=vm((N, D), BF),
        S=vm((N, 4 * G), BF),
        dq=vm((N, G), F32),
        dk=vm((N, G), F32),
        dv=vm((N, G), F32),
        att_st=vm((N, G), BF),
        dj=vm((N, 3 * G), BF),
        act=vm((N, H), BF),
        gp=vm((N, H), BF),
        dl=vm((N, H), BF),
        Po=vm((N, D), BF),
        Pc=vm((N, D), BF),
        r1=vm((2, 2 * s.T, D), BF),
        r2=vm((2, s.T, D), BF),
        cs=vm((8, D), F32),
        xo=vm((s.T, D), BF),
        xg=vm((s.T, D), F32),
    )
    if s.packed:
        plan["vecs"] = vm((8, D), F32)
        plan["FV"] = vm((s.nctx * VROWS, 128), F32)
        plan["vtot"] = vm((VROWS, 128), F32)
    for kind in s.kinds:
        name = "ipudv"[kind]
        u, r, cl = s.units[kind], s.rows[kind], s.cols[kind]
        dt = s.types[kind]
        per = 1 if kind == PROJ else s.A
        plan["W" + name] = vm((u * r, cl), dt)
        plan["G" + name] = vm((u * r, cl), dt)
        plan["Y" + name] = vm((s.NY * per * r, cl), dt)
        plan["Z" + name] = vm(((2 if kind == PROJ else s.A + 1) * r, cl), dt)
    plan.update(
        ag_s=dma((5, 4, s.F)),
        ag_r=dma((5, s.F)),
        xa_s=dma((3, 3)),
        xa_r=dma((3, s.nctx)),
        ry_s=dma((5, 2, s.F)),
        ry_r=dma((5, 2, s.F)),
        rz_s=dma((5, 2, s.A)),
        rz_r=dma((5, 2, s.A)),
        cr_s=dma((2, 3)),
        cr_r=dma((2, 3)),
        fa_s=dma((5, 3, s.F)),
        fa_r=dma((5, 3, s.F)),
        fa_l=dma((5, s.F)),
        loc=dma((16,)),
        loc_i=dma((3,)),
        loc_u=dma((s.F,)),
    )
    return plan


def kernel_body(s, names, *refs):
    n = dict(zip(names, refs))
    T, N, D, G, H, A, B, R = s.T, s.N, s.D, s.G, s.H, s.A, s.B, s.R
    c = lax.axis_index("ctx")
    f = lax.axis_index("fsdp")
    zi, yi = f // B, f % B
    sib_c = c + 1 - 2 * (c % 2)
    xn_c = (c + s.nctx // 2) % s.nctx
    xs_c = (sib_c + s.nctx // 2) % s.nctx
    sib, xn = (sib_c, f), (xn_c, f)
    edge = (zi < A - 1, zi > 0, yi < B - 1, yi > 0)
    hop = ((c, f + B), (c, f - B), (c, f + 1), (c, f - 1))

    def when(cond, fn):
        pl.when(cond)(fn)

    def rcopy(src, dst, ssem, rsem, dev):
        return pltpu.make_async_remote_copy(
            src_ref=src, dst_ref=dst, send_sem=ssem, recv_sem=rsem, device_id=dev, device_id_type=MESH
        )

    def rows(ref, start, size):
        return ref.at[pl.ds(mult(start, size), size)]

    bar = pltpu.get_barrier_semaphore()
    for dev in (sib, xn):
        pl.semaphore_signal(bar, inc=1, device_id=dev, device_id_type=MESH)
    for d in range(4):
        when(
            edge[d],
            lambda d=d: pl.semaphore_signal(bar, inc=1, device_id=hop[d], device_id_type=MESH),
        )
    count = 2 + sum(jnp.where(e, 1, 0) for e in edge)
    pl.semaphore_wait(bar, count)

    W = [n.get("W" + x) for x in "ipudv"]

    def has(kind, oz):
        return (oz == c) if kind == PROJ else (oz == oz)

    def wunit(ref, kind, oz, oy):
        r = s.rows[kind]
        at = oy if kind == PROJ else oz * B + oy
        return rows(ref, at * r, r)

    def ag_copy(kind, oz, oy, d):
        u = wunit(W[kind], kind, oz, oy)
        at = oz * B + oy
        return rcopy(u, u, n["ag_s"].at[kind, d, at], n["ag_r"].at[kind, at], hop[d])

    def ag_send(kind, oz, oy, dirs, cond):
        for d in dirs:
            when(both(cond, edge[d]), lambda d=d: ag_copy(kind, oz, oy, d).start())

    def ag_start(kind):
        ag_send(kind, zi, yi, (0, 1, 2, 3), has(kind, zi))

    def ag_z(kind, t):
        for sign, d in ((-1, 0), (1, 1)):
            oz = zi + sign * (1 + t)
            cond = both(oz >= 0, oz < A, has(kind, oz))

            def go(oz=oz, d=d):
                ag_copy(kind, oz, yi, d).wait_recv()
                for dd in (d, 2, 3):
                    when(edge[dd], lambda dd=dd: ag_copy(kind, oz, yi, dd).start())

            when(cond, go)

    def ag_y(kind):
        for t in range(B - 1):
            for zz in [c] if kind == PROJ else list(range(A)):
                for sign, d in ((-1, 2), (1, 3)):
                    oy = yi + sign * (1 + t)

                    def go(oy=oy, d=d, zz=zz):
                        ag_copy(kind, zz, oy, d).wait_recv()
                        if B > 2:
                            when(edge[d], lambda: ag_copy(kind, zz, oy, d).start())

                    when(both(oy >= 0, oy < B), go)

    def ag_drain(kind):
        for oz in [c] if kind == PROJ else list(range(A)):
            when(both(oz <= zi, edge[0]), lambda oz=oz: ag_copy(kind, oz, yi, 0).wait_send())
            when(both(oz >= zi, edge[1]), lambda oz=oz: ag_copy(kind, oz, yi, 1).wait_send())
            for oy in range(B):
                when(both(oy <= yi, edge[2]), lambda oz=oz, oy=oy: ag_copy(kind, oz, oy, 2).wait_send())
                when(both(oy >= yi, edge[3]), lambda oz=oz, oy=oy: ag_copy(kind, oz, oy, 3).wait_send())

    XA = ((n["Xs"], T), (n["Gs"], T), (n["Bs"], 8))

    def xa_copy(arr, slot, which):
        ref, r = XA[arr]
        u = rows(ref, slot * r, r)
        return rcopy(u, u, n["xa_s"].at[arr, which], n["xa_r"].at[arr, slot], (xn, sib)[which != 0])

    def xa_start(arr):
        xa_copy(arr, c, 0).start()
        xa_copy(arr, c, 1).start()

    def xa_wait(arr, slot):
        xa_copy(arr, slot, 0).wait_recv()

    def xa_fwd(arr):
        xa_wait(arr, xn_c)
        xa_copy(arr, xn_c, 2).start()

    def xa_drain(arr):
        xa_copy(arr, c, 0).wait_send()
        xa_copy(arr, c, 1).wait_send()
        xa_copy(arr, xn_c, 2).wait_send()

    GR = [n.get("G" + x) for x in "ipudv"]
    YB = [n.get("Y" + x) for x in "ipudv"]
    ZB = [n.get("Z" + x) for x in "ipudv"]

    def add_into(dst, src):
        dst[...] = (dst[...].astype(F32) + src[...].astype(F32)).astype(dst.dtype)

    def ry_copy(kind, zz, target, d, receiver):
        r = s.rows[kind]
        per = 1 if kind == PROJ else A
        at = 0 if kind == PROJ else zz
        if B == 2:
            slot = 0
        elif d == 0:
            slot = target
        else:
            slot = jnp.where(receiver == target, B, target)
        return rcopy(
            wunit(GR[kind], kind, zz, target),
            rows(YB[kind], (slot * per + at) * r, r),
            n["ry_s"].at[kind, d, zz * B + target],
            n["ry_r"].at[kind, d, zz * B + target],
            hop[2 + d],
        )

    def ry_dst(kind, zz, target, d):
        r = s.rows[kind]
        per = 1 if kind == PROJ else A
        at = 0 if kind == PROJ else zz
        if B == 2:
            slot = 0
        elif d == 0:
            slot = target
        else:
            slot = jnp.where(yi == target, B, target)
        return rows(YB[kind], (slot * per + at) * r, r)

    def ry_zz(kind):
        return [c] if kind == PROJ else [A - 1, 0] + list(range(A - 2, 0, -1))

    def ry_send(kind, t, zz):
        hi, lo = B - 1 - t, t
        when(yi == 0, lambda: ry_copy(kind, zz, hi, 0, yi + 1).start())
        when(yi == B - 1, lambda: ry_copy(kind, zz, lo, 1, yi - 1).start())

    def ry_recv(kind, t, zz):
        hi, lo = B - 1 - t, t
        for target, d, cond, onward in (
            (hi, 0, both(yi > 0, yi <= hi), both(yi > 0, yi < hi)),
            (lo, 1, both(yi < B - 1, yi >= lo), both(yi < B - 1, yi > lo)),
        ):

            def go(target=target, d=d):
                ry_copy(kind, zz, target, d, yi).wait_recv()
                add_into(wunit(GR[kind], kind, zz, target), ry_dst(kind, zz, target, d))

            when(cond, go)
            if B > 2:
                when(
                    onward,
                    lambda target=target, d=d: ry_copy(
                        kind, zz, target, d, yi + 1 - 2 * d
                    ).start(),
                )

    def ry_drain(kind):
        for zz in [c] if kind == PROJ else list(range(A)):
            for target in range(B):
                when(yi < target, lambda zz=zz, target=target: ry_copy(kind, zz, target, 0, yi + 1).wait_send())
                when(yi > target, lambda zz=zz, target=target: ry_copy(kind, zz, target, 1, yi - 1).wait_send())

    def rz_slot(kind, target, d, receiver):
        r = s.rows[kind]
        if kind == PROJ:
            slot = d
        elif d == 0:
            slot = target
        else:
            slot = jnp.where(receiver == target, A, target)
        return rows(ZB[kind], slot * r, r)

    def rz_copy(kind, target, d, receiver):
        return rcopy(
            wunit(GR[kind], kind, target, yi),
            rz_slot(kind, target, d, receiver),
            n["rz_s"].at[kind, d, target],
            n["rz_r"].at[kind, d, target],
            hop[d],
        )

    def rz_send(kind, zz):
        if zz > 0:
            when(both(zi == 0, has(kind, zz)), lambda: rz_copy(kind, zz, 0, zi + 1).start())
        if zz < A - 1:
            when(both(zi == A - 1, has(kind, zz)), lambda: rz_copy(kind, zz, 1, zi - 1).start())

    def rz_recv(kind, t):
        hi, lo = A - 1 - t, t
        for target, d, cond, onward in (
            (hi, 0, both(zi > 0, zi <= hi, has(kind, hi)), both(zi > 0, zi < hi, has(kind, hi))),
            (lo, 1, both(zi < A - 1, zi >= lo, has(kind, lo)), both(zi < A - 1, zi > lo, has(kind, lo))),
        ):

            def go(target=target, d=d):
                rz_copy(kind, target, d, zi).wait_recv()
                add_into(wunit(GR[kind], kind, target, yi), rz_slot(kind, target, d, zi))

            when(cond, go)
            when(
                onward,
                lambda target=target, d=d: rz_copy(kind, target, d, zi + 1 - 2 * d).start(),
            )

    def rz_drain(kind):
        for target in range(A):
            when(both(zi < target, has(kind, target)), lambda target=target: rz_copy(kind, target, 0, zi + 1).wait_send())
            when(both(zi > target, has(kind, target)), lambda target=target: rz_copy(kind, target, 1, zi - 1).wait_send())

    def fa_has(kind, slot):
        return (zi == slot) if kind == PROJ else (c == c)

    def fa_pairs(kind, slot):
        r = s.rows[kind]
        if kind == VEC:
            return [(slice(None), rows(n["FV"], slot * r, r))]
        if kind == PROJ:
            return [(slice(None), n["out_p"])]
        if kind == DOWN:
            return [(slice(None), rows(n["out_d"], slot * r, r))]
        if kind == IN:
            return [
                (pl.ds(j * G, G), n["out_i"].at[:, pl.ds(mult(j * D + slot * G, 128), G)]) for j in range(3)
            ]
        if not s.packed:
            return [(slice(None), rows(n["out_u"], slot * r, r))]
        hc = s.hc
        return [
            (pl.ds(j * hc, hc), n["out_u"].at[:, pl.ds(mult((j * s.nctx + slot) * hc, 128), hc)])
            for j in range(s.F)
        ]

    def fa_copies(kind, slot, which):
        own = wunit(GR[kind], kind, zi, yi)
        out = []
        for j, (cols, dst) in enumerate(fa_pairs(kind, slot)):
            src = own.at[:, cols] if which < 2 else dst
            out.append(
                rcopy(src, dst, n["fa_s"].at[kind, which, j], n["fa_r"].at[kind, which, j], (sib, xn, sib)[which])
            )
        return out

    def fa_local(kind):
        own = wunit(GR[kind], kind, zi, yi)
        return [
            pltpu.make_async_copy(own.at[:, cols], dst, n["fa_l"].at[kind, j])
            for j, (cols, dst) in enumerate(fa_pairs(kind, c))
        ]

    def each(copies, what):
        for copy in copies:
            getattr(copy, what)()

    def fa_start(kind):
        def go():
            each(fa_copies(kind, c, 1), "start")
            each(fa_copies(kind, c, 0), "start")
            each(fa_local(kind), "start")

        when(fa_has(kind, c), go)

    def fa_fwd(kind):
        def go():
            for copy, onward in zip(fa_copies(kind, xn_c, 1), fa_copies(kind, xn_c, 2)):
                copy.wait_recv()
                onward.start()

        when(fa_has(kind, xn_c), go)

    def fa_end(kind):
        when(fa_has(kind, sib_c), lambda: each(fa_copies(kind, sib_c, 0), "wait_recv"))
        when(fa_has(kind, xs_c), lambda: each(fa_copies(kind, xs_c, 2), "wait_recv"))

        def own():
            each(fa_copies(kind, c, 1), "wait_send")
            each(fa_copies(kind, c, 0), "wait_send")
            each(fa_local(kind), "wait")

        when(fa_has(kind, c), own)
        when(fa_has(kind, xn_c), lambda: each(fa_copies(kind, xn_c, 2), "wait_send"))

    PC = (n["Po"], n["Pc"])

    def cr_copy(arr, which, slot):
        if which < 2:
            return rcopy(
                rows(PC[arr], slot * T, T),
                n["r1"].at[arr, pl.ds(which * T, T)],
                n["cr_s"].at[arr, which],
                n["cr_r"].at[arr, which],
                sib,
            )
        return rcopy(rows(PC[arr], slot * T, T), n["r2"].at[arr], n["cr_s"].at[arr, 2], n["cr_r"].at[arr, 2], xn)

    def cr_start(arr):
        cr_copy(arr, 1, xs_c).start()
        cr_copy(arr, 0, sib_c).start()

    def cr_mid(arr):
        cr_copy(arr, 1, xs_c).wait_recv()
        add_into(rows(PC[arr], xn_c * T, T), n["r1"].at[arr, pl.ds(T, T)])
        cr_copy(arr, 2, xn_c).start()

    def cr_wait(arr):
        cr_copy(arr, 0, sib_c).wait_recv()
        cr_copy(arr, 2, xn_c).wait_recv()

    def cr_drain(arr):
        cr_copy(arr, 1, xs_c).wait_send()
        cr_copy(arr, 0, sib_c).wait_send()
        cr_copy(arr, 2, xn_c).wait_send()

    vecs, cos, sin = n["vecs"], n["cos"], n["sin"]

    def vec(row, width=D):
        return vecs[row : row + 1, 0:width]

    def loop(count, fn):
        def step(i, carry):
            fn(i)
            return carry

        lax.fori_loop(0, count, step, 0)

    def tile(ref, start, size, cols=slice(None)):
        return ref[pl.ds(mult(start, size), size), cols]

    def here(j, k, width):
        at = 8 * (j // 2) + j % 2
        return jnp.where(n["Bs"][at : at + 1, 0:width] == k, 1.0, 0.0)

    def to_order(dst, src):
        def one(k):
            total = None
            for j in range(2 * s.nctx):
                w = here(j, k, src.shape[1]).astype(src.dtype)
                term = src[j * BLK : (j + 1) * BLK, :] * w
                total = term if total is None else total + term
            dst[pl.ds(mult(k * BLK, BLK), BLK), :] = total

        loop(2 * s.nctx, one)

    def from_order(src, put):
        for j in range(2 * s.nctx):
            total = None
            for k in range(2 * s.nctx):
                w = here(j, k, src.shape[1]).astype(src.dtype)
                term = src[k * BLK : (k + 1) * BLK, :] * w
                total = term if total is None else total + term
            put(slice(j * BLK, (j + 1) * BLK), total)

    def norms(slot):
        def one(i):
            at = pl.ds(mult(slot * T + i * BLK, BLK), BLK)
            x = n["Xs"][at, :].astype(F32)
            center = x - jnp.mean(x, axis=-1, keepdims=True)
            nn = center * lax.rsqrt(jnp.mean(center * center, axis=-1, keepdims=True) + EPS)
            n["nb"][at, :] = nn.astype(BF)
            n["A1"][at, :] = (nn * vec(0) + vec(1)).astype(BF)
            n["A2"][at, :] = (nn * vec(2) + vec(3)).astype(BF)

        loop(T // BLK, one)

    lane64 = lax.broadcasted_iota(jnp.int32, (T, 128), 1) % HEAD_DIM
    first_half = lane64 < ROT // 2

    def rope(u, cs_, sn_, sign):
        partner = jnp.where(first_half, pltpu.roll(u, 128 - ROT // 2, 1), pltpu.roll(u, ROT // 2, 1))
        return u * cs_ + (partner * sn_) * sign

    def tables():
        def put(name):
            def store(at, value):
                n[name][at, :] = value

            return store

        from_order(cos, put("cos_st"))
        from_order(sin, put("sin_st"))

    raw, S = n["dl"], n["S"]

    def qkv():
        def one(i):
            at = pl.ds(mult(i * T, T), T)
            j = dot(n["A1"][at, :], n["Wi"][...]) + vec(7, 3 * G)
            cs_, sn_ = n["cos_st"][at, :], n["sin_st"][at, :]
            for p in range(G // 128):
                lo = 128 * p
                q = rope(j[:, lo : lo + 128], cs_, sn_, 1.0).astype(BF)
                raw[at, lo : lo + 128] = (q.astype(F32) * HEAD_DIM**-0.5).astype(BF)
                raw[at, G + lo : G + lo + 128] = rope(j[:, G + lo : G + lo + 128], cs_, sn_, 1.0).astype(BF)
            raw[at, 2 * G : 3 * G] = j[:, 2 * G : 3 * G].astype(BF)

        loop(N // T, one)

    def dattended():
        def one(i):
            at = pl.ds(mult(i * T, T), T)
            raw[at, 3 * G : 4 * G] = dot11(n["Gs"][at, :], n["Wp"][...]).astype(BF)

        loop(N // T, one)

    def order():
        to_order(S, raw)

    def zero_dkv():
        n["dk"][...] = jnp.zeros((N, G), F32)
        n["dv"][...] = jnp.zeros((N, G), F32)

    def attention(p, i):
        L = (i + 1) * T
        cols = slice(128 * p, 128 * p + 128)
        at = slice(i * T, i * T + T)
        part = [slice(j * G + 128 * p, j * G + 128 * p + 128) for j in range(4)]
        kb, vb = S[0:L, part[1]], S[0:L, part[2]]
        qb, db = S[at, part[0]], S[at, part[3]]
        lane = lax.broadcasted_iota(jnp.int32, (T, 128), 1)
        key_at = lax.broadcasted_iota(jnp.int32, (T, T), 0)
        query_at = lax.broadcasted_iota(jnp.int32, (T, T), 1)
        keep = key_at <= query_at
        outs, dqs, ps, ds_, qs, dbs = [], [], [], [], [], []
        for h in range(2):
            mine = (lane >= HEAD_DIM) if h else (lane < HEAD_DIM)
            qh = jnp.where(mine, qb, jnp.zeros_like(qb))
            dh = jnp.where(mine, db, jnp.zeros_like(db))
            sc = dot11(kb, qh)
            last = jnp.where(keep, sc[L - T :], -1e30)
            sc = last if i == 0 else jnp.concatenate([sc[: L - T], last], axis=0)
            e = jnp.exp(sc - jnp.max(sc, axis=0, keepdims=True))
            pr = e * (1.0 / jnp.sum(e, axis=0, keepdims=True))
            dp = dot11(vb, dh)
            delta = jnp.sum(pr * dp, axis=0, keepdims=True)
            dsl = (pr * (dp - delta)).astype(BF)
            pb = pr.astype(BF)
            outs.append(dot00(vb, pb))
            dqs.append(dot00(kb, dsl))
            n["dv"][0:L, cols] += dot(pb, dh)
            n["dk"][0:L, cols] += dot(dsl, qh)
        feature = lax.broadcasted_iota(jnp.int32, (128, T), 0)
        raw[at, part[3]] = jnp.where(feature < HEAD_DIM, outs[0], outs[1]).T.astype(BF)
        n["dq"][at, cols] = jnp.where(feature < HEAD_DIM, dqs[0], dqs[1]).T * HEAD_DIM**-0.5

    def joined_back():
        n["cs"][2:3, :] = jnp.zeros((1, D), F32)

        def one(i):
            at = pl.ds(mult(i * T, T), T)
            cs_, sn_ = cos[at, :], sin[at, :]
            for p in range(G // 128):
                cols = slice(128 * p, 128 * p + 128)
                for j, (name, turn) in enumerate((("dq", True), ("dk", True), ("dv", False))):
                    u = n[name][at, cols]
                    if turn:
                        u = rope(u, cs_, sn_, -1.0)
                    u = u.astype(BF)
                    lo = j * G + 128 * p
                    raw[at, lo : lo + 128] = u
                    n["cs"][2:3, lo : lo + 128] += jnp.sum(u.astype(F32), axis=0, keepdims=True)

        loop(N // T, one)

        def put(at, value):
            n["dj"][at, :] = value[:, 0 : 3 * G]
            n["att_st"][at, :] = value[:, 3 * G : 4 * G]

        from_order(raw, put)

    def in_grad():
        def one(i):
            at = pl.ds(mult(i * 256, 256), 256)
            n["Gi"][at, :] = dot00(n["A1"][:, at], n["dj"][...]).astype(BF)

        loop(D // 256, one)

    def proj_grad():
        def one(i):
            at = pl.ds(mult(i * 256, 256), 256)
            n["Gp"][:, at] = dot00(n["att_st"][...], n["Gs"][:, at]).astype(BF)

        loop(D // 256, one)

    def mlp_up():
        def one(i):
            at = pl.ds(mult((i // 4) * T, T), T)
            cols = pl.ds(mult((i % 4) * 256, 256), 256)
            x = dot(n["A2"][at, :], n["Wu"][:, cols]) + vecs[6:7, cols]
            phi = 0.5 + 0.5 * lax.erf(x * math.sqrt(0.5))
            pdf = jnp.exp(-0.5 * x * x) * (1.0 / math.sqrt(2.0 * math.pi))
            n["act"][at, cols] = (x * phi).astype(BF)
            n["gp"][at, cols] = (phi + x * pdf).astype(BF)

        loop(16, one)

    def down_grad():
        def one(i):
            at = pl.ds(mult(i * 256, 256), 256)
            n["Gd"][at, :] = dot00(n["act"][:, at], n["Gs"][...]).astype(BF)

        loop(H // 256, one)

    def mlp_back():
        n["cs"][6:7, :] = jnp.zeros((1, D), F32)

        def one(i):
            at = pl.ds(mult((i // 4) * T, T), T)
            cols = pl.ds(mult((i % 4) * 256, 256), 256)
            da = dot11(n["Gs"][at, :], n["Wd"][cols, :])
            dl = (da * n["gp"][at, cols].astype(F32)).astype(BF)
            n["dl"][at, cols] = dl
            n["cs"][6:7, cols] += jnp.sum(dl.astype(F32), axis=0, keepdims=True)

        loop(16, one)

    def up_grad():
        def one(i):
            at = pl.ds(mult(i * 256, 256), 256)
            n["Gu"][at, :] = dot00(n["A2"][:, at], n["dl"][...]).astype(BF)

        loop(D // 256, one)

    def out_part():
        def one(i):
            at = pl.ds(mult(i * T, T), T)
            n["Po"][at, :] = (dot(n["att_st"][at, :], n["Wp"][...]) + dot(n["act"][at, :], n["Wd"][...])).astype(BF)

        loop(N // T, one)

    def input_part():
        for row in (0, 1, 4, 5):
            n["cs"][row : row + 1, :] = jnp.zeros((1, D), F32)

        def one(i):
            at = pl.ds(mult(i * T, T), T)
            nn = n["nb"][at, :].astype(F32)
            e1 = dot11(n["dj"][at, :], n["Wi"][...])
            n["cs"][0:1, :] += jnp.sum(e1 * nn, axis=0, keepdims=True)
            n["cs"][1:2, :] += jnp.sum(e1, axis=0, keepdims=True)
            e2 = dot11(n["dl"][at, :], n["Wu"][...])
            n["cs"][4:5, :] += jnp.sum(e2 * nn, axis=0, keepdims=True)
            n["cs"][5:6, :] += jnp.sum(e2, axis=0, keepdims=True)
            n["Pc"][at, :] = (e1 * vec(0) + e2 * vec(2)).astype(BF)

        loop(N // T, one)

    def own_g_sum():
        n["cs"][7:8, :] = jnp.zeros((1, D), F32)
        g = tile(n["Gs"], c * T, T).astype(F32)
        n["cs"][3:4, :] = jnp.sum(g, axis=0, keepdims=True)

    def finish_out():
        base = c * T
        x = tile(n["Xs"], base, T).astype(F32)
        total = tile(n["Po"], base, T).astype(F32) + n["r1"][0, 0:T].astype(F32) + n["r2"][0].astype(F32)
        n["xo"][...] = (x + total + vec(4) + vec(5)).astype(BF)

    def finish_input():
        base = c * T
        x = tile(n["Xs"], base, T).astype(F32)
        center = x - jnp.mean(x, axis=-1, keepdims=True)
        rstd = lax.rsqrt(jnp.mean(center * center, axis=-1, keepdims=True) + EPS)
        nn = center * rstd
        cc = tile(n["Pc"], base, T).astype(F32) + n["r1"][1, 0:T].astype(F32) + n["r2"][1].astype(F32)
        mean_c = jnp.mean(cc, axis=-1, keepdims=True)
        mean_cn = jnp.mean(cc * nn, axis=-1, keepdims=True)
        n["xg"][...] = tile(n["Gs"], base, T).astype(F32) + (cc - mean_c - nn * mean_cn) * rstd

    def unpack_vectors():
        for j in range(s.F):
            n["vecs"][0:7, j * 128 : (j + 1) * 128] = n["Wv"][j * VROWS : j * VROWS + 7, :]
        per = G // 128
        for j in range(3):
            for p in range(per):
                b = j * (D // 128) + c * per + p
                lo = (j * per + p) * 128
                n["vecs"][7:8, lo : lo + 128] = n["Wv"][pl.ds((b // 3) * VROWS + 7 + b % 3, 1), :]

    def pack_sums():
        n["Gv"][...] = jnp.zeros((s.F * VROWS, 128), F32)
        cs = n["cs"]
        for j in range(s.F):
            cols = slice(j * 128, (j + 1) * 128)
            base = j * VROWS
            for row, place in ((0, 0), (1, 1), (3, 5), (4, 6), (5, 7)):
                n["Gv"][base + place : base + place + 1, :] = cs[row : row + 1, cols]
            n["Gv"][pl.ds(base + 8 + c, 1), :] = cs[6:7, cols]
        per = G // 128
        for j in range(3):
            for p in range(per):
                b = j * (D // 128) + c * per + p
                lo = (j * per + p) * 128
                n["Gv"][pl.ds((b // 3) * VROWS + 2 + b % 3, 1), :] = cs[2:3, lo : lo + 128]

    def local(i, src, dst):
        return pltpu.make_async_copy(src, dst, n["loc"].at[i])

    own_i = wunit(W[IN], IN, zi, yi)
    own_u = wunit(W[UP], UP, zi, yi)
    hc = s.hc
    lc = {
        "x": [local(0, n["x"], rows(n["Xs"], c * T, T))],
        "b": [local(1, n["blk"], rows(n["Bs"], c * 8, 8))],
        "i": [
            pltpu.make_async_copy(
                n["w_i"].at[:, pl.ds(mult(j * D + c * G, 128), G)], own_i.at[:, pl.ds(j * G, G)], n["loc_i"].at[j]
            )
            for j in range(3)
        ],
        "p": [local(3, n["w_p"], wunit(W[PROJ], PROJ, zi, yi))],
        "g": [local(4, n["g"], rows(n["Gs"], c * T, T))],
        "u": [local(5, n["w_u"], own_u)]
        if not s.packed
        else [
            pltpu.make_async_copy(
                n["w_u"].at[:, pl.ds(mult((j * s.nctx + c) * hc, 128), hc)],
                own_u.at[:, pl.ds(j * hc, hc)],
                n["loc_u"].at[j],
            )
            for j in range(s.F)
        ],
        "d": [local(6, rows(n["w_d"], c * hc, hc), wunit(W[DOWN], DOWN, zi, yi))],
    }
    if s.packed:
        lc["v"] = [local(2, n["vpack"], wunit(W[VEC], VEC, zi, yi))]

    def lstart(key):
        if key == "p":
            when(zi == c, lambda: each(lc[key], "start"))
        else:
            each(lc[key], "start")

    def lwait(key):
        if key == "p":
            when(zi == c, lambda: each(lc[key], "wait"))
        else:
            each(lc[key], "wait")

    for key in lc:
        lstart(key)
    lwait("i")
    if s.packed:
        lwait("v")
        ag_start(VEC)
    ag_start(IN)
    lwait("b")
    xa_start(2)
    lwait("x")
    xa_start(0)
    lwait("p")
    ag_start(PROJ)
    lwait("g")
    lwait("u")
    lwait("d")
    if s.packed:
        for t in range(A - 1):
            ag_z(VEC, t)
        ag_y(VEC)
        unpack_vectors()
    norms(c)
    ag_z(IN, 0)
    xa_start(1)
    xa_wait(0, sib_c)
    norms(sib_c)
    ag_z(IN, 1)
    ag_start(UP)
    xa_fwd(2)
    xa_fwd(0)
    norms(xn_c)
    ag_z(IN, 2)
    for t in range(A - 1):
        ag_z(PROJ, t)
    xa_wait(0, xs_c)
    norms(xs_c)
    ag_z(UP, 0)
    ag_start(DOWN)
    xa_wait(2, sib_c)
    xa_wait(2, xs_c)
    tables()
    xa_fwd(1)
    ag_y(IN)
    qkv()
    ag_z(UP, 1)
    xa_wait(1, sib_c)
    xa_wait(1, xs_c)
    ag_y(PROJ)
    dattended()
    order()
    own_g_sum()
    zero_dkv()
    ag_z(UP, 2)
    pump = [lambda t=t: ag_z(DOWN, t) for t in range(A - 1)]
    for p in range(G // 128):
        for i in range(N // T):
            attention(p, i)
            if pump:
                pump.pop(0)()
    joined_back()
    in_grad()
    for zz in ry_zz(IN):
        ry_send(IN, 0, zz)
    proj_grad()
    for zz in ry_zz(PROJ):
        ry_send(PROJ, 0, zz)
    ag_y(UP)
    mlp_up()

    def ry_all(kind):
        for t in range(B - 1):
            if t:
                for zz in ry_zz(kind):
                    ry_send(kind, t, zz)
            for zz in ry_zz(kind):
                ry_recv(kind, t, zz)
                if t == B - 2 and kind != PROJ:
                    rz_send(kind, zz)
        if kind == PROJ:
            for zz in range(A):
                rz_send(kind, zz)

    down_grad()
    for zz in ry_zz(DOWN):
        ry_send(DOWN, 0, zz)
    ry_all(IN)
    ry_all(PROJ)
    ag_y(DOWN)
    mlp_back()
    rz_recv(IN, 0)
    rz_recv(PROJ, 0)
    up_grad()
    for zz in ry_zz(UP):
        ry_send(UP, 0, zz)
    rz_recv(IN, 1)
    rz_recv(PROJ, 1)
    out_part()
    cr_start(0)
    rz_recv(IN, 2)
    rz_recv(PROJ, 2)
    fa_start(IN)
    fa_start(PROJ)
    ry_all(DOWN)
    cr_mid(0)
    input_part()
    cr_start(1)
    if s.packed:
        pack_sums()
        for zz in ry_zz(VEC):
            ry_send(VEC, 0, zz)
    rz_recv(DOWN, 0)
    ry_all(UP)
    if s.packed:
        ry_all(VEC)
    cr_mid(1)
    rz_recv(DOWN, 1)
    cr_wait(0)
    finish_out()
    put_out = local(12, n["xo"], n["out"])
    put_out.start()
    rz_recv(UP, 0)
    rz_recv(DOWN, 2)
    fa_start(DOWN)
    rz_recv(UP, 1)
    cr_wait(1)
    finish_input()
    put_in = local(13, n["xg"], n["input_grad"])
    put_in.start()
    rz_recv(UP, 2)
    fa_start(UP)
    if s.packed:
        for t in range(A - 1):
            rz_recv(VEC, t)
        fa_start(VEC)
    for kind in s.kinds:
        fa_fwd(kind)
    for kind in s.kinds:
        fa_end(kind)
    if s.packed:
        n["vtot"][...] = sum(n["FV"][j * VROWS : (j + 1) * VROWS, :] for j in range(s.nctx))
    put_cs = local(14, n["vtot"] if s.packed else n["cs"], n["sums"])
    put_cs.start()
    for kind in s.kinds:
        ag_drain(kind)
        ry_drain(kind)
        rz_drain(kind)
    for arr in range(3):
        xa_drain(arr)
    for arr in range(2):
        cr_drain(arr)
    put_out.wait()
    put_in.wait()
    put_cs.wait()


def rope_tables(length):
    half = ROT // 2
    freq = np.power(np.float32(10000.0), np.float32(-2.0) * np.arange(half, dtype=np.float32) / np.float32(ROT))
    angle = np.arange(length, dtype=np.float32)[:, None] * freq[None, :].astype(np.float32)
    cos = np.ones((length, 128), np.float32)
    sin = np.zeros((length, 128), np.float32)
    for base in range(0, 128, HEAD_DIM):
        cos[:, base : base + half] = np.cos(angle)
        cos[:, base + half : base + ROT] = np.cos(angle)
        sin[:, base : base + half] = -np.sin(angle)
        sin[:, base + half : base + ROT] = np.sin(angle)
    return cos, sin


def body(
    hidden_in,
    positions,
    out_grad,
    attn_gain,
    attn_shift,
    in_weight,
    in_bias,
    proj_weight,
    proj_bias,
    mlp_gain,
    mlp_shift,
    up_weight,
    up_bias,
    down_weight,
    down_bias,
):
    nctx, nshard = lax.axis_size("ctx"), lax.axis_size("fsdp")
    T, D = hidden_in.shape[1:]
    hidden = up_weight.shape[1]
    s = Sizes(T, D, hidden, nctx, nshard)
    R, G, F = s.R, s.G, s.F
    hc = s.hc
    c, f = lax.axis_index("ctx"), lax.axis_index("fsdp")

    def pick_ctx(array, axis):
        return lax.dynamic_index_in_dim(array, c, axis, keepdims=False)

    small = [attn_gain, attn_shift, mlp_gain, mlp_shift, proj_bias, down_bias, up_bias, in_bias]
    if s.packed:
        w_u = up_weight
        small[6] = pick_ctx(up_bias.reshape(nctx, hc), 0)
        flat = jnp.concatenate(small).astype(F32)
        extra = dict(vpack=jnp.pad(flat, (0, VROWS * 128 - flat.shape[0])).reshape(VROWS, 128))
    else:
        w_u = pick_ctx(up_weight.reshape(R, F, nctx, hc), 2).reshape(R, s.H)
        lengths = [v.shape[0] for v in small]
        gathered = lax.all_gather(jnp.concatenate(small).astype(F32), "fsdp", axis=0)
        full, at = [], 0
        for length in lengths:
            full.append(gathered[:, at : at + length].reshape(-1))
            at += length
        full[6] = pick_ctx(full[6].reshape(F, nctx, hc), 1).reshape(-1)
        full[7] = jnp.pad(pick_ctx(full[7].reshape(3, nctx, G), 1).reshape(-1), (0, D - 3 * G))
        extra = dict(vecs=jnp.stack(full))
    blk = jnp.pad((positions[0, ::BLK] // BLK)[:, None], ((0, 8 - T // BLK), (0, 0)))
    blk = jnp.broadcast_to(blk, (8, D))
    cos, sin = rope_tables(s.N)

    plan = scratch_plan(s)
    any_ = pl.BlockSpec(memory_space=pl.ANY)
    vmem = pl.BlockSpec(memory_space=pltpu.VMEM)
    ins = dict(
        x=hidden_in[0],
        g=out_grad[0],
        blk=blk,
        w_i=in_weight,
        w_p=proj_weight,
        w_u=w_u,
        w_d=down_weight,
        **extra,
        cos=jnp.asarray(cos),
        sin=jnp.asarray(sin),
    )
    in_vmem = {"vecs", "cos", "sin"}
    outs = dict(
        out=jax.ShapeDtypeStruct((T, D), BF),
        input_grad=jax.ShapeDtypeStruct((T, D), F32),
        out_i=jax.ShapeDtypeStruct((R, 3 * D), BF),
        out_p=jax.ShapeDtypeStruct((R, D), BF),
        out_u=jax.ShapeDtypeStruct((R, hidden) if s.packed else (nctx * R, s.H), BF),
        out_d=jax.ShapeDtypeStruct((nctx * hc, D), BF),
        sums=jax.ShapeDtypeStruct((VROWS, 128) if s.packed else (8, D), F32),
    )
    names = list(ins) + list(outs) + list(plan)
    out, input_grad, gi, gp, gu, gd, sums = pl.pallas_call(
        lambda *refs: kernel_body(s, names, *refs),
        out_shape=tuple(outs.values()),
        in_specs=[vmem if name in in_vmem else any_ for name in ins],
        out_specs=tuple(any_ for _ in outs),
        scratch_shapes=list(plan.values()),
        compiler_params=pltpu.CompilerParams(
            collective_id=0, has_side_effects=True, vmem_limit_bytes=63 << 20
        ),
        name="block",
    )(*ins.values())

    def own(full_vector):
        length = full_vector.shape[0] // F
        return lax.dynamic_slice_in_dim(full_vector, f * length, length)

    if s.packed:
        gain1, shift1, g_sum, gain2, shift2 = (sums[row] for row in (0, 1, 5, 6, 7))
        in_bias_sum, up_bias_sum = sums[2:5].reshape(-1), sums[8 : 8 + nctx].reshape(-1)
        up_total = gu.astype(F32)
    else:
        here = (jnp.arange(nctx) == c).astype(F32)
        in_b = (sums[2, : 3 * G].reshape(3, 1, G) * here[None, :, None]).reshape(-1)
        up_b = (sums[6].reshape(F, 1, hc) * here[None, :, None]).reshape(-1)
        total = lax.psum(
            jnp.concatenate([sums[0], sums[1], in_b, sums[3], sums[4], sums[5], up_b]), ("ctx", "fsdp")
        )
        parts, at = [], 0
        for length in (D, D, 3 * D, D, D, D, hidden):
            parts.append(own(total[at : at + length]))
            at += length
        gain1, shift1, in_bias_sum, g_sum, gain2, shift2, up_bias_sum = parts
        up_total = gu.astype(F32).reshape(nctx, R, F, hc).transpose(1, 2, 0, 3).reshape(R, hidden)
    return (
        out[None],
        input_grad[None],
        gain1,
        shift1,
        gi.astype(F32),
        in_bias_sum,
        gp.astype(F32),
        g_sum,
        gain2,
        shift2,
        up_total,
        up_bias_sum,
        gd.astype(F32),
        g_sum,
    )


def solution(mesh):
    tok, vec, mat = P("fsdp", "ctx", None), P("fsdp"), P("fsdp", None)
    placed = (tok, P("fsdp", "ctx"), tok, vec, vec, mat, vec, mat, vec, vec, vec, mat, vec, mat, vec)
    return jax.shard_map(
        body,
        mesh=mesh,
        in_specs=placed,
        out_specs=(tok, tok, vec, vec, mat, vec, mat, vec, vec, vec, mat, vec, mat, vec),
        check_vma=False,
    )
```

```python
import math

import jax
import jax.numpy as jnp
import numpy as np
from jax import lax
from jax.experimental import pallas as pl
from jax.experimental.pallas import tpu as pltpu
from jax.sharding import PartitionSpec as P

HEADS = 16
HEAD_DIM = 64
ROT = 16
BLK = 128
EPS = 1e-05
MESH = pl.DeviceIdType.MESH
BF = jnp.bfloat16
F32 = jnp.float32
IN, PROJ, UP, DOWN, VEC = range(5)
VROWS = 16
BOTH1 = (((1,), (1,)), ((), ()))
BOTH0 = (((0,), (0,)), ((), ()))


def dot(a, b):
    return jnp.dot(a, b, preferred_element_type=F32)


def dot11(a, b):
    return lax.dot_general(a, b, BOTH1, preferred_element_type=F32)


def dot00(a, b):
    return lax.dot_general(a, b, BOTH0, preferred_element_type=F32)


def mult(value, of):
    return pl.multiple_of(value, of)


def both(*conds):
    out = conds[0]
    for cond in conds[1:]:
        out = jnp.logical_and(out, cond)
    return out


class Sizes:
    def __init__(self, tokens, width, hidden, nctx, nshard):
        self.T = tokens
        self.N = tokens * nctx
        self.D = width
        self.H = hidden // nctx
        self.G = width // nctx
        self.nctx = nctx
        self.F = nshard
        self.A = nctx
        self.B = nshard // nctx
        self.R = width // nshard
        self.hc = hidden // nshard // nctx
        self.packed = self.R % 128 == 0 and self.hc % 128 == 0
        self.rows = (self.R, self.R, self.R, self.hc, VROWS)
        self.cols = (3 * self.G, width, self.H, width, 128)
        self.units = (self.F, self.B, self.F, self.F, self.F)
        self.types = (BF, BF, BF, BF, F32)
        self.kinds = (IN, PROJ, UP, DOWN) + ((VEC,) if self.packed else ())
        self.NY = 1 if self.B == 2 else self.B + 1


def scratch_plan(s):
    N, D, G, H = s.N, s.D, s.G, s.H
    vm = pltpu.VMEM
    dma = pltpu.SemaphoreType.DMA
    plan = dict(
        Xs=vm((N, D), BF),
        Gs=vm((N, D), BF),
        Bs=vm((s.nctx * 8, D), jnp.int32),
        cos_st=vm((N, 128), F32),
        sin_st=vm((N, 128), F32),
        nb=vm((N, D), BF),
        A1=vm((N, D), BF),
        A2=vm((N, D), BF),
        S=vm((N, 4 * G), BF),
        dq=vm((N, G), F32),
        dk=vm((N, G), F32),
        dv=vm((N, G), F32),
        att_st=vm((N, G), BF),
        dj=vm((N, 3 * G), BF),
        act=vm((N, H), BF),
        gp=vm((N, H), BF),
        dl=vm((N, H), BF),
        Po=vm((N, D), BF),
        Pc=vm((N, D), BF),
        r1=vm((2, 2 * s.T, D), BF),
        r2=vm((2, s.T, D), BF),
        cs=vm((8, D), F32),
        xo=vm((s.T, D), BF),
        xg=vm((s.T, D), F32),
    )
    if s.packed:
        plan["vecs"] = vm((8, D), F32)
        plan["FV"] = vm((s.nctx * VROWS, 128), F32)
        plan["vtot"] = vm((VROWS, 128), F32)
    for kind in s.kinds:
        name = "ipudv"[kind]
        u, r, cl = s.units[kind], s.rows[kind], s.cols[kind]
        dt = s.types[kind]
        per = 1 if kind == PROJ else s.A
        plan["W" + name] = vm((u * r, cl), dt)
        plan["G" + name] = vm((u * r, cl), dt)
        plan["Y" + name] = vm((s.NY * per * r, cl), dt)
        plan["Z" + name] = vm((s.A * r, cl), dt)
    plan.update(
        ag_s=dma((5, 4, s.F)),
        ag_r=dma((5, s.F)),
        xa_s=dma((3, 3)),
        xa_r=dma((3, s.nctx)),
        ry_s=dma((5, 2, s.F)),
        ry_r=dma((5, 2, s.F)),
        rz_s=dma((5, s.A)),
        rz_r=dma((5, s.A)),
        cr_s=dma((2, 3)),
        cr_r=dma((2, 3)),
        fa_s=dma((5, 3, s.F)),
        fa_r=dma((5, 3, s.F)),
        fa_l=dma((5, s.F)),
        loc=dma((16,)),
        loc_i=dma((3,)),
        loc_u=dma((s.F,)),
    )
    return plan


def kernel_body(s, names, *refs):
    n = dict(zip(names, refs))
    T, N, D, G, H, A, B, R = s.T, s.N, s.D, s.G, s.H, s.A, s.B, s.R
    c = lax.axis_index("ctx")
    f = lax.axis_index("fsdp")
    zi, yi = f // B, f % B
    sib_c = c + 1 - 2 * (c % 2)
    xn_c = (c + s.nctx // 2) % s.nctx
    xs_c = (sib_c + s.nctx // 2) % s.nctx
    sib, xn = (sib_c, f), (xn_c, f)
    edge = (zi < A - 1, zi > 0, yi < B - 1, yi > 0)
    hop = ((c, f + B), (c, f - B), (c, f + 1), (c, f - 1))

    def when(cond, fn):
        pl.when(cond)(fn)

    def rcopy(src, dst, ssem, rsem, dev):
        return pltpu.make_async_remote_copy(
            src_ref=src, dst_ref=dst, send_sem=ssem, recv_sem=rsem, device_id=dev, device_id_type=MESH
        )

    def rows(ref, start, size):
        return ref.at[pl.ds(mult(start, size), size)]

    bar = pltpu.get_barrier_semaphore()
    for dev in (sib, xn):
        pl.semaphore_signal(bar, inc=1, device_id=dev, device_id_type=MESH)
    for step in range(1, A):
        pl.semaphore_signal(bar, inc=1, device_id=(c, (zi + step) % A * B + yi), device_id_type=MESH)
    for d in (2, 3):
        when(
            edge[d],
            lambda d=d: pl.semaphore_signal(bar, inc=1, device_id=hop[d], device_id_type=MESH),
        )
    count = 2 + A - 1 + sum(jnp.where(e, 1, 0) for e in edge[2:])
    pl.semaphore_wait(bar, count)

    W = [n.get("W" + x) for x in "ipudv"]

    def has(kind, oz):
        return (oz == c) if kind == PROJ else (oz == oz)

    def wunit(ref, kind, oz, oy):
        r = s.rows[kind]
        at = oy if kind == PROJ else oz * B + oy
        return rows(ref, at * r, r)

    def ag_copy(kind, oz, oy, d):
        u = wunit(W[kind], kind, oz, oy)
        at = oz * B + oy
        return rcopy(u, u, n["ag_s"].at[kind, d, at], n["ag_r"].at[kind, at], hop[d])

    def ag_send(kind, oz, oy, dirs, cond):
        for d in dirs:
            when(both(cond, edge[d]), lambda d=d: ag_copy(kind, oz, oy, d).start())

    def ag_start(kind):
        ag_send(kind, zi, yi, (0, 1, 2, 3), has(kind, zi))

    def ag_z(kind, t):
        for sign, d in ((-1, 0), (1, 1)):
            oz = zi + sign * (1 + t)
            cond = both(oz >= 0, oz < A, has(kind, oz))

            def go(oz=oz, d=d):
                ag_copy(kind, oz, yi, d).wait_recv()
                for dd in (d, 2, 3):
                    when(edge[dd], lambda dd=dd: ag_copy(kind, oz, yi, dd).start())

            when(cond, go)

    def ag_y(kind):
        for t in range(B - 1):
            for zz in [c] if kind == PROJ else list(range(A)):
                for sign, d in ((-1, 2), (1, 3)):
                    oy = yi + sign * (1 + t)

                    def go(oy=oy, d=d, zz=zz):
                        ag_copy(kind, zz, oy, d).wait_recv()
                        if B > 2:
                            when(edge[d], lambda: ag_copy(kind, zz, oy, d).start())

                    when(both(oy >= 0, oy < B), go)

    def ag_drain(kind):
        for oz in [c] if kind == PROJ else list(range(A)):
            when(both(oz <= zi, edge[0]), lambda oz=oz: ag_copy(kind, oz, yi, 0).wait_send())
            when(both(oz >= zi, edge[1]), lambda oz=oz: ag_copy(kind, oz, yi, 1).wait_send())
            for oy in range(B):
                when(both(oy <= yi, edge[2]), lambda oz=oz, oy=oy: ag_copy(kind, oz, oy, 2).wait_send())
                when(both(oy >= yi, edge[3]), lambda oz=oz, oy=oy: ag_copy(kind, oz, oy, 3).wait_send())

    XA = ((n["Xs"], T), (n["Gs"], T), (n["Bs"], 8))

    def xa_copy(arr, slot, which):
        ref, r = XA[arr]
        u = rows(ref, slot * r, r)
        return rcopy(u, u, n["xa_s"].at[arr, which], n["xa_r"].at[arr, slot], (xn, sib)[which != 0])

    def xa_start(arr):
        xa_copy(arr, c, 0).start()
        xa_copy(arr, c, 1).start()

    def xa_wait(arr, slot):
        xa_copy(arr, slot, 0).wait_recv()

    def xa_fwd(arr):
        xa_wait(arr, xn_c)
        xa_copy(arr, xn_c, 2).start()

    def xa_drain(arr):
        xa_copy(arr, c, 0).wait_send()
        xa_copy(arr, c, 1).wait_send()
        xa_copy(arr, xn_c, 2).wait_send()

    GR = [n.get("G" + x) for x in "ipudv"]
    YB = [n.get("Y" + x) for x in "ipudv"]
    ZB = [n.get("Z" + x) for x in "ipudv"]

    def add_into(dst, src):
        dst[...] = (dst[...].astype(F32) + src[...].astype(F32)).astype(dst.dtype)

    def ry_copy(kind, zz, target, d, receiver):
        r = s.rows[kind]
        per = 1 if kind == PROJ else A
        at = 0 if kind == PROJ else zz
        if B == 2:
            slot = 0
        elif d == 0:
            slot = target
        else:
            slot = jnp.where(receiver == target, B, target)
        return rcopy(
            wunit(GR[kind], kind, zz, target),
            rows(YB[kind], (slot * per + at) * r, r),
            n["ry_s"].at[kind, d, zz * B + target],
            n["ry_r"].at[kind, d, zz * B + target],
            hop[2 + d],
        )

    def ry_dst(kind, zz, target, d):
        r = s.rows[kind]
        per = 1 if kind == PROJ else A
        at = 0 if kind == PROJ else zz
        if B == 2:
            slot = 0
        elif d == 0:
            slot = target
        else:
            slot = jnp.where(yi == target, B, target)
        return rows(YB[kind], (slot * per + at) * r, r)

    def ry_zz(kind):
        return [c] if kind == PROJ else [A - 1, 0] + list(range(A - 2, 0, -1))

    def ry_send(kind, t, zz):
        hi, lo = B - 1 - t, t
        when(yi == 0, lambda: ry_copy(kind, zz, hi, 0, yi + 1).start())
        when(yi == B - 1, lambda: ry_copy(kind, zz, lo, 1, yi - 1).start())

    def ry_recv(kind, t, zz):
        hi, lo = B - 1 - t, t
        for target, d, cond, onward in (
            (hi, 0, both(yi > 0, yi <= hi), both(yi > 0, yi < hi)),
            (lo, 1, both(yi < B - 1, yi >= lo), both(yi < B - 1, yi > lo)),
        ):

            def go(target=target, d=d):
                ry_copy(kind, zz, target, d, yi).wait_recv()
                add_into(wunit(GR[kind], kind, zz, target), ry_dst(kind, zz, target, d))

            when(cond, go)
            if B > 2:
                when(
                    onward,
                    lambda target=target, d=d: ry_copy(
                        kind, zz, target, d, yi + 1 - 2 * d
                    ).start(),
                )

    def ry_drain(kind):
        for zz in [c] if kind == PROJ else list(range(A)):
            for target in range(B):
                when(yi < target, lambda zz=zz, target=target: ry_copy(kind, zz, target, 0, yi + 1).wait_send())
                when(yi > target, lambda zz=zz, target=target: ry_copy(kind, zz, target, 1, yi - 1).wait_send())

    def rz_copy(kind, target, source):
        r = s.rows[kind]
        return rcopy(
            wunit(GR[kind], kind, target, yi),
            rows(ZB[kind], source * r, r),
            n["rz_s"].at[kind, target],
            n["rz_r"].at[kind, source],
            (c, target * B + yi),
        )

    def rz_send(kind, target):
        when(zi != target, lambda: rz_copy(kind, target, zi).start())

    def rz_sum(kind):
        def go():
            for source in range(A):
                def take(source=source):
                    rz_copy(kind, zi, source).wait_recv()
                    add_into(wunit(GR[kind], kind, zi, yi), rows(ZB[kind], source * s.rows[kind], s.rows[kind]))

                when(zi != source, take)

        if kind == PROJ:
            when(zi == c, go)
        else:
            go()

    def rz_drain(kind):
        for target in [c] if kind == PROJ else list(range(A)):
            when(zi != target, lambda target=target: rz_copy(kind, target, zi).wait_send())

    def fa_has(kind, slot):
        return (zi == slot) if kind == PROJ else (c == c)

    def fa_pairs(kind, slot):
        r = s.rows[kind]
        if kind == VEC:
            return [(slice(None), rows(n["FV"], slot * r, r))]
        if kind == PROJ:
            return [(slice(None), n["out_p"])]
        if kind == DOWN:
            return [(slice(None), rows(n["out_d"], slot * r, r))]
        if kind == IN:
            return [
                (pl.ds(j * G, G), n["out_i"].at[:, pl.ds(mult(j * D + slot * G, 128), G)]) for j in range(3)
            ]
        if not s.packed:
            return [(slice(None), rows(n["out_u"], slot * r, r))]
        hc = s.hc
        return [
            (pl.ds(j * hc, hc), n["out_u"].at[:, pl.ds(mult((j * s.nctx + slot) * hc, 128), hc)])
            for j in range(s.F)
        ]

    def fa_copies(kind, slot, which):
        own = wunit(GR[kind], kind, zi, yi)
        out = []
        for j, (cols, dst) in enumerate(fa_pairs(kind, slot)):
            src = own.at[:, cols] if which < 2 else dst
            out.append(
                rcopy(src, dst, n["fa_s"].at[kind, which, j], n["fa_r"].at[kind, which, j], (sib, xn, sib)[which])
            )
        return out

    def fa_local(kind):
        own = wunit(GR[kind], kind, zi, yi)
        return [
            pltpu.make_async_copy(own.at[:, cols], dst, n["fa_l"].at[kind, j])
            for j, (cols, dst) in enumerate(fa_pairs(kind, c))
        ]

    def each(copies, what):
        for copy in copies:
            getattr(copy, what)()

    def fa_start(kind):
        def go():
            each(fa_copies(kind, c, 1), "start")
            each(fa_copies(kind, c, 0), "start")
            each(fa_local(kind), "start")

        when(fa_has(kind, c), go)

    def fa_fwd(kind):
        def go():
            for copy, onward in zip(fa_copies(kind, xn_c, 1), fa_copies(kind, xn_c, 2)):
                copy.wait_recv()
                onward.start()

        when(fa_has(kind, xn_c), go)

    def fa_end(kind):
        when(fa_has(kind, sib_c), lambda: each(fa_copies(kind, sib_c, 0), "wait_recv"))
        when(fa_has(kind, xs_c), lambda: each(fa_copies(kind, xs_c, 2), "wait_recv"))

        def own():
            each(fa_copies(kind, c, 1), "wait_send")
            each(fa_copies(kind, c, 0), "wait_send")
            each(fa_local(kind), "wait")

        when(fa_has(kind, c), own)
        when(fa_has(kind, xn_c), lambda: each(fa_copies(kind, xn_c, 2), "wait_send"))

    PC = (n["Po"], n["Pc"])

    def cr_copy(arr, which, slot):
        if which < 2:
            return rcopy(
                rows(PC[arr], slot * T, T),
                n["r1"].at[arr, pl.ds(which * T, T)],
                n["cr_s"].at[arr, which],
                n["cr_r"].at[arr, which],
                sib,
            )
        return rcopy(rows(PC[arr], slot * T, T), n["r2"].at[arr], n["cr_s"].at[arr, 2], n["cr_r"].at[arr, 2], xn)

    def cr_start(arr):
        cr_copy(arr, 1, xs_c).start()
        cr_copy(arr, 0, sib_c).start()

    def cr_mid(arr):
        cr_copy(arr, 1, xs_c).wait_recv()
        add_into(rows(PC[arr], xn_c * T, T), n["r1"].at[arr, pl.ds(T, T)])
        cr_copy(arr, 2, xn_c).start()

    def cr_wait(arr):
        cr_copy(arr, 0, sib_c).wait_recv()
        cr_copy(arr, 2, xn_c).wait_recv()

    def cr_drain(arr):
        cr_copy(arr, 1, xs_c).wait_send()
        cr_copy(arr, 0, sib_c).wait_send()
        cr_copy(arr, 2, xn_c).wait_send()

    vecs, cos, sin = n["vecs"], n["cos"], n["sin"]

    def vec(row, width=D):
        return vecs[row : row + 1, 0:width]

    def loop(count, fn):
        def step(i, carry):
            fn(i)
            return carry

        lax.fori_loop(0, count, step, 0)

    def tile(ref, start, size, cols=slice(None)):
        return ref[pl.ds(mult(start, size), size), cols]

    def here(j, k, width):
        at = 8 * (j // 2) + j % 2
        return jnp.where(n["Bs"][at : at + 1, 0:width] == k, 1.0, 0.0)

    def to_order(dst, src):
        def one(k):
            total = None
            for j in range(2 * s.nctx):
                w = here(j, k, src.shape[1]).astype(src.dtype)
                term = src[j * BLK : (j + 1) * BLK, :] * w
                total = term if total is None else total + term
            dst[pl.ds(mult(k * BLK, BLK), BLK), :] = total

        loop(2 * s.nctx, one)

    def from_order(src, put):
        for j in range(2 * s.nctx):
            total = None
            for k in range(2 * s.nctx):
                w = here(j, k, src.shape[1]).astype(src.dtype)
                term = src[k * BLK : (k + 1) * BLK, :] * w
                total = term if total is None else total + term
            put(slice(j * BLK, (j + 1) * BLK), total)

    def norms(slot):
        def one(i):
            at = pl.ds(mult(slot * T + i * BLK, BLK), BLK)
            x = n["Xs"][at, :].astype(F32)
            center = x - jnp.mean(x, axis=-1, keepdims=True)
            nn = center * lax.rsqrt(jnp.mean(center * center, axis=-1, keepdims=True) + EPS)
            n["nb"][at, :] = nn.astype(BF)
            n["A1"][at, :] = (nn * vec(0) + vec(1)).astype(BF)
            n["A2"][at, :] = (nn * vec(2) + vec(3)).astype(BF)

        loop(T // BLK, one)

    lane64 = lax.broadcasted_iota(jnp.int32, (T, 128), 1) % HEAD_DIM
    first_half = lane64 < ROT // 2

    def rope(u, cs_, sn_, sign):
        partner = jnp.where(first_half, pltpu.roll(u, 128 - ROT // 2, 1), pltpu.roll(u, ROT // 2, 1))
        return u * cs_ + (partner * sn_) * sign

    def tables():
        def put(name):
            def store(at, value):
                n[name][at, :] = value

            return store

        from_order(cos, put("cos_st"))
        from_order(sin, put("sin_st"))

    raw, S = n["dl"], n["S"]

    def qkv():
        def one(i):
            at = pl.ds(mult(i * T, T), T)
            j = dot(n["A1"][at, :], n["Wi"][...]) + vec(7, 3 * G)
            cs_, sn_ = n["cos_st"][at, :], n["sin_st"][at, :]
            for p in range(G // 128):
                lo = 128 * p
                q = rope(j[:, lo : lo + 128], cs_, sn_, 1.0).astype(BF)
                raw[at, lo : lo + 128] = (q.astype(F32) * HEAD_DIM**-0.5).astype(BF)
                raw[at, G + lo : G + lo + 128] = rope(j[:, G + lo : G + lo + 128], cs_, sn_, 1.0).astype(BF)
            raw[at, 2 * G : 3 * G] = j[:, 2 * G : 3 * G].astype(BF)

        loop(N // T, one)

    def dattended():
        def one(i):
            at = pl.ds(mult(i * T, T), T)
            raw[at, 3 * G : 4 * G] = dot11(n["Gs"][at, :], n["Wp"][...]).astype(BF)

        loop(N // T, one)

    def order():
        to_order(S, raw)

    def zero_dkv():
        n["dk"][...] = jnp.zeros((N, G), F32)
        n["dv"][...] = jnp.zeros((N, G), F32)

    def attention(p, i):
        L = (i + 1) * T
        cols = slice(128 * p, 128 * p + 128)
        at = slice(i * T, i * T + T)
        part = [slice(j * G + 128 * p, j * G + 128 * p + 128) for j in range(4)]
        kb, vb = S[0:L, part[1]], S[0:L, part[2]]
        qb, db = S[at, part[0]], S[at, part[3]]
        lane = lax.broadcasted_iota(jnp.int32, (T, 128), 1)
        key_at = lax.broadcasted_iota(jnp.int32, (T, T), 0)
        query_at = lax.broadcasted_iota(jnp.int32, (T, T), 1)
        keep = key_at <= query_at
        outs, dqs, ps, ds_, qs, dbs = [], [], [], [], [], []
        for h in range(2):
            mine = (lane >= HEAD_DIM) if h else (lane < HEAD_DIM)
            qh = jnp.where(mine, qb, jnp.zeros_like(qb))
            dh = jnp.where(mine, db, jnp.zeros_like(db))
            sc = dot11(kb, qh)
            last = jnp.where(keep, sc[L - T :], -1e30)
            sc = last if i == 0 else jnp.concatenate([sc[: L - T], last], axis=0)
            e = jnp.exp(sc - jnp.max(sc, axis=0, keepdims=True))
            pr = e * (1.0 / jnp.sum(e, axis=0, keepdims=True))
            dp = dot11(vb, dh)
            delta = jnp.sum(pr * dp, axis=0, keepdims=True)
            dsl = (pr * (dp - delta)).astype(BF)
            pb = pr.astype(BF)
            outs.append(dot00(vb, pb))
            dqs.append(dot00(kb, dsl))
            n["dv"][0:L, cols] += dot(pb, dh)
            n["dk"][0:L, cols] += dot(dsl, qh)
        feature = lax.broadcasted_iota(jnp.int32, (128, T), 0)
        raw[at, part[3]] = jnp.where(feature < HEAD_DIM, outs[0], outs[1]).T.astype(BF)
        n["dq"][at, cols] = jnp.where(feature < HEAD_DIM, dqs[0], dqs[1]).T * HEAD_DIM**-0.5

    def joined_back():
        n["cs"][2:3, :] = jnp.zeros((1, D), F32)

        def one(i):
            at = pl.ds(mult(i * T, T), T)
            cs_, sn_ = cos[at, :], sin[at, :]
            for p in range(G // 128):
                cols = slice(128 * p, 128 * p + 128)
                for j, (name, turn) in enumerate((("dq", True), ("dk", True), ("dv", False))):
                    u = n[name][at, cols]
                    if turn:
                        u = rope(u, cs_, sn_, -1.0)
                    u = u.astype(BF)
                    lo = j * G + 128 * p
                    raw[at, lo : lo + 128] = u
                    n["cs"][2:3, lo : lo + 128] += jnp.sum(u.astype(F32), axis=0, keepdims=True)

        loop(N // T, one)

        def put(at, value):
            n["dj"][at, :] = value[:, 0 : 3 * G]
            n["att_st"][at, :] = value[:, 3 * G : 4 * G]

        from_order(raw, put)

    def in_grad():
        def one(i):
            at = pl.ds(mult(i * 256, 256), 256)
            n["Gi"][at, :] = dot00(n["A1"][:, at], n["dj"][...]).astype(BF)

        loop(D // 256, one)

    def proj_grad():
        def one(i):
            at = pl.ds(mult(i * 256, 256), 256)
            n["Gp"][:, at] = dot00(n["att_st"][...], n["Gs"][:, at]).astype(BF)

        loop(D // 256, one)

    def mlp_up():
        def one(i):
            at = pl.ds(mult((i // 4) * T, T), T)
            cols = pl.ds(mult((i % 4) * 256, 256), 256)
            x = dot(n["A2"][at, :], n["Wu"][:, cols]) + vecs[6:7, cols]
            phi = 0.5 + 0.5 * lax.erf(x * math.sqrt(0.5))
            pdf = jnp.exp(-0.5 * x * x) * (1.0 / math.sqrt(2.0 * math.pi))
            n["act"][at, cols] = (x * phi).astype(BF)
            n["gp"][at, cols] = (phi + x * pdf).astype(BF)

        loop(16, one)

    def down_grad():
        def one(i):
            at = pl.ds(mult(i * 256, 256), 256)
            n["Gd"][at, :] = dot00(n["act"][:, at], n["Gs"][...]).astype(BF)

        loop(H // 256, one)

    def mlp_back():
        n["cs"][6:7, :] = jnp.zeros((1, D), F32)

        def one(i):
            at = pl.ds(mult((i // 4) * T, T), T)
            cols = pl.ds(mult((i % 4) * 256, 256), 256)
            da = dot11(n["Gs"][at, :], n["Wd"][cols, :])
            dl = (da * n["gp"][at, cols].astype(F32)).astype(BF)
            n["dl"][at, cols] = dl
            n["cs"][6:7, cols] += jnp.sum(dl.astype(F32), axis=0, keepdims=True)

        loop(16, one)

    def up_grad():
        def one(i):
            at = pl.ds(mult(i * 256, 256), 256)
            n["Gu"][at, :] = dot00(n["A2"][:, at], n["dl"][...]).astype(BF)

        loop(D // 256, one)

    def out_part():
        def one(i):
            at = pl.ds(mult(i * T, T), T)
            n["Po"][at, :] = (dot(n["att_st"][at, :], n["Wp"][...]) + dot(n["act"][at, :], n["Wd"][...])).astype(BF)

        loop(N // T, one)

    def input_part():
        for row in (0, 1, 4, 5):
            n["cs"][row : row + 1, :] = jnp.zeros((1, D), F32)

        def one(i):
            at = pl.ds(mult(i * T, T), T)
            nn = n["nb"][at, :].astype(F32)
            e1 = dot11(n["dj"][at, :], n["Wi"][...])
            n["cs"][0:1, :] += jnp.sum(e1 * nn, axis=0, keepdims=True)
            n["cs"][1:2, :] += jnp.sum(e1, axis=0, keepdims=True)
            e2 = dot11(n["dl"][at, :], n["Wu"][...])
            n["cs"][4:5, :] += jnp.sum(e2 * nn, axis=0, keepdims=True)
            n["cs"][5:6, :] += jnp.sum(e2, axis=0, keepdims=True)
            n["Pc"][at, :] = (e1 * vec(0) + e2 * vec(2)).astype(BF)

        loop(N // T, one)

    def own_g_sum():
        n["cs"][7:8, :] = jnp.zeros((1, D), F32)
        g = tile(n["Gs"], c * T, T).astype(F32)
        n["cs"][3:4, :] = jnp.sum(g, axis=0, keepdims=True)

    def finish_out():
        base = c * T
        x = tile(n["Xs"], base, T).astype(F32)
        total = tile(n["Po"], base, T).astype(F32) + n["r1"][0, 0:T].astype(F32) + n["r2"][0].astype(F32)
        n["xo"][...] = (x + total + vec(4) + vec(5)).astype(BF)

    def finish_input():
        base = c * T
        x = tile(n["Xs"], base, T).astype(F32)
        center = x - jnp.mean(x, axis=-1, keepdims=True)
        rstd = lax.rsqrt(jnp.mean(center * center, axis=-1, keepdims=True) + EPS)
        nn = center * rstd
        cc = tile(n["Pc"], base, T).astype(F32) + n["r1"][1, 0:T].astype(F32) + n["r2"][1].astype(F32)
        mean_c = jnp.mean(cc, axis=-1, keepdims=True)
        mean_cn = jnp.mean(cc * nn, axis=-1, keepdims=True)
        n["xg"][...] = tile(n["Gs"], base, T).astype(F32) + (cc - mean_c - nn * mean_cn) * rstd

    def unpack_vectors():
        for j in range(s.F):
            n["vecs"][0:7, j * 128 : (j + 1) * 128] = n["Wv"][j * VROWS : j * VROWS + 7, :]
        per = G // 128
        for j in range(3):
            for p in range(per):
                b = j * (D // 128) + c * per + p
                lo = (j * per + p) * 128
                n["vecs"][7:8, lo : lo + 128] = n["Wv"][pl.ds((b // 3) * VROWS + 7 + b % 3, 1), :]

    def pack_sums():
        n["Gv"][...] = jnp.zeros((s.F * VROWS, 128), F32)
        cs = n["cs"]
        for j in range(s.F):
            cols = slice(j * 128, (j + 1) * 128)
            base = j * VROWS
            for row, place in ((0, 0), (1, 1), (3, 5), (4, 6), (5, 7)):
                n["Gv"][base + place : base + place + 1, :] = cs[row : row + 1, cols]
            n["Gv"][pl.ds(base + 8 + c, 1), :] = cs[6:7, cols]
        per = G // 128
        for j in range(3):
            for p in range(per):
                b = j * (D // 128) + c * per + p
                lo = (j * per + p) * 128
                n["Gv"][pl.ds((b // 3) * VROWS + 2 + b % 3, 1), :] = cs[2:3, lo : lo + 128]

    def local(i, src, dst):
        return pltpu.make_async_copy(src, dst, n["loc"].at[i])

    own_i = wunit(W[IN], IN, zi, yi)
    own_u = wunit(W[UP], UP, zi, yi)
    hc = s.hc
    lc = {
        "x": [local(0, n["x"], rows(n["Xs"], c * T, T))],
        "b": [local(1, n["blk"], rows(n["Bs"], c * 8, 8))],
        "i": [
            pltpu.make_async_copy(
                n["w_i"].at[:, pl.ds(mult(j * D + c * G, 128), G)], own_i.at[:, pl.ds(j * G, G)], n["loc_i"].at[j]
            )
            for j in range(3)
        ],
        "p": [local(3, n["w_p"], wunit(W[PROJ], PROJ, zi, yi))],
        "g": [local(4, n["g"], rows(n["Gs"], c * T, T))],
        "u": [local(5, n["w_u"], own_u)]
        if not s.packed
        else [
            pltpu.make_async_copy(
                n["w_u"].at[:, pl.ds(mult((j * s.nctx + c) * hc, 128), hc)],
                own_u.at[:, pl.ds(j * hc, hc)],
                n["loc_u"].at[j],
            )
            for j in range(s.F)
        ],
        "d": [local(6, rows(n["w_d"], c * hc, hc), wunit(W[DOWN], DOWN, zi, yi))],
    }
    if s.packed:
        lc["v"] = [local(2, n["vpack"], wunit(W[VEC], VEC, zi, yi))]

    def lstart(key):
        if key == "p":
            when(zi == c, lambda: each(lc[key], "start"))
        else:
            each(lc[key], "start")

    def lwait(key):
        if key == "p":
            when(zi == c, lambda: each(lc[key], "wait"))
        else:
            each(lc[key], "wait")

    for key in lc:
        lstart(key)
    lwait("i")
    if s.packed:
        lwait("v")
        ag_start(VEC)
    ag_start(IN)
    lwait("b")
    xa_start(2)
    lwait("x")
    xa_start(0)
    lwait("p")
    ag_start(PROJ)
    lwait("g")
    lwait("u")
    lwait("d")
    if s.packed:
        for t in range(A - 1):
            ag_z(VEC, t)
        ag_y(VEC)
        unpack_vectors()
    norms(c)
    ag_z(IN, 0)
    xa_start(1)
    xa_wait(0, sib_c)
    norms(sib_c)
    ag_z(IN, 1)
    ag_start(UP)
    xa_fwd(2)
    xa_fwd(0)
    norms(xn_c)
    ag_z(IN, 2)
    for t in range(A - 1):
        ag_z(PROJ, t)
    xa_wait(0, xs_c)
    norms(xs_c)
    ag_z(UP, 0)
    ag_start(DOWN)
    xa_wait(2, sib_c)
    xa_wait(2, xs_c)
    tables()
    xa_fwd(1)
    ag_y(IN)
    qkv()
    ag_z(UP, 1)
    xa_wait(1, sib_c)
    xa_wait(1, xs_c)
    ag_y(PROJ)
    dattended()
    order()
    own_g_sum()
    zero_dkv()
    ag_z(UP, 2)
    pump = [lambda t=t: ag_z(DOWN, t) for t in range(A - 1)]
    for p in range(G // 128):
        for i in range(N // T):
            attention(p, i)
            if pump:
                pump.pop(0)()
    joined_back()
    in_grad()
    for zz in ry_zz(IN):
        ry_send(IN, 0, zz)
    proj_grad()
    for zz in ry_zz(PROJ):
        ry_send(PROJ, 0, zz)
    ag_y(UP)
    mlp_up()

    def ry_all(kind):
        for t in range(B - 1):
            if t:
                for zz in ry_zz(kind):
                    ry_send(kind, t, zz)
            for zz in ry_zz(kind):
                ry_recv(kind, t, zz)
                if t == B - 2:
                    rz_send(kind, zz)

    down_grad()
    for zz in ry_zz(DOWN):
        ry_send(DOWN, 0, zz)
    ry_all(IN)
    ry_all(PROJ)
    ag_y(DOWN)
    mlp_back()
    up_grad()
    for zz in ry_zz(UP):
        ry_send(UP, 0, zz)
    rz_sum(IN)
    fa_start(IN)
    rz_sum(PROJ)
    fa_start(PROJ)
    out_part()
    cr_start(0)
    ry_all(DOWN)
    cr_mid(0)
    input_part()
    cr_start(1)
    fa_fwd(IN)
    fa_fwd(PROJ)
    if s.packed:
        pack_sums()
        for zz in ry_zz(VEC):
            ry_send(VEC, 0, zz)
    ry_all(UP)
    if s.packed:
        ry_all(VEC)
    cr_mid(1)
    rz_sum(DOWN)
    fa_start(DOWN)
    cr_wait(0)
    finish_out()
    put_out = local(12, n["xo"], n["out"])
    put_out.start()
    cr_wait(1)
    finish_input()
    put_in = local(13, n["xg"], n["input_grad"])
    put_in.start()
    fa_fwd(DOWN)
    rz_sum(UP)
    fa_start(UP)
    if s.packed:
        rz_sum(VEC)
        fa_start(VEC)
    fa_fwd(UP)
    if s.packed:
        fa_fwd(VEC)
    for kind in s.kinds:
        fa_end(kind)
    if s.packed:
        n["vtot"][...] = sum(n["FV"][j * VROWS : (j + 1) * VROWS, :] for j in range(s.nctx))
    put_cs = local(14, n["vtot"] if s.packed else n["cs"], n["sums"])
    put_cs.start()
    for kind in s.kinds:
        ag_drain(kind)
        ry_drain(kind)
        rz_drain(kind)
    for arr in range(3):
        xa_drain(arr)
    for arr in range(2):
        cr_drain(arr)
    put_out.wait()
    put_in.wait()
    put_cs.wait()


def rope_tables(length):
    half = ROT // 2
    freq = np.power(np.float32(10000.0), np.float32(-2.0) * np.arange(half, dtype=np.float32) / np.float32(ROT))
    angle = np.arange(length, dtype=np.float32)[:, None] * freq[None, :].astype(np.float32)
    cos = np.ones((length, 128), np.float32)
    sin = np.zeros((length, 128), np.float32)
    for base in range(0, 128, HEAD_DIM):
        cos[:, base : base + half] = np.cos(angle)
        cos[:, base + half : base + ROT] = np.cos(angle)
        sin[:, base : base + half] = -np.sin(angle)
        sin[:, base + half : base + ROT] = np.sin(angle)
    return cos, sin


def body(
    hidden_in,
    positions,
    out_grad,
    attn_gain,
    attn_shift,
    in_weight,
    in_bias,
    proj_weight,
    proj_bias,
    mlp_gain,
    mlp_shift,
    up_weight,
    up_bias,
    down_weight,
    down_bias,
):
    nctx, nshard = lax.axis_size("ctx"), lax.axis_size("fsdp")
    T, D = hidden_in.shape[1:]
    hidden = up_weight.shape[1]
    s = Sizes(T, D, hidden, nctx, nshard)
    R, G, F = s.R, s.G, s.F
    hc = s.hc
    c, f = lax.axis_index("ctx"), lax.axis_index("fsdp")

    def pick_ctx(array, axis):
        return lax.dynamic_index_in_dim(array, c, axis, keepdims=False)

    small = [attn_gain, attn_shift, mlp_gain, mlp_shift, proj_bias, down_bias, up_bias, in_bias]
    if s.packed:
        w_u = up_weight
        small[6] = pick_ctx(up_bias.reshape(nctx, hc), 0)
        flat = jnp.concatenate(small).astype(F32)
        extra = dict(vpack=jnp.pad(flat, (0, VROWS * 128 - flat.shape[0])).reshape(VROWS, 128))
    else:
        w_u = pick_ctx(up_weight.reshape(R, F, nctx, hc), 2).reshape(R, s.H)
        lengths = [v.shape[0] for v in small]
        gathered = lax.all_gather(jnp.concatenate(small).astype(F32), "fsdp", axis=0)
        full, at = [], 0
        for length in lengths:
            full.append(gathered[:, at : at + length].reshape(-1))
            at += length
        full[6] = pick_ctx(full[6].reshape(F, nctx, hc), 1).reshape(-1)
        full[7] = jnp.pad(pick_ctx(full[7].reshape(3, nctx, G), 1).reshape(-1), (0, D - 3 * G))
        extra = dict(vecs=jnp.stack(full))
    blk = jnp.pad((positions[0, ::BLK] // BLK)[:, None], ((0, 8 - T // BLK), (0, 0)))
    blk = jnp.broadcast_to(blk, (8, D))
    cos, sin = rope_tables(s.N)

    plan = scratch_plan(s)
    any_ = pl.BlockSpec(memory_space=pl.ANY)
    vmem = pl.BlockSpec(memory_space=pltpu.VMEM)
    ins = dict(
        x=hidden_in[0],
        g=out_grad[0],
        blk=blk,
        w_i=in_weight,
        w_p=proj_weight,
        w_u=w_u,
        w_d=down_weight,
        **extra,
        cos=jnp.asarray(cos),
        sin=jnp.asarray(sin),
    )
    in_vmem = {"vecs", "cos", "sin"}
    outs = dict(
        out=jax.ShapeDtypeStruct((T, D), BF),
        input_grad=jax.ShapeDtypeStruct((T, D), F32),
        out_i=jax.ShapeDtypeStruct((R, 3 * D), BF),
        out_p=jax.ShapeDtypeStruct((R, D), BF),
        out_u=jax.ShapeDtypeStruct((R, hidden) if s.packed else (nctx * R, s.H), BF),
        out_d=jax.ShapeDtypeStruct((nctx * hc, D), BF),
        sums=jax.ShapeDtypeStruct((VROWS, 128) if s.packed else (8, D), F32),
    )
    names = list(ins) + list(outs) + list(plan)
    out, input_grad, gi, gp, gu, gd, sums = pl.pallas_call(
        lambda *refs: kernel_body(s, names, *refs),
        out_shape=tuple(outs.values()),
        in_specs=[vmem if name in in_vmem else any_ for name in ins],
        out_specs=tuple(any_ for _ in outs),
        scratch_shapes=list(plan.values()),
        compiler_params=pltpu.CompilerParams(
            collective_id=0, has_side_effects=True, vmem_limit_bytes=63 << 20
        ),
        name="block",
    )(*ins.values())

    def own(full_vector):
        length = full_vector.shape[0] // F
        return lax.dynamic_slice_in_dim(full_vector, f * length, length)

    if s.packed:
        gain1, shift1, g_sum, gain2, shift2 = (sums[row] for row in (0, 1, 5, 6, 7))
        in_bias_sum, up_bias_sum = sums[2:5].reshape(-1), sums[8 : 8 + nctx].reshape(-1)
        up_total = gu.astype(F32)
    else:
        here = (jnp.arange(nctx) == c).astype(F32)
        in_b = (sums[2, : 3 * G].reshape(3, 1, G) * here[None, :, None]).reshape(-1)
        up_b = (sums[6].reshape(F, 1, hc) * here[None, :, None]).reshape(-1)
        total = lax.psum(
            jnp.concatenate([sums[0], sums[1], in_b, sums[3], sums[4], sums[5], up_b]), ("ctx", "fsdp")
        )
        parts, at = [], 0
        for length in (D, D, 3 * D, D, D, D, hidden):
            parts.append(own(total[at : at + length]))
            at += length
        gain1, shift1, in_bias_sum, g_sum, gain2, shift2, up_bias_sum = parts
        up_total = gu.astype(F32).reshape(nctx, R, F, hc).transpose(1, 2, 0, 3).reshape(R, hidden)
    return (
        out[None],
        input_grad[None],
        gain1,
        shift1,
        gi.astype(F32),
        in_bias_sum,
        gp.astype(F32),
        g_sum,
        gain2,
        shift2,
        up_total,
        up_bias_sum,
        gd.astype(F32),
        g_sum,
    )


def solution(mesh):
    tok, vec, mat = P("fsdp", "ctx", None), P("fsdp"), P("fsdp", None)
    placed = (tok, P("fsdp", "ctx"), tok, vec, vec, mat, vec, mat, vec, vec, vec, mat, vec, mat, vec)
    return jax.shard_map(
        body,
        mesh=mesh,
        in_specs=placed,
        out_specs=(tok, tok, vec, vec, mat, vec, mat, vec, vec, vec, mat, vec, mat, vec),
        check_vma=False,
    )
```

```python
import math

import jax
import jax.numpy as jnp
import numpy as np
from jax import lax
from jax.experimental import pallas as pl
from jax.experimental.pallas import tpu as pltpu
from jax.sharding import PartitionSpec as P

HEADS = 16
HEAD_DIM = 64
ROT = 16
BLK = 128
EPS = 1e-05
MESH = pl.DeviceIdType.MESH
BF = jnp.bfloat16
F32 = jnp.float32
IN, PROJ, UP, DOWN, VEC = range(5)
VROWS = 16
BOTH1 = (((1,), (1,)), ((), ()))
BOTH0 = (((0,), (0,)), ((), ()))


def dot(a, b):
    return jnp.dot(a, b, preferred_element_type=F32)


def dot11(a, b):
    return lax.dot_general(a, b, BOTH1, preferred_element_type=F32)


def dot00(a, b):
    return lax.dot_general(a, b, BOTH0, preferred_element_type=F32)


def mult(value, of):
    return pl.multiple_of(value, of)


def both(*conds):
    out = conds[0]
    for cond in conds[1:]:
        out = jnp.logical_and(out, cond)
    return out


class Sizes:
    def __init__(self, tokens, width, hidden, nctx, nshard):
        self.T = tokens
        self.N = tokens * nctx
        self.D = width
        self.H = hidden // nctx
        self.G = width // nctx
        self.nctx = nctx
        self.F = nshard
        self.A = nctx
        self.B = nshard // nctx
        self.R = width // nshard
        self.hc = hidden // nshard // nctx
        self.packed = self.R % 128 == 0 and self.hc % 128 == 0
        self.rows = (self.R, self.R, self.R, self.hc, VROWS)
        self.cols = (3 * self.G, width, self.H, width, 128)
        self.units = (self.F, self.B, self.F, self.F, self.F)
        self.types = (BF, BF, BF, BF, F32)
        self.kinds = (IN, PROJ, UP, DOWN) + ((VEC,) if self.packed else ())
        self.NY = 1 if self.B == 2 else self.B + 1


def scratch_plan(s):
    N, D, G, H = s.N, s.D, s.G, s.H
    vm = pltpu.VMEM
    dma = pltpu.SemaphoreType.DMA
    plan = dict(
        Xs=vm((N, D), BF),
        Gs=vm((N, D), BF),
        Bs=vm((s.nctx * 8, D), jnp.int32),
        cos_st=vm((N, 128), F32),
        sin_st=vm((N, 128), F32),
        nb=vm((N, D), BF),
        A1=vm((N, D), BF),
        A2=vm((N, D), BF),
        S=vm((N, 4 * G), BF),
        dq=vm((N, G), F32),
        dk=vm((N, G), F32),
        dv=vm((N, G), F32),
        att_st=vm((N, G), BF),
        dj=vm((N, 3 * G), BF),
        act=vm((N, H), BF),
        gp=vm((N, H), BF),
        dl=vm((N, H), BF),
        Po=vm((N, D), BF),
        Pc=vm((N, D), BF),
        r1=vm((2, 2 * s.T, D), BF),
        r2=vm((2, s.T, D), BF),
        cs=vm((8, D), F32),
        xo=vm((s.T, D), BF),
        xg=vm((s.T, D), F32),
    )
    if s.packed:
        plan["vecs"] = vm((8, D), F32)
        plan["FV"] = vm((s.nctx * VROWS, 128), F32)
        plan["vtot"] = vm((VROWS, 128), F32)
    for kind in s.kinds:
        name = "ipudv"[kind]
        u, r, cl = s.units[kind], s.rows[kind], s.cols[kind]
        dt = s.types[kind]
        per = 1 if kind == PROJ else s.A
        plan["W" + name] = vm((u * r, cl), dt)
        plan["G" + name] = vm((u * r, cl), dt)
        plan["Y" + name] = vm((s.NY * per * r, cl), dt)
        plan["Z" + name] = vm((3 * r, cl), dt)
    plan.update(
        ag_s=dma((5, 4, s.F)),
        ag_r=dma((5, s.F)),
        xa_s=dma((3, 3)),
        xa_r=dma((3, s.nctx)),
        ry_s=dma((5, 2, s.F)),
        ry_r=dma((5, 2, s.F)),
        rz_s=dma((5, 3)),
        rz_r=dma((5, 3)),
        cr_s=dma((2, 3)),
        cr_r=dma((2, 3)),
        fa_s=dma((5, 3, s.F)),
        fa_r=dma((5, 3, s.F)),
        fa_l=dma((5, s.F)),
        loc=dma((16,)),
        loc_i=dma((3,)),
        loc_u=dma((s.F,)),
    )
    return plan


def kernel_body(s, names, *refs):
    n = dict(zip(names, refs))
    T, N, D, G, H, A, B, R = s.T, s.N, s.D, s.G, s.H, s.A, s.B, s.R
    c = lax.axis_index("ctx")
    f = lax.axis_index("fsdp")
    zi, yi = f // B, f % B
    sib_c = c + 1 - 2 * (c % 2)
    xn_c = (c + s.nctx // 2) % s.nctx
    xs_c = (sib_c + s.nctx // 2) % s.nctx
    sib, xn = (sib_c, f), (xn_c, f)
    edge = (zi < A - 1, zi > 0, yi < B - 1, yi > 0)
    hop = ((c, f + B), (c, f - B), (c, f + 1), (c, f - 1))

    def when(cond, fn):
        pl.when(cond)(fn)

    def rcopy(src, dst, ssem, rsem, dev):
        return pltpu.make_async_remote_copy(
            src_ref=src, dst_ref=dst, send_sem=ssem, recv_sem=rsem, device_id=dev, device_id_type=MESH
        )

    def rows(ref, start, size):
        return ref.at[pl.ds(mult(start, size), size)]

    W = [n.get("W" + x) for x in "ipudv"]

    def has(kind, oz):
        return (oz == c) if kind == PROJ else (oz == oz)

    def wunit(ref, kind, oz, oy):
        r = s.rows[kind]
        at = oy if kind == PROJ else oz * B + oy
        return rows(ref, at * r, r)

    def ag_copy(kind, oz, oy, d):
        u = wunit(W[kind], kind, oz, oy)
        at = oz * B + oy
        return rcopy(u, u, n["ag_s"].at[kind, d, at], n["ag_r"].at[kind, at], hop[d])

    def ag_send(kind, oz, oy, dirs, cond):
        for d in dirs:
            when(both(cond, edge[d]), lambda d=d: ag_copy(kind, oz, oy, d).start())

    def ag_start(kind):
        ag_send(kind, zi, yi, (0, 1, 2, 3), has(kind, zi))

    def ag_z(kind, t):
        for sign, d in ((-1, 0), (1, 1)):
            oz = zi + sign * (1 + t)
            cond = both(oz >= 0, oz < A, has(kind, oz))

            def go(oz=oz, d=d):
                ag_copy(kind, oz, yi, d).wait_recv()
                for dd in (d, 2, 3):
                    when(edge[dd], lambda dd=dd: ag_copy(kind, oz, yi, dd).start())

            when(cond, go)

    def ag_y(kind):
        for t in range(B - 1):
            for zz in [c] if kind == PROJ else list(range(A)):
                for sign, d in ((-1, 2), (1, 3)):
                    oy = yi + sign * (1 + t)

                    def go(oy=oy, d=d, zz=zz):
                        ag_copy(kind, zz, oy, d).wait_recv()
                        if B > 2:
                            when(edge[d], lambda: ag_copy(kind, zz, oy, d).start())

                    when(both(oy >= 0, oy < B), go)

    def ag_drain(kind):
        for oz in [c] if kind == PROJ else list(range(A)):
            when(both(oz <= zi, edge[0]), lambda oz=oz: ag_copy(kind, oz, yi, 0).wait_send())
            when(both(oz >= zi, edge[1]), lambda oz=oz: ag_copy(kind, oz, yi, 1).wait_send())
            for oy in range(B):
                when(both(oy <= yi, edge[2]), lambda oz=oz, oy=oy: ag_copy(kind, oz, oy, 2).wait_send())
                when(both(oy >= yi, edge[3]), lambda oz=oz, oy=oy: ag_copy(kind, oz, oy, 3).wait_send())

    XA = ((n["Xs"], T), (n["Gs"], T), (n["Bs"], 8))

    def xa_copy(arr, slot, which):
        ref, r = XA[arr]
        u = rows(ref, slot * r, r)
        return rcopy(u, u, n["xa_s"].at[arr, which], n["xa_r"].at[arr, slot], (xn, sib)[which != 0])

    def xa_start(arr):
        xa_copy(arr, c, 0).start()
        xa_copy(arr, c, 1).start()

    def xa_wait(arr, slot):
        xa_copy(arr, slot, 0).wait_recv()

    def xa_fwd(arr):
        xa_wait(arr, xn_c)
        xa_copy(arr, xn_c, 2).start()

    def xa_drain(arr):
        xa_copy(arr, c, 0).wait_send()
        xa_copy(arr, c, 1).wait_send()
        xa_copy(arr, xn_c, 2).wait_send()

    GR = [n.get("G" + x) for x in "ipudv"]
    YB = [n.get("Y" + x) for x in "ipudv"]
    ZB = [n.get("Z" + x) for x in "ipudv"]

    def add_into(dst, src):
        dst[...] = (dst[...].astype(F32) + src[...].astype(F32)).astype(dst.dtype)

    def ry_copy(kind, zz, target, d, receiver):
        r = s.rows[kind]
        per = 1 if kind == PROJ else A
        at = 0 if kind == PROJ else zz
        if B == 2:
            slot = 0
        elif d == 0:
            slot = target
        else:
            slot = jnp.where(receiver == target, B, target)
        return rcopy(
            wunit(GR[kind], kind, zz, target),
            rows(YB[kind], (slot * per + at) * r, r),
            n["ry_s"].at[kind, d, zz * B + target],
            n["ry_r"].at[kind, d, zz * B + target],
            hop[2 + d],
        )

    def ry_dst(kind, zz, target, d):
        r = s.rows[kind]
        per = 1 if kind == PROJ else A
        at = 0 if kind == PROJ else zz
        if B == 2:
            slot = 0
        elif d == 0:
            slot = target
        else:
            slot = jnp.where(yi == target, B, target)
        return rows(YB[kind], (slot * per + at) * r, r)

    pair_z = zi + 1 - 2 * (zi % 2)
    far_z = (zi + A // 2) % A
    diag_z = (pair_z + A // 2) % A
    by_step = [diag_z, pair_z, far_z, zi]

    def ry_zz(kind):
        return [c] if kind == PROJ else by_step

    def ry_send(kind, t, zz):
        hi, lo = B - 1 - t, t
        when(yi == 0, lambda: ry_copy(kind, zz, hi, 0, yi + 1).start())
        when(yi == B - 1, lambda: ry_copy(kind, zz, lo, 1, yi - 1).start())

    def ry_recv(kind, t, zz):
        hi, lo = B - 1 - t, t
        for target, d, cond, onward in (
            (hi, 0, both(yi > 0, yi <= hi), both(yi > 0, yi < hi)),
            (lo, 1, both(yi < B - 1, yi >= lo), both(yi < B - 1, yi > lo)),
        ):

            def go(target=target, d=d):
                ry_copy(kind, zz, target, d, yi).wait_recv()
                add_into(wunit(GR[kind], kind, zz, target), ry_dst(kind, zz, target, d))

            when(cond, go)
            if B > 2:
                when(
                    onward,
                    lambda target=target, d=d: ry_copy(
                        kind, zz, target, d, yi + 1 - 2 * d
                    ).start(),
                )

    def ry_drain(kind):
        for zz in [c] if kind == PROJ else list(range(A)):
            for target in range(B):
                when(yi < target, lambda zz=zz, target=target: ry_copy(kind, zz, target, 0, yi + 1).wait_send())
                when(yi > target, lambda zz=zz, target=target: ry_copy(kind, zz, target, 1, yi - 1).wait_send())

    def rz_copy(kind, which):
        target = by_step[which]
        r = s.rows[kind]
        return rcopy(
            wunit(GR[kind], kind, target, yi),
            rows(ZB[kind], which * r, r),
            n["rz_s"].at[kind, which],
            n["rz_r"].at[kind, which],
            (c, (pair_z, pair_z, far_z)[which] * B + yi),
        )

    def rz_take(kind, which, target):
        r = s.rows[kind]
        rz_copy(kind, which).wait_recv()
        add_into(wunit(GR[kind], kind, target, yi), rows(ZB[kind], which * r, r))

    def rz_pair(kind, which):
        when(has(kind, by_step[which]), lambda: rz_copy(kind, which).start())

    def rz_far(kind):
        def go():
            rz_take(kind, 0, far_z)
            rz_copy(kind, 2).start()

        when(has(kind, far_z), go)

    def rz_sum(kind):
        def go():
            rz_take(kind, 1, zi)
            rz_take(kind, 2, zi)

        when(has(kind, zi), go)

    def rz_drain(kind):
        for which in range(3):
            when(has(kind, by_step[which]), lambda which=which: rz_copy(kind, which).wait_send())

    def ry_first(kind):
        for t in range(B - 2):
            for zz in ry_zz(kind):
                if t:
                    ry_send(kind, t, zz)
                ry_recv(kind, t, zz)
        if B > 2:
            for zz in ry_zz(kind):
                ry_send(kind, B - 2, zz)

    def ry_unit(kind, i):
        if i == 0:
            ry_first(kind)
        ry_recv(kind, B - 2, by_step[i])
        if i < 2:
            rz_pair(kind, i)
        elif i == 2:
            rz_far(kind)

    def ry_proj():
        ry_first(PROJ)
        ry_recv(PROJ, B - 2, c)
        rz_pair(PROJ, 0)
        rz_pair(PROJ, 1)
        rz_far(PROJ)

    def fa_has(kind, slot):
        return (zi == slot) if kind == PROJ else (c == c)

    def fa_pairs(kind, slot):
        r = s.rows[kind]
        if kind == VEC:
            return [(slice(None), rows(n["FV"], slot * r, r))]
        if kind == PROJ:
            return [(slice(None), n["out_p"])]
        if kind == DOWN:
            return [(slice(None), rows(n["out_d"], slot * r, r))]
        if kind == IN:
            return [
                (pl.ds(j * G, G), n["out_i"].at[:, pl.ds(mult(j * D + slot * G, 128), G)]) for j in range(3)
            ]
        if not s.packed:
            return [(slice(None), rows(n["out_u"], slot * r, r))]
        hc = s.hc
        return [
            (pl.ds(j * hc, hc), n["out_u"].at[:, pl.ds(mult((j * s.nctx + slot) * hc, 128), hc)])
            for j in range(s.F)
        ]

    def fa_copies(kind, slot, which):
        own = wunit(GR[kind], kind, zi, yi)
        out = []
        for j, (cols, dst) in enumerate(fa_pairs(kind, slot)):
            src = own.at[:, cols] if which < 2 else dst
            out.append(
                rcopy(src, dst, n["fa_s"].at[kind, which, j], n["fa_r"].at[kind, which, j], (sib, xn, sib)[which])
            )
        return out

    def fa_local(kind):
        own = wunit(GR[kind], kind, zi, yi)
        return [
            pltpu.make_async_copy(own.at[:, cols], dst, n["fa_l"].at[kind, j])
            for j, (cols, dst) in enumerate(fa_pairs(kind, c))
        ]

    def each(copies, what):
        for copy in copies:
            getattr(copy, what)()

    def fa_start(kind):
        def go():
            each(fa_copies(kind, c, 1), "start")
            each(fa_copies(kind, c, 0), "start")
            each(fa_local(kind), "start")

        when(fa_has(kind, c), go)

    def fa_fwd(kind):
        def go():
            for copy, onward in zip(fa_copies(kind, xn_c, 1), fa_copies(kind, xn_c, 2)):
                copy.wait_recv()
                onward.start()

        when(fa_has(kind, xn_c), go)

    def fa_end(kind):
        when(fa_has(kind, sib_c), lambda: each(fa_copies(kind, sib_c, 0), "wait_recv"))
        when(fa_has(kind, xs_c), lambda: each(fa_copies(kind, xs_c, 2), "wait_recv"))

        def own():
            each(fa_copies(kind, c, 1), "wait_send")
            each(fa_copies(kind, c, 0), "wait_send")
            each(fa_local(kind), "wait")

        when(fa_has(kind, c), own)
        when(fa_has(kind, xn_c), lambda: each(fa_copies(kind, xn_c, 2), "wait_send"))

    PC = (n["Po"], n["Pc"])

    def cr_copy(arr, which, slot):
        if which < 2:
            return rcopy(
                rows(PC[arr], slot * T, T),
                n["r1"].at[arr, pl.ds(which * T, T)],
                n["cr_s"].at[arr, which],
                n["cr_r"].at[arr, which],
                sib,
            )
        return rcopy(rows(PC[arr], slot * T, T), n["r2"].at[arr], n["cr_s"].at[arr, 2], n["cr_r"].at[arr, 2], xn)

    def cr_start(arr):
        cr_copy(arr, 1, xs_c).start()
        cr_copy(arr, 0, sib_c).start()

    def cr_mid(arr):
        cr_copy(arr, 1, xs_c).wait_recv()
        add_into(rows(PC[arr], xn_c * T, T), n["r1"].at[arr, pl.ds(T, T)])
        cr_copy(arr, 2, xn_c).start()

    def cr_wait(arr):
        cr_copy(arr, 0, sib_c).wait_recv()
        cr_copy(arr, 2, xn_c).wait_recv()

    def cr_drain(arr):
        cr_copy(arr, 1, xs_c).wait_send()
        cr_copy(arr, 0, sib_c).wait_send()
        cr_copy(arr, 2, xn_c).wait_send()

    vecs, cos, sin = n["vecs"], n["cos"], n["sin"]

    def vec(row, width=D):
        return vecs[row : row + 1, 0:width]

    def loop(count, fn):
        def step(i, carry):
            fn(i)
            return carry

        lax.fori_loop(0, count, step, 0)

    def tile(ref, start, size, cols=slice(None)):
        return ref[pl.ds(mult(start, size), size), cols]

    def here(j, k, width):
        at = 8 * (j // 2) + j % 2
        return jnp.where(n["Bs"][at : at + 1, 0:width] == k, 1.0, 0.0)

    def to_order(dst, src):
        def one(k):
            total = None
            for j in range(2 * s.nctx):
                w = here(j, k, src.shape[1]).astype(src.dtype)
                term = src[j * BLK : (j + 1) * BLK, :] * w
                total = term if total is None else total + term
            dst[pl.ds(mult(k * BLK, BLK), BLK), :] = total

        loop(2 * s.nctx, one)

    def from_order(src, put):
        for j in range(2 * s.nctx):
            total = None
            for k in range(2 * s.nctx):
                w = here(j, k, src.shape[1]).astype(src.dtype)
                term = src[k * BLK : (k + 1) * BLK, :] * w
                total = term if total is None else total + term
            put(slice(j * BLK, (j + 1) * BLK), total)

    def norms(slot):
        def one(i):
            at = pl.ds(mult(slot * T + i * BLK, BLK), BLK)
            x = n["Xs"][at, :].astype(F32)
            center = x - jnp.mean(x, axis=-1, keepdims=True)
            nn = center * lax.rsqrt(jnp.mean(center * center, axis=-1, keepdims=True) + EPS)
            n["nb"][at, :] = nn.astype(BF)
            n["A1"][at, :] = (nn * vec(0) + vec(1)).astype(BF)
            n["A2"][at, :] = (nn * vec(2) + vec(3)).astype(BF)

        loop(T // BLK, one)

    lane64 = lax.broadcasted_iota(jnp.int32, (T, 128), 1) % HEAD_DIM
    first_half = lane64 < ROT // 2

    def rope(u, cs_, sn_, sign):
        partner = jnp.where(first_half, pltpu.roll(u, 128 - ROT // 2, 1), pltpu.roll(u, ROT // 2, 1))
        return u * cs_ + (partner * sn_) * sign

    def tables():
        def put(name):
            def store(at, value):
                n[name][at, :] = value

            return store

        from_order(cos, put("cos_st"))
        from_order(sin, put("sin_st"))

    raw, S = n["dl"], n["S"]

    def qkv():
        def one(i):
            at = pl.ds(mult(i * T, T), T)
            j = dot(n["A1"][at, :], n["Wi"][...]) + vec(7, 3 * G)
            cs_, sn_ = n["cos_st"][at, :], n["sin_st"][at, :]
            for p in range(G // 128):
                lo = 128 * p
                q = rope(j[:, lo : lo + 128], cs_, sn_, 1.0).astype(BF)
                raw[at, lo : lo + 128] = (q.astype(F32) * HEAD_DIM**-0.5).astype(BF)
                raw[at, G + lo : G + lo + 128] = rope(j[:, G + lo : G + lo + 128], cs_, sn_, 1.0).astype(BF)
            raw[at, 2 * G : 3 * G] = j[:, 2 * G : 3 * G].astype(BF)

        loop(N // T, one)

    def dattended():
        def one(i):
            at = pl.ds(mult(i * T, T), T)
            raw[at, 3 * G : 4 * G] = dot11(n["Gs"][at, :], n["Wp"][...]).astype(BF)

        loop(N // T, one)

    def order():
        to_order(S, raw)

    def zero_dkv():
        n["dk"][...] = jnp.zeros((N, G), F32)
        n["dv"][...] = jnp.zeros((N, G), F32)

    def attention(p, i):
        L = (i + 1) * T
        cols = slice(128 * p, 128 * p + 128)
        at = slice(i * T, i * T + T)
        part = [slice(j * G + 128 * p, j * G + 128 * p + 128) for j in range(4)]
        kb, vb = S[0:L, part[1]], S[0:L, part[2]]
        qb, db = S[at, part[0]], S[at, part[3]]
        lane = lax.broadcasted_iota(jnp.int32, (T, 128), 1)
        key_at = lax.broadcasted_iota(jnp.int32, (T, T), 0)
        query_at = lax.broadcasted_iota(jnp.int32, (T, T), 1)
        keep = key_at <= query_at
        outs, dqs, ps, ds_, qs, dbs = [], [], [], [], [], []
        for h in range(2):
            mine = (lane >= HEAD_DIM) if h else (lane < HEAD_DIM)
            qh = jnp.where(mine, qb, jnp.zeros_like(qb))
            dh = jnp.where(mine, db, jnp.zeros_like(db))
            sc = dot11(kb, qh)
            last = jnp.where(keep, sc[L - T :], -1e30)
            sc = last if i == 0 else jnp.concatenate([sc[: L - T], last], axis=0)
            e = jnp.exp(sc - jnp.max(sc, axis=0, keepdims=True))
            pr = e * (1.0 / jnp.sum(e, axis=0, keepdims=True))
            dp = dot11(vb, dh)
            delta = jnp.sum(pr * dp, axis=0, keepdims=True)
            dsl = (pr * (dp - delta)).astype(BF)
            pb = pr.astype(BF)
            outs.append(dot00(vb, pb))
            dqs.append(dot00(kb, dsl))
            n["dv"][0:L, cols] += dot(pb, dh)
            n["dk"][0:L, cols] += dot(dsl, qh)
        feature = lax.broadcasted_iota(jnp.int32, (128, T), 0)
        raw[at, part[3]] = jnp.where(feature < HEAD_DIM, outs[0], outs[1]).T.astype(BF)
        n["dq"][at, cols] = jnp.where(feature < HEAD_DIM, dqs[0], dqs[1]).T * HEAD_DIM**-0.5

    def joined_back():
        n["cs"][2:3, :] = jnp.zeros((1, D), F32)

        def one(i):
            at = pl.ds(mult(i * T, T), T)
            cs_, sn_ = cos[at, :], sin[at, :]
            for p in range(G // 128):
                cols = slice(128 * p, 128 * p + 128)
                for j, (name, turn) in enumerate((("dq", True), ("dk", True), ("dv", False))):
                    u = n[name][at, cols]
                    if turn:
                        u = rope(u, cs_, sn_, -1.0)
                    u = u.astype(BF)
                    lo = j * G + 128 * p
                    raw[at, lo : lo + 128] = u
                    n["cs"][2:3, lo : lo + 128] += jnp.sum(u.astype(F32), axis=0, keepdims=True)

        loop(N // T, one)

        def put(at, value):
            n["dj"][at, :] = value[:, 0 : 3 * G]
            n["att_st"][at, :] = value[:, 3 * G : 4 * G]

        from_order(raw, put)

    def in_grad():
        def one(i):
            at = pl.ds(mult(i * 256, 256), 256)
            n["Gi"][at, :] = dot00(n["A1"][:, at], n["dj"][...]).astype(BF)

        loop(D // 256, one)

    def proj_grad():
        def one(i):
            at = pl.ds(mult(i * 256, 256), 256)
            n["Gp"][:, at] = dot00(n["att_st"][...], n["Gs"][:, at]).astype(BF)

        loop(D // 256, one)

    def mlp_up():
        def one(i):
            at = pl.ds(mult((i // 4) * T, T), T)
            cols = pl.ds(mult((i % 4) * 256, 256), 256)
            x = dot(n["A2"][at, :], n["Wu"][:, cols]) + vecs[6:7, cols]
            phi = 0.5 + 0.5 * lax.erf(x * math.sqrt(0.5))
            pdf = jnp.exp(-0.5 * x * x) * (1.0 / math.sqrt(2.0 * math.pi))
            n["act"][at, cols] = (x * phi).astype(BF)
            n["gp"][at, cols] = (phi + x * pdf).astype(BF)

        loop(16, one)

    def down_grad():
        def one(i):
            at = pl.ds(mult(i * 256, 256), 256)
            n["Gd"][at, :] = dot00(n["act"][:, at], n["Gs"][...]).astype(BF)

        loop(H // 256, one)

    def mlp_back():
        n["cs"][6:7, :] = jnp.zeros((1, D), F32)

        def one(i):
            at = pl.ds(mult((i // 4) * T, T), T)
            cols = pl.ds(mult((i % 4) * 256, 256), 256)
            da = dot11(n["Gs"][at, :], n["Wd"][cols, :])
            dl = (da * n["gp"][at, cols].astype(F32)).astype(BF)
            n["dl"][at, cols] = dl
            n["cs"][6:7, cols] += jnp.sum(dl.astype(F32), axis=0, keepdims=True)

        loop(16, one)

    def up_grad():
        def one(i):
            at = pl.ds(mult(i * 256, 256), 256)
            n["Gu"][at, :] = dot00(n["A2"][:, at], n["dl"][...]).astype(BF)

        loop(D // 256, one)

    def out_part():
        def one(i):
            at = pl.ds(mult(i * T, T), T)
            n["Po"][at, :] = (dot(n["att_st"][at, :], n["Wp"][...]) + dot(n["act"][at, :], n["Wd"][...])).astype(BF)

        loop(N // T, one)

    def input_part():
        for row in (0, 1, 4, 5):
            n["cs"][row : row + 1, :] = jnp.zeros((1, D), F32)

        def one(i):
            at = pl.ds(mult(i * T, T), T)
            nn = n["nb"][at, :].astype(F32)
            e1 = dot11(n["dj"][at, :], n["Wi"][...])
            n["cs"][0:1, :] += jnp.sum(e1 * nn, axis=0, keepdims=True)
            n["cs"][1:2, :] += jnp.sum(e1, axis=0, keepdims=True)
            e2 = dot11(n["dl"][at, :], n["Wu"][...])
            n["cs"][4:5, :] += jnp.sum(e2 * nn, axis=0, keepdims=True)
            n["cs"][5:6, :] += jnp.sum(e2, axis=0, keepdims=True)
            n["Pc"][at, :] = (e1 * vec(0) + e2 * vec(2)).astype(BF)

        loop(N // T, one)

    def own_g_sum():
        n["cs"][7:8, :] = jnp.zeros((1, D), F32)
        g = tile(n["Gs"], c * T, T).astype(F32)
        n["cs"][3:4, :] = jnp.sum(g, axis=0, keepdims=True)

    def finish_out():
        base = c * T
        x = tile(n["Xs"], base, T).astype(F32)
        total = tile(n["Po"], base, T).astype(F32) + n["r1"][0, 0:T].astype(F32) + n["r2"][0].astype(F32)
        n["xo"][...] = (x + total + vec(4) + vec(5)).astype(BF)

    def finish_input():
        base = c * T
        x = tile(n["Xs"], base, T).astype(F32)
        center = x - jnp.mean(x, axis=-1, keepdims=True)
        rstd = lax.rsqrt(jnp.mean(center * center, axis=-1, keepdims=True) + EPS)
        nn = center * rstd
        cc = tile(n["Pc"], base, T).astype(F32) + n["r1"][1, 0:T].astype(F32) + n["r2"][1].astype(F32)
        mean_c = jnp.mean(cc, axis=-1, keepdims=True)
        mean_cn = jnp.mean(cc * nn, axis=-1, keepdims=True)
        n["xg"][...] = tile(n["Gs"], base, T).astype(F32) + (cc - mean_c - nn * mean_cn) * rstd

    def unpack_vectors():
        for j in range(s.F):
            cols = slice(j * 128, (j + 1) * 128)
            n["vecs"][0:6, cols] = n["Wv"][j * VROWS : j * VROWS + 6, :]
            n["vecs"][6:7, cols] = n["Wv"][pl.ds(j * VROWS + 6 + c, 1), :]
        per = G // 128
        for j in range(3):
            for p in range(per):
                b = j * (D // 128) + c * per + p
                lo = (j * per + p) * 128
                n["vecs"][7:8, lo : lo + 128] = n["Wv"][pl.ds((b // 3) * VROWS + 6 + s.nctx + b % 3, 1), :]

    def pack_sums():
        n["Gv"][...] = jnp.zeros((s.F * VROWS, 128), F32)
        cs = n["cs"]
        for j in range(s.F):
            cols = slice(j * 128, (j + 1) * 128)
            base = j * VROWS
            for row, place in ((0, 0), (1, 1), (3, 5), (4, 6), (5, 7)):
                n["Gv"][base + place : base + place + 1, :] = cs[row : row + 1, cols]
            n["Gv"][pl.ds(base + 8 + c, 1), :] = cs[6:7, cols]
        per = G // 128
        for j in range(3):
            for p in range(per):
                b = j * (D // 128) + c * per + p
                lo = (j * per + p) * 128
                n["Gv"][pl.ds((b // 3) * VROWS + 2 + b % 3, 1), :] = cs[2:3, lo : lo + 128]

    def local(i, src, dst):
        return pltpu.make_async_copy(src, dst, n["loc"].at[i])

    own_i = wunit(W[IN], IN, zi, yi)
    own_u = wunit(W[UP], UP, zi, yi)
    hc = s.hc
    lc = {
        "x": [local(0, n["x"], rows(n["Xs"], c * T, T))],
        "i": [
            pltpu.make_async_copy(
                n["w_i"].at[:, pl.ds(mult(j * D + c * G, 128), G)], own_i.at[:, pl.ds(j * G, G)], n["loc_i"].at[j]
            )
            for j in range(3)
        ],
        "p": [local(3, n["w_p"], wunit(W[PROJ], PROJ, zi, yi))],
        "g": [local(4, n["g"], rows(n["Gs"], c * T, T))],
        "u": [local(5, n["w_u"], own_u)]
        if not s.packed
        else [
            pltpu.make_async_copy(
                n["w_u"].at[:, pl.ds(mult((j * s.nctx + c) * hc, 128), hc)],
                own_u.at[:, pl.ds(j * hc, hc)],
                n["loc_u"].at[j],
            )
            for j in range(s.F)
        ],
        "d": [local(6, rows(n["w_d"], c * hc, hc), wunit(W[DOWN], DOWN, zi, yi))],
    }
    if s.packed:
        lc["v"] = [local(2, n["vpack"], wunit(W[VEC], VEC, zi, yi))]

    def lstart(key):
        if key == "p":
            when(zi == c, lambda: each(lc[key], "start"))
        else:
            each(lc[key], "start")

    def lwait(key):
        if key == "p":
            when(zi == c, lambda: each(lc[key], "wait"))
        else:
            each(lc[key], "wait")

    for key in lc:
        lstart(key)
    bar = pltpu.get_barrier_semaphore()
    for dev in (sib, xn):
        pl.semaphore_signal(bar, inc=1, device_id=dev, device_id_type=MESH)
    for step in range(1, A):
        pl.semaphore_signal(bar, inc=1, device_id=(c, (zi + step) % A * B + yi), device_id_type=MESH)
    for d in (2, 3):
        when(
            edge[d],
            lambda d=d: pl.semaphore_signal(bar, inc=1, device_id=hop[d], device_id_type=MESH),
        )
    count = 2 + A - 1 + sum(jnp.where(e, 1, 0) for e in edge[2:])
    pl.semaphore_wait(bar, count)

    lwait("i")
    if s.packed:
        lwait("v")
        ag_start(VEC)
    ag_start(IN)
    for j in range(T // BLK):
        first = n["places"][0:1, j * BLK : j * BLK + 1] // BLK
        n["Bs"][pl.ds(c * 8 + j, 1), :] = jnp.broadcast_to(first, (1, D))
    xa_start(2)
    lwait("x")
    xa_start(0)
    lwait("p")
    ag_start(PROJ)
    lwait("g")
    lwait("u")
    lwait("d")
    if s.packed:
        for t in range(A - 1):
            ag_z(VEC, t)
        ag_y(VEC)
        unpack_vectors()
    norms(c)
    ag_z(IN, 0)
    xa_start(1)
    xa_wait(0, sib_c)
    norms(sib_c)
    ag_z(IN, 1)
    ag_start(UP)
    xa_fwd(2)
    xa_fwd(0)
    norms(xn_c)
    ag_z(IN, 2)
    for t in range(A - 1):
        ag_z(PROJ, t)
    xa_wait(0, xs_c)
    norms(xs_c)
    ag_z(UP, 0)
    ag_start(DOWN)
    xa_wait(2, sib_c)
    xa_wait(2, xs_c)
    tables()
    xa_fwd(1)
    ag_y(IN)
    qkv()
    ag_z(UP, 1)
    xa_wait(1, sib_c)
    xa_wait(1, xs_c)
    ag_y(PROJ)
    dattended()
    order()
    own_g_sum()
    zero_dkv()
    ag_z(UP, 2)
    pump = [lambda t=t: ag_z(DOWN, t) for t in range(A - 1)]
    for p in range(G // 128):
        for i in range(N // T):
            attention(p, i)
            if pump:
                pump.pop(0)()
    joined_back()
    proj_grad()
    ry_send(PROJ, 0, c)
    in_grad()
    ag_y(UP)
    mlp_up()
    down_grad()
    for zz in ry_zz(DOWN):
        ry_send(DOWN, 0, zz)
    ry_proj()
    ag_y(DOWN)
    mlp_back()
    up_grad()
    for zz in ry_zz(UP):
        ry_send(UP, 0, zz)
    rz_sum(PROJ)
    fa_start(PROJ)
    ry_unit(DOWN, 0)
    out_part()
    cr_start(0)
    ry_unit(DOWN, 1)
    input_part()
    cr_start(1)
    if s.packed:
        pack_sums()
        for zz in ry_zz(VEC):
            ry_send(VEC, 0, zz)
    for zz in ry_zz(IN):
        ry_send(IN, 0, zz)
    ry_unit(DOWN, 2)
    fa_fwd(PROJ)
    cr_mid(0)
    ry_unit(DOWN, 3)
    ry_unit(UP, 0)
    rz_sum(DOWN)
    fa_start(DOWN)
    cr_mid(1)
    ry_unit(UP, 1)
    ry_unit(UP, 2)
    cr_wait(0)
    finish_out()
    put_out = local(12, n["xo"], n["out"])
    put_out.start()
    ry_unit(UP, 3)
    fa_fwd(DOWN)
    if s.packed:
        for i in range(4):
            ry_unit(VEC, i)
    ry_unit(IN, 0)
    rz_sum(UP)
    fa_start(UP)
    if s.packed:
        rz_sum(VEC)
        fa_start(VEC)
    ry_unit(IN, 1)
    cr_wait(1)
    finish_input()
    put_in = local(13, n["xg"], n["input_grad"])
    put_in.start()
    ry_unit(IN, 2)
    fa_fwd(UP)
    if s.packed:
        fa_fwd(VEC)
    ry_unit(IN, 3)
    rz_sum(IN)
    fa_start(IN)
    fa_fwd(IN)
    for kind in s.kinds:
        fa_end(kind)
    if s.packed:
        n["vtot"][...] = sum(n["FV"][j * VROWS : (j + 1) * VROWS, :] for j in range(s.nctx))
    put_cs = local(14, n["vtot"] if s.packed else n["cs"], n["sums"])
    put_cs.start()
    for kind in s.kinds:
        ag_drain(kind)
        ry_drain(kind)
        rz_drain(kind)
    for arr in range(3):
        xa_drain(arr)
    for arr in range(2):
        cr_drain(arr)
    put_out.wait()
    put_in.wait()
    put_cs.wait()


def finish_kernel(s, hidden, *refs):
    gi, gp, gu, gd, out, input_grad, sums = refs[:7]
    to = refs[7:]
    to[0][...] = out[...]
    to[1][...] = input_grad[...]
    for src, dst in zip((gi, gp, gu, gd), to[2:6]):
        dst[...] = src[...].astype(F32)
    singles = ((0, 6), (1, 7), (5, 8), (6, 9), (7, 10), (5, 11))
    for row, at in singles:
        to[at][...] = sums[row : row + 1, :]
    for first, count, at in ((2, 3, 12), (8, s.nctx, 13)):
        for j in range(count):
            to[at][:, j * 128 : (j + 1) * 128] = sums[first + j : first + j + 1, :]


def finish(s, hidden, arrays):
    steps = max(1, s.R // 32)

    def part(shape):
        return pl.BlockSpec((shape[0] // steps, shape[1]), lambda i: (i, 0))

    def whole(shape):
        return pl.BlockSpec(shape, lambda i: (0, 0))

    D = s.D
    shapes = [(s.T, D), (s.T, D), (s.R, 3 * D), (s.R, D), (s.R, hidden), (hidden // s.F, D)]
    types = [BF, F32, F32, F32, F32, F32]
    small = [(1, 128)] * 6 + [(1, 3 * s.R), (1, hidden // s.F)]
    return pl.pallas_call(
        lambda *refs: finish_kernel(s, hidden, *refs),
        grid=(steps,),
        out_shape=tuple(jax.ShapeDtypeStruct(sh, dt) for sh, dt in zip(shapes + small, types + [F32] * 8)),
        in_specs=[part(a.shape) for a in arrays[:-1]] + [whole(arrays[-1].shape)],
        out_specs=tuple([part(sh) for sh in shapes] + [whole(sh) for sh in small]),
        compiler_params=pltpu.CompilerParams(vmem_limit_bytes=63 << 20),
        name="finish",
    )(*arrays)


def rope_tables(length):
    half = ROT // 2
    freq = np.power(np.float32(10000.0), np.float32(-2.0) * np.arange(half, dtype=np.float32) / np.float32(ROT))
    angle = np.arange(length, dtype=np.float32)[:, None] * freq[None, :].astype(np.float32)
    cos = np.ones((length, 128), np.float32)
    sin = np.zeros((length, 128), np.float32)
    for base in range(0, 128, HEAD_DIM):
        cos[:, base : base + half] = np.cos(angle)
        cos[:, base + half : base + ROT] = np.cos(angle)
        sin[:, base : base + half] = -np.sin(angle)
        sin[:, base + half : base + ROT] = np.sin(angle)
    return cos, sin


def body(
    hidden_in,
    positions,
    out_grad,
    attn_gain,
    attn_shift,
    in_weight,
    in_bias,
    proj_weight,
    proj_bias,
    mlp_gain,
    mlp_shift,
    up_weight,
    up_bias,
    down_weight,
    down_bias,
):
    nctx, nshard = lax.axis_size("ctx"), lax.axis_size("fsdp")
    T, D = hidden_in.shape[1:]
    hidden = up_weight.shape[1]
    s = Sizes(T, D, hidden, nctx, nshard)
    R, G, F = s.R, s.G, s.F
    hc = s.hc
    c, f = lax.axis_index("ctx"), lax.axis_index("fsdp")

    def pick_ctx(array, axis):
        return lax.dynamic_index_in_dim(array, c, axis, keepdims=False)

    small = [attn_gain, attn_shift, mlp_gain, mlp_shift, proj_bias, down_bias, up_bias, in_bias]
    if s.packed:
        w_u = up_weight
        flat, at = 0.0, 0
        for v in small:
            flat = flat + jnp.pad(v.astype(F32), (at, VROWS * 128 - at - v.shape[0]))
            at += v.shape[0]
        extra = dict(vpack=flat.reshape(VROWS, 128))
    else:
        w_u = pick_ctx(up_weight.reshape(R, F, nctx, hc), 2).reshape(R, s.H)
        lengths = [v.shape[0] for v in small]
        gathered = lax.all_gather(jnp.concatenate(small).astype(F32), "fsdp", axis=0)
        full, at = [], 0
        for length in lengths:
            full.append(gathered[:, at : at + length].reshape(-1))
            at += length
        full[6] = pick_ctx(full[6].reshape(F, nctx, hc), 1).reshape(-1)
        full[7] = jnp.pad(pick_ctx(full[7].reshape(3, nctx, G), 1).reshape(-1), (0, D - 3 * G))
        extra = dict(vecs=jnp.stack(full))
    cos, sin = rope_tables(s.N)

    plan = scratch_plan(s)
    any_ = pl.BlockSpec(memory_space=pl.ANY)
    vmem = pl.BlockSpec(memory_space=pltpu.VMEM)
    ins = dict(
        x=hidden_in[0],
        g=out_grad[0],
        places=positions,
        w_i=in_weight,
        w_p=proj_weight,
        w_u=w_u,
        w_d=down_weight,
        **extra,
        cos=jnp.asarray(cos),
        sin=jnp.asarray(sin),
    )
    in_vmem = {"vecs", "cos", "sin", "places"}
    outs = dict(
        out=jax.ShapeDtypeStruct((T, D), BF),
        input_grad=jax.ShapeDtypeStruct((T, D), F32),
        out_i=jax.ShapeDtypeStruct((R, 3 * D), BF),
        out_p=jax.ShapeDtypeStruct((R, D), BF),
        out_u=jax.ShapeDtypeStruct((R, hidden) if s.packed else (nctx * R, s.H), BF),
        out_d=jax.ShapeDtypeStruct((nctx * hc, D), BF),
        sums=jax.ShapeDtypeStruct((VROWS, 128) if s.packed else (8, D), F32),
    )
    names = list(ins) + list(outs) + list(plan)
    out, input_grad, gi, gp, gu, gd, sums = pl.pallas_call(
        lambda *refs: kernel_body(s, names, *refs),
        out_shape=tuple(outs.values()),
        in_specs=[vmem if name in in_vmem else any_ for name in ins],
        out_specs=tuple(any_ for _ in outs),
        scratch_shapes=list(plan.values()),
        compiler_params=pltpu.CompilerParams(
            collective_id=0, has_side_effects=True, vmem_limit_bytes=63 << 20
        ),
        name="block",
    )(*ins.values())

    def own(full_vector):
        length = full_vector.shape[0] // F
        return lax.dynamic_slice_in_dim(full_vector, f * length, length)

    if s.packed:
        done = finish(s, hidden, (gi, gp, gu, gd, out, input_grad, sums))
        out, input_grad, in_total, proj_total, up_total, down_total = done[:6]
        gain1, shift1, g_sum, gain2, shift2, g_again, in_bias_sum, up_bias_sum = (v.reshape(-1) for v in done[6:])
    else:
        here = (jnp.arange(nctx) == c).astype(F32)
        in_b = (sums[2, : 3 * G].reshape(3, 1, G) * here[None, :, None]).reshape(-1)
        up_b = (sums[6].reshape(F, 1, hc) * here[None, :, None]).reshape(-1)
        total = lax.psum(
            jnp.concatenate([sums[0], sums[1], in_b, sums[3], sums[4], sums[5], up_b]), ("ctx", "fsdp")
        )
        parts, at = [], 0
        for length in (D, D, 3 * D, D, D, D, hidden):
            parts.append(own(total[at : at + length]))
            at += length
        gain1, shift1, in_bias_sum, g_sum, gain2, shift2, up_bias_sum = parts
        g_again = g_sum
        in_total, proj_total, down_total = gi.astype(F32), gp.astype(F32), gd.astype(F32)
        up_total = gu.astype(F32).reshape(nctx, R, F, hc).transpose(1, 2, 0, 3).reshape(R, hidden)
    return (
        out[None],
        input_grad[None],
        gain1,
        shift1,
        in_total,
        in_bias_sum,
        proj_total,
        g_sum,
        gain2,
        shift2,
        up_total,
        up_bias_sum,
        down_total,
        g_again,
    )


def solution(mesh):
    tok, vec, mat = P("fsdp", "ctx", None), P("fsdp"), P("fsdp", None)
    placed = (tok, P("fsdp", "ctx"), tok, vec, vec, mat, vec, mat, vec, vec, vec, mat, vec, mat, vec)
    return jax.shard_map(
        body,
        mesh=mesh,
        in_specs=placed,
        out_specs=(tok, tok, vec, vec, mat, vec, mat, vec, vec, vec, mat, vec, mat, vec),
        check_vma=False,
    )
```

```python
import math

import jax
import jax.numpy as jnp
import numpy as np
from jax import lax
from jax.experimental import pallas as pl
from jax.experimental.pallas import tpu as pltpu
from jax.sharding import PartitionSpec as P

HEADS = 16
HEAD_DIM = 64
ROT = 16
BLK = 128
EPS = 1e-05
MESH = pl.DeviceIdType.MESH
BF = jnp.bfloat16
F32 = jnp.float32
IN, PROJ, UP, DOWN, VEC, CROSS = range(6)
NAMES = "ipudve"
VROWS = 16
BOTH1 = (((1,), (1,)), ((), ()))
BOTH0 = (((0,), (0,)), ((), ()))


def dot(a, b):
    return jnp.dot(a, b, preferred_element_type=F32)


def dot11(a, b):
    return lax.dot_general(a, b, BOTH1, preferred_element_type=F32)


def dot00(a, b):
    return lax.dot_general(a, b, BOTH0, preferred_element_type=F32)


def mult(value, of):
    return pl.multiple_of(value, of)


def both(*conds):
    out = conds[0]
    for cond in conds[1:]:
        out = jnp.logical_and(out, cond)
    return out


class Sizes:
    def __init__(self, tokens, width, hidden, nctx, nshard):
        self.T = tokens
        self.N = tokens * nctx
        self.D = width
        self.H = hidden // nctx
        self.G = width // nctx
        self.nctx = nctx
        self.F = nshard
        self.A = nctx
        self.B = nshard // nctx
        self.R = width // nshard
        self.hc = hidden // nshard // nctx
        self.packed = self.R % 128 == 0 and self.hc % 128 == 0
        half = self.hc // 2
        self.buffer = ("i", "p", "u", "d", "v", "d")
        self.stride = (self.R, self.R, self.R, self.hc, VROWS, self.hc)
        self.offset = (0, 0, 0, 0, 0, self.hc - half)
        self.rows = (self.R, self.R, self.R, self.hc - half, VROWS, half)
        self.cols = (3 * self.G, width, self.H, width, 128, width)
        self.units = (self.F, self.B, self.F, self.F, self.F, self.F)
        self.types = (BF, BF, BF, BF, F32, BF)
        self.kinds = (IN, PROJ, UP, DOWN, CROSS) + ((VEC,) if self.packed else ())
        self.NY = 1 if self.B == 2 else self.B + 1


def scratch_plan(s):
    N, D, G, H = s.N, s.D, s.G, s.H
    vm = pltpu.VMEM
    dma = pltpu.SemaphoreType.DMA
    plan = dict(
        Xs=vm((N, D), BF),
        Gs=vm((N, D), BF),
        Bs=vm((s.nctx * 8, D), jnp.int32),
        cos_st=vm((N, 128), F32),
        sin_st=vm((N, 128), F32),
        nb=vm((N, D), BF),
        A1=vm((N, D), BF),
        A2=vm((N, D), BF),
        S=vm((N, 4 * G), BF),
        dq=vm((N, G), F32),
        dk=vm((N, G), F32),
        dv=vm((N, G), F32),
        att_st=vm((N, G), BF),
        dj=vm((N, 3 * G), BF),
        act=vm((N, H), BF),
        gp=vm((N, H), BF),
        dl=vm((N, H), BF),
        Po=vm((N, D), BF),
        Pc=vm((N, D), BF),
        r1=vm((2, 2 * s.T, D), BF),
        r2=vm((2, s.T, D), BF),
        cs=vm((8, D), F32),
        xo=vm((s.T, D), BF),
        xg=vm((s.T, D), F32),
    )
    if s.packed:
        plan["vecs"] = vm((8, D), F32)
        plan["FV"] = vm((s.nctx * VROWS, 128), F32)
        plan["vtot"] = vm((VROWS, 128), F32)
    A, B, F = s.A, s.B, s.F
    for kind in s.kinds:
        name = NAMES[kind]
        r, cl = s.rows[kind], s.cols[kind]
        dt = s.types[kind]
        if kind != CROSS:
            size = (s.units[kind] * s.stride[kind], cl)
            plan["W" + name] = vm(size, dt)
            plan["G" + name] = vm(size, dt)
        cross, proj = kind == CROSS, kind == PROJ
        per = 1 if cross or proj else A
        cols = B if cross else 1
        plan["Y" + name] = vm((s.NY * per * r, cl), dt)
        plan["Z" + name] = vm((A * B * r if kind == VEC else 3 * cols * r, cl), dt)
        along_y = per if B == 2 else 2 * per * B
        plan["az" + name] = dma(((2 if proj else A + 1) * cols,))
        plan["ay" + name] = dma((along_y,))
        plan["ar" + name] = dma((s.units[kind],))
        plan["ys" + name] = dma((along_y,))
        plan["yr" + name] = dma((along_y,))
        plan["zs" + name] = dma((A if kind == VEC else 3 * cols,))
        plan["zr" + name] = dma((A if kind == VEC else 3 * cols,))
    plan.update(
        xa_s=dma((3, 3)),
        xa_r=dma((3, s.nctx)),
        cr_s=dma((2, 3)),
        cr_r=dma((2, 3)),
        fa_s=dma((6, 3)),
        fa_r=dma((6, 3)),
        fa_l=dma((6,)),
        loc=dma((16,)),
        loc_i=dma((3,)),
        loc_u=dma((s.F if s.packed else 1,)),
    )
    return plan


def kernel_body(s, names, *refs):
    n = dict(zip(names, refs))
    T, N, D, G, H, A, B, R = s.T, s.N, s.D, s.G, s.H, s.A, s.B, s.R
    c = lax.axis_index("ctx")
    f = lax.axis_index("fsdp")
    zi, yi = f // B, f % B
    sib_c = c + 1 - 2 * (c % 2)
    xn_c = (c + s.nctx // 2) % s.nctx
    xs_c = (sib_c + s.nctx // 2) % s.nctx
    sib, xn = (sib_c, f), (xn_c, f)
    edge = (zi < A - 1, zi > 0, yi < B - 1, yi > 0)
    hop = ((c, f + B), (c, f - B), (c, f + 1), (c, f - 1))

    def when(cond, fn):
        pl.when(cond)(fn)

    def rcopy(src, dst, ssem, rsem, dev):
        return pltpu.make_async_remote_copy(
            src_ref=src, dst_ref=dst, send_sem=ssem, recv_sem=rsem, device_id=dev, device_id_type=MESH
        )

    def rows(ref, start, size):
        return ref.at[pl.ds(mult(start, size), size)]

    W = [n.get("W" + x) for x in s.buffer]

    def has(kind, oz):
        return (oz == c) if kind == PROJ else (oz == oz)

    def wunit(ref, kind, oz, oy):
        at = oy if kind == PROJ else oz * B + oy
        return rows(ref, at * s.stride[kind] + s.offset[kind], s.rows[kind])

    def along_y(kind, oz, oy, d):
        per = 1 if kind in (PROJ, CROSS) else A
        at = 0 if per == 1 else oz
        return at if B == 2 else (d * per + at) * B + oy

    def ag_copy(kind, oz, oy, d):
        u = wunit(W[kind], kind, oz, oy)
        name = NAMES[kind]
        if d >= 2:
            send = n["ay" + name].at[along_y(kind, oz, oy, d - 2)]
        elif kind == PROJ:
            send = n["az" + name].at[d]
        else:
            at = oz if d == 0 else jnp.where(oz == zi, A, oz)
            send = n["az" + name].at[at + (oy * (A + 1) if kind == CROSS else 0)]
        return rcopy(u, u, send, n["ar" + name].at[oy if kind == PROJ else oz * B + oy], hop[d])

    def va_copy(source, oz):
        u = wunit(W[VEC], VEC, source, yi)
        return rcopy(
            u, u, n["azv"].at[oz], n["arv"].at[source * B + yi], (c, oz * B + yi)
        )

    def va_start():
        for oz in range(A):
            when(zi != oz, lambda oz=oz: va_copy(zi, oz).start())
        for d in (2, 3):
            when(edge[d], lambda d=d: ag_copy(VEC, zi, yi, d).start())

    def va_z():
        for i in range(1, A):
            oz = (zi + i) % A
            va_copy(oz, zi).wait_recv()
            for d in (2, 3):
                when(edge[d], lambda d=d, oz=oz: ag_copy(VEC, oz, yi, d).start())

    def va_drain():
        for oz in range(A):
            when(zi != oz, lambda oz=oz: va_copy(zi, oz).wait_send())
        for oz in range(A):
            for oy in range(B):
                when(both(oy <= yi, edge[2]), lambda oz=oz, oy=oy: ag_copy(VEC, oz, oy, 2).wait_send())
                when(both(oy >= yi, edge[3]), lambda oz=oz, oy=oy: ag_copy(VEC, oz, oy, 3).wait_send())

    def ag_start(kind):
        for d in range(4):
            when(both(has(kind, zi), edge[d]), lambda d=d: ag_copy(kind, zi, yi, d).start())

    def ag_z(kind, t):
        for i in range(B if kind == CROSS else 1):
            oy = (yi + i) % B if i else yi
            for sign, d in ((-1, 0), (1, 1)):
                oz = zi + sign * (1 + t)

                def go(oz=oz, d=d, oy=oy):
                    ag_copy(kind, oz, oy, d).wait_recv()
                    for dd in (d,) if kind == CROSS else (d, 2, 3):
                        when(edge[dd], lambda dd=dd: ag_copy(kind, oz, oy, dd).start())

                when(both(oz >= 0, oz < A, has(kind, oz)), go)

    def ag_y(kind):
        for t in range(B - 1):
            for zz in {PROJ: [c], CROSS: [zi]}.get(kind, list(range(A))):
                for sign, d in ((-1, 2), (1, 3)):
                    oy = yi + sign * (1 + t)

                    def go(oy=oy, d=d, zz=zz):
                        ag_copy(kind, zz, oy, d).wait_recv()
                        onward = ([d] if B > 2 else []) + ([0, 1] if kind == CROSS else [])
                        for dd in onward:
                            when(edge[dd], lambda dd=dd: ag_copy(kind, zz, oy, dd).start())

                    when(both(oy >= 0, oy < B), go)

    def ag_drain(kind):
        for oz in [c] if kind == PROJ else list(range(A)):
            for oy in range(B) if kind == CROSS else [yi]:
                when(both(oz <= zi, edge[0]), lambda oz=oz, oy=oy: ag_copy(kind, oz, oy, 0).wait_send())
                when(both(oz >= zi, edge[1]), lambda oz=oz, oy=oy: ag_copy(kind, oz, oy, 1).wait_send())
        for oz in {PROJ: [c], CROSS: [zi]}.get(kind, list(range(A))):
            for oy in range(B):
                when(both(oy <= yi, edge[2]), lambda oz=oz, oy=oy: ag_copy(kind, oz, oy, 2).wait_send())
                when(both(oy >= yi, edge[3]), lambda oz=oz, oy=oy: ag_copy(kind, oz, oy, 3).wait_send())

    XA = ((n["Xs"], T), (n["Gs"], T), (n["Bs"], 8))

    def xa_copy(arr, slot, which):
        ref, r = XA[arr]
        u = rows(ref, slot * r, r)
        return rcopy(u, u, n["xa_s"].at[arr, which], n["xa_r"].at[arr, slot], (xn, sib)[which != 0])

    def xa_start(arr):
        xa_copy(arr, c, 0).start()
        xa_copy(arr, c, 1).start()

    def xa_wait(arr, slot):
        xa_copy(arr, slot, 0).wait_recv()

    def xa_fwd(arr):
        xa_wait(arr, xn_c)
        xa_copy(arr, xn_c, 2).start()

    def xa_drain(arr):
        xa_copy(arr, c, 0).wait_send()
        xa_copy(arr, c, 1).wait_send()
        xa_copy(arr, xn_c, 2).wait_send()

    GR = [n.get("G" + x) for x in s.buffer]
    YB = [n.get("Y" + x) for x in NAMES]
    ZB = [n.get("Z" + x) for x in NAMES]

    def add_into(dst, src):
        dst[...] = (dst[...].astype(F32) + src[...].astype(F32)).astype(dst.dtype)

    def ry_slot(kind, zz, target, d, receiver):
        r = s.rows[kind]
        per = 1 if kind in (PROJ, CROSS) else A
        at = 0 if per == 1 else zz
        if B == 2:
            slot = 0
        elif d == 0:
            slot = target
        else:
            slot = jnp.where(receiver == target, B, target)
        return rows(YB[kind], (slot * per + at) * r, r)

    def ry_copy(kind, zz, target, d, receiver):
        at = along_y(kind, zz, target, d)
        return rcopy(
            wunit(GR[kind], kind, zz, target),
            ry_slot(kind, zz, target, d, receiver),
            n["ys" + NAMES[kind]].at[at],
            n["yr" + NAMES[kind]].at[at],
            hop[2 + d],
        )

    pair_z = zi + 1 - 2 * (zi % 2)
    far_z = (zi + A // 2) % A
    diag_z = (pair_z + A // 2) % A
    by_step = [diag_z, pair_z, far_z, zi]

    def ry_zz(kind):
        return {PROJ: [c], CROSS: [zi], VEC: [zi]}.get(kind, by_step)

    def ry_send(kind, t, zz):
        hi, lo = B - 1 - t, t
        when(yi == 0, lambda: ry_copy(kind, zz, hi, 0, yi + 1).start())
        when(yi == B - 1, lambda: ry_copy(kind, zz, lo, 1, yi - 1).start())

    def ry_recv(kind, t, zz):
        hi, lo = B - 1 - t, t
        for target, d, cond, onward in (
            (hi, 0, both(yi > 0, yi <= hi), both(yi > 0, yi < hi)),
            (lo, 1, both(yi < B - 1, yi >= lo), both(yi < B - 1, yi > lo)),
        ):

            def go(target=target, d=d):
                ry_copy(kind, zz, target, d, yi).wait_recv()
                add_into(wunit(GR[kind], kind, zz, target), ry_slot(kind, zz, target, d, yi))

            when(cond, go)
            if B > 2:
                when(
                    onward,
                    lambda target=target, d=d: ry_copy(
                        kind, zz, target, d, yi + 1 - 2 * d
                    ).start(),
                )

    def ry_drain(kind):
        for zz in {PROJ: [c], CROSS: [zi], VEC: [zi]}.get(kind, list(range(A))):
            for target in range(B):
                when(yi < target, lambda zz=zz, target=target: ry_copy(kind, zz, target, 0, yi + 1).wait_send())
                when(yi > target, lambda zz=zz, target=target: ry_copy(kind, zz, target, 1, yi - 1).wait_send())

    def rz_cols(kind):
        return [(yi + i) % B for i in range(B)] if kind == CROSS else [yi]

    def rz_slot(kind, which, col):
        r = s.rows[kind]
        return rows(ZB[kind], (which * B + col if kind == CROSS else which) * r, r)

    def rz_copy(kind, which, col):
        at = which * B + col if kind == CROSS else which
        return rcopy(
            wunit(GR[kind], kind, by_step[which], col),
            rz_slot(kind, which, col),
            n["zs" + NAMES[kind]].at[at],
            n["zr" + NAMES[kind]].at[at],
            (c, (pair_z, pair_z, far_z)[which] * B + yi),
        )

    def rz_take(kind, which, target, col):
        rz_copy(kind, which, col).wait_recv()
        add_into(wunit(GR[kind], kind, target, col), rz_slot(kind, which, col))

    def rz_pair(kind, which):
        def go():
            for col in rz_cols(kind):
                rz_copy(kind, which, col).start()

        when(has(kind, by_step[which]), go)

    def rz_far(kind):
        def go():
            for col in rz_cols(kind):
                rz_take(kind, 0, far_z, col)
                rz_copy(kind, 2, col).start()

        when(has(kind, far_z), go)

    def rz_sum(kind):
        def go():
            for col in rz_cols(kind):
                rz_take(kind, 1, zi, col)
                rz_take(kind, 2, zi, col)

        when(has(kind, zi), go)

    def rz_drain(kind):
        for which in range(3):

            def go(which=which):
                for col in rz_cols(kind):
                    rz_copy(kind, which, col).wait_send()

            when(has(kind, by_step[which]), go)

    def ry_first(kind):
        for t in range(B - 2):
            for zz in ry_zz(kind):
                if t:
                    ry_send(kind, t, zz)
                ry_recv(kind, t, zz)
        if B > 2:
            for zz in ry_zz(kind):
                ry_send(kind, B - 2, zz)

    def ry_start(kind):
        if kind in s.kinds:
            for zz in ry_zz(kind):
                ry_send(kind, 0, zz)

    def ry_unit(kind, i):
        if i == 0:
            ry_first(kind)
        ry_recv(kind, B - 2, by_step[i])
        if i < 2:
            rz_pair(kind, i)

    def vs_copy(source, target):
        return rcopy(
            rows(GR[VEC], target * B * VROWS, B * VROWS),
            rows(ZB[VEC], source * B * VROWS, B * VROWS),
            n["zsv"].at[target],
            n["zrv"].at[source],
            (c, target * B + yi),
        )

    def vs_start():
        for i in range(1, A):
            vs_copy(zi, (zi + i) % A).start()

    def vs_sum():
        mine = rows(GR[VEC], zi * B * VROWS, B * VROWS)
        for i in range(1, A):
            source = (zi + i) % A
            vs_copy(source, zi).wait_recv()
            add_into(mine, rows(ZB[VEC], source * B * VROWS, B * VROWS))

    def vs_drain():
        for i in range(1, A):
            vs_copy(zi, (zi + i) % A).wait_send()

    def ry_vec():
        ry_first(VEC)
        ry_recv(VEC, B - 2, zi)

    def ry_cross():
        ry_first(CROSS)
        ry_recv(CROSS, B - 2, zi)

    def ry_proj():
        ry_first(PROJ)
        ry_recv(PROJ, B - 2, c)
        rz_pair(PROJ, 0)
        rz_pair(PROJ, 1)

    def fa_has(kind, slot):
        return (zi == slot) if kind == PROJ else (c == c)

    def fa_dst(kind, slot):
        if kind == VEC:
            return rows(n["FV"], slot * VROWS, VROWS)
        if kind == PROJ:
            return n["out_p"]
        out = n["out_" + s.buffer[kind]]
        if s.buffer[kind] == "d":
            return rows(out, slot * s.hc + s.offset[kind], s.rows[kind])
        return out.at[slot]

    def fa_copy(kind, slot, which):
        src = wunit(GR[kind], kind, zi, yi) if which < 2 else fa_dst(kind, slot)
        return rcopy(
            src, fa_dst(kind, slot), n["fa_s"].at[kind, which], n["fa_r"].at[kind, which], (sib, xn, sib)[which]
        )

    def fa_local(kind):
        return pltpu.make_async_copy(wunit(GR[kind], kind, zi, yi), fa_dst(kind, c), n["fa_l"].at[kind])

    def each(copies, what):
        for copy in copies:
            getattr(copy, what)()

    def fa_start(kind):
        def go():
            fa_copy(kind, c, 1).start()
            fa_copy(kind, c, 0).start()
            fa_local(kind).start()

        when(fa_has(kind, c), go)

    def fa_fwd(kind):
        def go():
            fa_copy(kind, xn_c, 1).wait_recv()
            fa_copy(kind, xn_c, 2).start()

        when(fa_has(kind, xn_c), go)

    def fa_end(kind):
        when(fa_has(kind, sib_c), lambda: fa_copy(kind, sib_c, 0).wait_recv())
        when(fa_has(kind, xs_c), lambda: fa_copy(kind, xs_c, 2).wait_recv())

        def own():
            fa_copy(kind, c, 1).wait_send()
            fa_copy(kind, c, 0).wait_send()
            fa_local(kind).wait()

        when(fa_has(kind, c), own)
        when(fa_has(kind, xn_c), lambda: fa_copy(kind, xn_c, 2).wait_send())

    PC = (n["Po"], n["Pc"])

    def cr_copy(arr, which, slot):
        if which < 2:
            return rcopy(
                rows(PC[arr], slot * T, T),
                n["r1"].at[arr, pl.ds(which * T, T)],
                n["cr_s"].at[arr, which],
                n["cr_r"].at[arr, which],
                sib,
            )
        return rcopy(rows(PC[arr], slot * T, T), n["r2"].at[arr], n["cr_s"].at[arr, 2], n["cr_r"].at[arr, 2], xn)

    def cr_start(arr):
        cr_copy(arr, 1, xs_c).start()
        cr_copy(arr, 0, sib_c).start()

    def cr_mid(arr):
        cr_copy(arr, 1, xs_c).wait_recv()
        add_into(rows(PC[arr], xn_c * T, T), n["r1"].at[arr, pl.ds(T, T)])
        cr_copy(arr, 2, xn_c).start()

    def cr_wait(arr):
        cr_copy(arr, 0, sib_c).wait_recv()
        cr_copy(arr, 2, xn_c).wait_recv()

    def cr_drain(arr):
        cr_copy(arr, 1, xs_c).wait_send()
        cr_copy(arr, 0, sib_c).wait_send()
        cr_copy(arr, 2, xn_c).wait_send()

    vecs, cos, sin = n["vecs"], n["cos"], n["sin"]

    def vec(row, width=D):
        return vecs[row : row + 1, 0:width]

    def loop(count, fn, first=0):
        def step(i, carry):
            fn(i)
            return carry

        lax.fori_loop(first, count, step, 0)

    def tile(ref, start, size, cols=slice(None)):
        return ref[pl.ds(mult(start, size), size), cols]

    def here(j, k, width):
        at = 8 * (j // 2) + j % 2
        return jnp.where(n["Bs"][at : at + 1, 0:width] == k, 1.0, 0.0)

    def to_order(dst, src):
        def one(k):
            total = None
            for j in range(2 * s.nctx):
                w = here(j, k, src.shape[1]).astype(src.dtype)
                term = src[j * BLK : (j + 1) * BLK, :] * w
                total = term if total is None else total + term
            dst[pl.ds(mult(k * BLK, BLK), BLK), :] = total

        loop(2 * s.nctx, one)

    def from_order(src, put):
        for j in range(2 * s.nctx):
            total = None
            for k in range(2 * s.nctx):
                w = here(j, k, src.shape[1]).astype(src.dtype)
                term = src[k * BLK : (k + 1) * BLK, :] * w
                total = term if total is None else total + term
            put(slice(j * BLK, (j + 1) * BLK), total)

    def norms(slot):
        def one(i):
            at = pl.ds(mult(slot * T + i * BLK, BLK), BLK)
            x = n["Xs"][at, :].astype(F32)
            center = x - jnp.mean(x, axis=-1, keepdims=True)
            nn = center * lax.rsqrt(jnp.mean(center * center, axis=-1, keepdims=True) + EPS)
            n["nb"][at, :] = nn.astype(BF)
            n["A1"][at, :] = (nn * vec(0) + vec(1)).astype(BF)
            n["A2"][at, :] = (nn * vec(2) + vec(3)).astype(BF)

        loop(T // BLK, one)

    lane64 = lax.broadcasted_iota(jnp.int32, (T, 128), 1) % HEAD_DIM
    first_half = lane64 < ROT // 2

    def rope(u, cs_, sn_, sign):
        partner = jnp.where(first_half, pltpu.roll(u, 128 - ROT // 2, 1), pltpu.roll(u, ROT // 2, 1))
        return u * cs_ + (partner * sn_) * sign

    def tables():
        def put(name):
            def store(at, value):
                n[name][at, :] = value

            return store

        from_order(cos, put("cos_st"))
        from_order(sin, put("sin_st"))

    raw, S = n["Pc"], n["S"]

    def qkv():
        def one(i):
            at = pl.ds(mult(i * T, T), T)
            j = dot(n["A1"][at, :], n["Wi"][...]) + vec(7, 3 * G)
            cs_, sn_ = n["cos_st"][at, :], n["sin_st"][at, :]
            for p in range(G // 128):
                lo = 128 * p
                q = rope(j[:, lo : lo + 128], cs_, sn_, 1.0).astype(BF)
                raw[at, lo : lo + 128] = (q.astype(F32) * HEAD_DIM**-0.5).astype(BF)
                raw[at, G + lo : G + lo + 128] = rope(j[:, G + lo : G + lo + 128], cs_, sn_, 1.0).astype(BF)
            raw[at, 2 * G : 3 * G] = j[:, 2 * G : 3 * G].astype(BF)

        loop(N // T, one)

    def dattended():
        def one(i):
            at = pl.ds(mult(i * T, T), T)
            raw[at, 3 * G : 4 * G] = dot11(n["Gs"][at, :], n["Wp"][...]).astype(BF)

        loop(N // T, one)

    def order():
        to_order(S, raw)

    def zero_dkv():
        n["dk"][...] = jnp.zeros((N, G), F32)
        n["dv"][...] = jnp.zeros((N, G), F32)

    def attention(p, i):
        L = (i + 1) * T
        cols = slice(128 * p, 128 * p + 128)
        at = slice(i * T, i * T + T)
        part = [slice(j * G + 128 * p, j * G + 128 * p + 128) for j in range(4)]
        kb, vb = S[0:L, part[1]], S[0:L, part[2]]
        qb, db = S[at, part[0]], S[at, part[3]]
        lane = lax.broadcasted_iota(jnp.int32, (T, 128), 1)
        key_at = lax.broadcasted_iota(jnp.int32, (T, T), 0)
        query_at = lax.broadcasted_iota(jnp.int32, (T, T), 1)
        keep = key_at <= query_at
        outs, dqs, ps, ds_, qs, dbs = [], [], [], [], [], []
        for h in range(2):
            mine = (lane >= HEAD_DIM) if h else (lane < HEAD_DIM)
            qh = jnp.where(mine, qb, jnp.zeros_like(qb))
            dh = jnp.where(mine, db, jnp.zeros_like(db))
            sc = dot11(kb, qh)
            last = jnp.where(keep, sc[L - T :], -1e30)
            sc = last if i == 0 else jnp.concatenate([sc[: L - T], last], axis=0)
            e = jnp.exp(sc - jnp.max(sc, axis=0, keepdims=True))
            pr = e * (1.0 / jnp.sum(e, axis=0, keepdims=True))
            dp = dot11(vb, dh)
            delta = jnp.sum(pr * dp, axis=0, keepdims=True)
            dsl = (pr * (dp - delta)).astype(BF)
            pb = pr.astype(BF)
            outs.append(dot00(vb, pb))
            dqs.append(dot00(kb, dsl))
            n["dv"][0:L, cols] += dot(pb, dh)
            n["dk"][0:L, cols] += dot(dsl, qh)
        feature = lax.broadcasted_iota(jnp.int32, (128, T), 0)
        raw[at, part[3]] = jnp.where(feature < HEAD_DIM, outs[0], outs[1]).T.astype(BF)
        n["dq"][at, cols] = jnp.where(feature < HEAD_DIM, dqs[0], dqs[1]).T * HEAD_DIM**-0.5

    def joined_back():
        n["cs"][2:3, :] = jnp.zeros((1, D), F32)

        def one(i):
            at = pl.ds(mult(i * T, T), T)
            cs_, sn_ = cos[at, :], sin[at, :]
            for p in range(G // 128):
                cols = slice(128 * p, 128 * p + 128)
                for j, (name, turn) in enumerate((("dq", True), ("dk", True), ("dv", False))):
                    u = n[name][at, cols]
                    if turn:
                        u = rope(u, cs_, sn_, -1.0)
                    u = u.astype(BF)
                    lo = j * G + 128 * p
                    raw[at, lo : lo + 128] = u
                    n["cs"][2:3, lo : lo + 128] += jnp.sum(u.astype(F32), axis=0, keepdims=True)

        loop(N // T, one)

        def put(at, value):
            n["dj"][at, :] = value[:, 0 : 3 * G]
            n["att_st"][at, :] = value[:, 3 * G : 4 * G]

        from_order(raw, put)

    def in_grad():
        def one(i):
            at = pl.ds(mult(i * 256, 256), 256)
            n["Gi"][at, :] = dot00(n["A1"][:, at], n["dj"][...]).astype(BF)

        loop(D // 256, one)

    def proj_grad():
        def one(i):
            at = pl.ds(mult(i * 256, 256), 256)
            n["Gp"][:, at] = dot00(n["att_st"][...], n["Gs"][:, at]).astype(BF)

        loop(D // 256, one)

    def mlp_up(part):
        def one(i):
            at = pl.ds(mult((i // 4) * T, T), T)
            cols = pl.ds(mult((i % 4) * 256, 256), 256)
            x = dot(n["A2"][at, :], n["Wu"][:, cols]) + vecs[6:7, cols]
            phi = 0.5 + 0.5 * lax.erf(x * math.sqrt(0.5))
            pdf = jnp.exp(-0.5 * x * x) * (1.0 / math.sqrt(2.0 * math.pi))
            n["act"][at, cols] = (x * phi).astype(BF)
            n["gp"][at, cols] = (phi + x * pdf).astype(BF)

        loop(4 * part + 4, one, 4 * part)

    def down_grad(part):
        def one(i):
            at = pl.ds(mult(i * 256, 256), 256)
            n["Gd"][at, :] = dot00(n["act"][:, at], n["Gs"][...]).astype(BF)

        loop(H // 512 * (part + 1), one, H // 512 * part)

    def mlp_back(part):
        if part == 0:
            n["cs"][6:7, :] = jnp.zeros((1, D), F32)

        def one(i):
            at = pl.ds(mult((i // 4) * T, T), T)
            cols = pl.ds(mult((i % 4) * 256, 256), 256)
            da = dot11(n["Gs"][at, :], n["Wd"][cols, :])
            dl = (da * n["gp"][at, cols].astype(F32)).astype(BF)
            n["dl"][at, cols] = dl
            n["cs"][6:7, cols] += jnp.sum(dl.astype(F32), axis=0, keepdims=True)

        loop(4 * part + 4, one, 4 * part)

    def up_grad(part):
        def one(i):
            at = pl.ds(mult(i * 256, 256), 256)
            n["Gu"][at, :] = dot00(n["A2"][:, at], n["dl"][...]).astype(BF)

        loop(D // 512 * (part + 1), one, D // 512 * part)

    def out_part():
        def one(i):
            at = pl.ds(mult(i * T, T), T)
            n["Po"][at, :] = (dot(n["att_st"][at, :], n["Wp"][...]) + dot(n["act"][at, :], n["Wd"][...])).astype(BF)

        loop(N // T, one)

    def input_part():
        for row in (0, 1, 4, 5):
            n["cs"][row : row + 1, :] = jnp.zeros((1, D), F32)

        def one(i):
            at = pl.ds(mult(i * T, T), T)
            nn = n["nb"][at, :].astype(F32)
            e1 = dot11(n["dj"][at, :], n["Wi"][...])
            n["cs"][0:1, :] += jnp.sum(e1 * nn, axis=0, keepdims=True)
            n["cs"][1:2, :] += jnp.sum(e1, axis=0, keepdims=True)
            e2 = dot11(n["dl"][at, :], n["Wu"][...])
            n["cs"][4:5, :] += jnp.sum(e2 * nn, axis=0, keepdims=True)
            n["cs"][5:6, :] += jnp.sum(e2, axis=0, keepdims=True)
            n["Pc"][at, :] = (e1 * vec(0) + e2 * vec(2)).astype(BF)

        loop(N // T, one)

    def own_g_sum():
        n["cs"][7:8, :] = jnp.zeros((1, D), F32)
        g = tile(n["Gs"], c * T, T).astype(F32)
        n["cs"][3:4, :] = jnp.sum(g, axis=0, keepdims=True)

    def finish_out():
        base = c * T
        x = tile(n["Xs"], base, T).astype(F32)
        total = tile(n["Po"], base, T).astype(F32) + n["r1"][0, 0:T].astype(F32) + n["r2"][0].astype(F32)
        n["xo"][...] = (x + total + vec(4) + vec(5)).astype(BF)

    def finish_input():
        base = c * T
        x = tile(n["Xs"], base, T).astype(F32)
        center = x - jnp.mean(x, axis=-1, keepdims=True)
        rstd = lax.rsqrt(jnp.mean(center * center, axis=-1, keepdims=True) + EPS)
        nn = center * rstd
        cc = tile(n["Pc"], base, T).astype(F32) + n["r1"][1, 0:T].astype(F32) + n["r2"][1].astype(F32)
        mean_c = jnp.mean(cc, axis=-1, keepdims=True)
        mean_cn = jnp.mean(cc * nn, axis=-1, keepdims=True)
        n["xg"][...] = tile(n["Gs"], base, T).astype(F32) + (cc - mean_c - nn * mean_cn) * rstd

    def unpack_vectors():
        for j in range(s.F):
            cols = slice(j * 128, (j + 1) * 128)
            n["vecs"][0:6, cols] = n["Wv"][j * VROWS : j * VROWS + 6, :]
            n["vecs"][6:7, cols] = n["Wv"][pl.ds(j * VROWS + 6 + c, 1), :]
        per = G // 128
        for j in range(3):
            for p in range(per):
                b = j * (D // 128) + c * per + p
                lo = (j * per + p) * 128
                n["vecs"][7:8, lo : lo + 128] = n["Wv"][pl.ds((b // 3) * VROWS + 6 + s.nctx + b % 3, 1), :]

    def pack_sums():
        n["Gv"][...] = jnp.zeros((s.F * VROWS, 128), F32)
        cs = n["cs"]
        for j in range(s.F):
            cols = slice(j * 128, (j + 1) * 128)
            base = j * VROWS
            for row, place in ((0, 0), (1, 1), (3, 5), (4, 6), (5, 7)):
                n["Gv"][base + place : base + place + 1, :] = cs[row : row + 1, cols]
            n["Gv"][pl.ds(base + 8 + c, 1), :] = cs[6:7, cols]
        per = G // 128
        for j in range(3):
            for p in range(per):
                b = j * (D // 128) + c * per + p
                lo = (j * per + p) * 128
                n["Gv"][pl.ds((b // 3) * VROWS + 2 + b % 3, 1), :] = cs[2:3, lo : lo + 128]

    def local(i, src, dst):
        return pltpu.make_async_copy(src, dst, n["loc"].at[i])

    own_i = rows(n["Wi"], (zi * B + yi) * R, R)
    own_u = wunit(W[UP], UP, zi, yi)
    hc = s.hc
    lc = {
        "x": [local(0, n["x"], rows(n["Xs"], c * T, T))],
        "i": [
            pltpu.make_async_copy(
                n["w_i"].at[:, pl.ds(mult(j * D + c * G, 128), G)], own_i.at[:, pl.ds(j * G, G)], n["loc_i"].at[j]
            )
            for j in range(3)
        ],
        "p": [local(3, n["w_p"], wunit(W[PROJ], PROJ, zi, yi))],
        "g": [local(4, n["g"], rows(n["Gs"], c * T, T))],
        "u": [local(5, n["w_u"], own_u)]
        if not s.packed
        else [
            pltpu.make_async_copy(
                n["w_u"].at[:, pl.ds(mult((j * s.nctx + c) * hc, 128), hc)],
                own_u.at[:, pl.ds(j * hc, hc)],
                n["loc_u"].at[j],
            )
            for j in range(s.F)
        ],
        "d": [local(6, rows(n["w_d"], c * hc, hc), rows(n["Wd"], (zi * B + yi) * hc, hc))],
    }
    if s.packed:
        lc["v"] = [local(2, n["vpack"], wunit(W[VEC], VEC, zi, yi))]

    def lstart(key):
        if key == "p":
            when(zi == c, lambda: each(lc[key], "start"))
        else:
            each(lc[key], "start")

    def lwait(key):
        if key == "p":
            when(zi == c, lambda: each(lc[key], "wait"))
        else:
            each(lc[key], "wait")

    for key in lc:
        lstart(key)
    bar = pltpu.get_barrier_semaphore()
    for dev in (sib, xn):
        pl.semaphore_signal(bar, inc=1, device_id=dev, device_id_type=MESH)
    for step in range(1, A):
        pl.semaphore_signal(bar, inc=1, device_id=(c, (zi + step) % A * B + yi), device_id_type=MESH)
    for d in (2, 3):
        when(
            edge[d],
            lambda d=d: pl.semaphore_signal(bar, inc=1, device_id=hop[d], device_id_type=MESH),
        )
    count = 2 + A - 1 + sum(jnp.where(e, 1, 0) for e in edge[2:])
    pl.semaphore_wait(bar, count)

    for key in lc:
        if key != "p":
            lwait(key)
    lwait("p")

    def blocks_start():
        for j in range(T // BLK):
            first = n["places"][0:1, j * BLK : j * BLK + 1] // BLK
            n["Bs"][pl.ds(c * 8 + j, 1), :] = jnp.broadcast_to(first, (1, D))
        xa_start(2)

    def vectors_start():
        if s.packed:
            va_start()

    def vectors_z():
        if s.packed:
            va_z()

    def vectors_y():
        if s.packed:
            ag_y(VEC)
            unpack_vectors()

    def sums_start():
        if s.packed:
            pack_sums()
            vs_start()

    def sums_y():
        if s.packed:
            vs_sum()
            ry_send(VEC, 0, zi)

    def sums_end():
        if s.packed:
            ry_vec()
            fa_start(VEC)

    def sums_fwd():
        if s.packed:
            fa_fwd(VEC)

    def cross_pair():
        rz_pair(CROSS, 0)
        rz_pair(CROSS, 1)

    def cross_y():
        rz_sum(CROSS)
        ry_send(CROSS, 0, zi)

    def cross_end():
        ry_cross()
        fa_start(CROSS)

    def done(kind):
        rz_sum(kind)
        fa_start(kind)

    put_out = local(12, n["xo"], n["out"])
    put_in = local(13, n["xg"], n["input_grad"])

    def store_out():
        cr_wait(0)
        finish_out()
        put_out.start()

    def store_input():
        cr_wait(1)
        finish_input()
        put_in.start()

    vectors_start()
    xa_start(0)
    zero_dkv()
    ag_start(IN)
    xa_wait(0, sib_c)
    vectors_z()
    ag_start(PROJ)
    ag_z(IN, 0)
    xa_start(1)
    ag_start(CROSS)
    ag_z(PROJ, 0)
    xa_fwd(0)
    ag_z(IN, 1)
    ag_start(UP)
    ag_z(IN, 2)
    vectors_y()
    blocks_start()
    ag_z(PROJ, 1)
    xa_wait(1, sib_c)
    norms(xn_c)
    xa_fwd(1)
    xa_fwd(2)
    xa_wait(2, sib_c)
    norms(sib_c)
    xa_wait(1, xs_c)
    norms(c)
    xa_wait(0, xs_c)
    ag_y(CROSS)
    ag_z(PROJ, 2)
    ag_z(UP, 0)
    norms(xs_c)
    xa_wait(2, xs_c)
    tables()
    ag_y(IN)
    qkv()
    ag_y(PROJ)
    dattended()
    order()
    ag_z(UP, 1)
    ag_z(CROSS, 0)
    attention(0, 0)
    attention(0, 1)
    ag_start(DOWN)
    attention(0, 2)
    attention(0, 3)
    attention(1, 0)
    ag_z(UP, 2)
    attention(1, 1)
    attention(1, 2)
    attention(1, 3)
    ag_z(DOWN, 0)
    joined_back()
    ag_y(UP)
    mlp_up(0)
    ag_z(DOWN, 1)
    proj_grad()
    own_g_sum()
    ag_z(DOWN, 2)
    ry_start(PROJ)
    ag_z(CROSS, 1)
    mlp_up(1)
    mlp_up(2)
    mlp_up(3)
    down_grad(0)
    down_grad(1)
    ag_z(CROSS, 2)
    ag_y(DOWN)
    cross_pair()
    ry_start(DOWN)
    mlp_back(0)
    out_part()
    mlp_back(1)
    ry_proj()
    mlp_back(2)
    ry_unit(DOWN, 0)
    mlp_back(3)
    up_grad(0)
    up_grad(1)
    cr_start(0)
    ry_start(UP)
    rz_far(CROSS)
    rz_far(PROJ)
    ry_unit(DOWN, 1)
    cr_mid(0)
    in_grad()
    input_part()
    cross_y()
    ry_unit(DOWN, 2)
    sums_start()
    ry_start(IN)
    rz_far(DOWN)
    done(PROJ)
    ry_unit(DOWN, 3)
    ry_unit(UP, 0)
    cr_start(1)
    ry_unit(UP, 1)
    ry_unit(UP, 2)
    cr_mid(1)
    ry_unit(IN, 0)
    sums_y()
    rz_far(UP)
    cross_end()
    ry_unit(IN, 1)
    ry_unit(IN, 2)
    done(DOWN)
    ry_unit(UP, 3)
    fa_fwd(CROSS)
    ry_unit(IN, 3)
    rz_far(IN)
    sums_end()
    done(UP)
    done(IN)
    fa_fwd(DOWN)
    sums_fwd()
    store_input()
    store_out()
    fa_fwd(PROJ)
    fa_fwd(UP)
    fa_fwd(IN)
    for kind in s.kinds:
        fa_end(kind)
    if s.packed:
        n["vtot"][...] = sum(n["FV"][j * VROWS : (j + 1) * VROWS, :] for j in range(s.nctx))
    put_cs = local(14, n["vtot"] if s.packed else n["cs"], n["sums"])
    put_cs.start()
    for kind in s.kinds:
        ry_drain(kind)
        if kind == VEC:
            va_drain()
            vs_drain()
        else:
            ag_drain(kind)
            rz_drain(kind)
    for arr in range(3):
        xa_drain(arr)
    for arr in range(2):
        cr_drain(arr)
    put_out.wait()
    put_in.wait()
    put_cs.wait()


def finish_kernel(s, hidden, *refs):
    gi, gp, gu, gd, out, input_grad, sums = refs[:7]
    to = refs[7:]
    to[0][...] = out[...]
    to[1][...] = input_grad[...]
    for slot in range(s.nctx):
        for j in range(3):
            lo = j * s.D + slot * s.G
            to[2][:, lo : lo + s.G] = gi[slot, :, j * s.G : (j + 1) * s.G].astype(F32)
        for j in range(s.F):
            lo = (j * s.nctx + slot) * s.hc
            to[4][:, lo : lo + s.hc] = gu[slot, :, j * s.hc : (j + 1) * s.hc].astype(F32)
    to[3][...] = gp[...].astype(F32)
    to[5][...] = gd[...].astype(F32)
    singles = ((0, 6), (1, 7), (5, 8), (6, 9), (7, 10), (5, 11))
    for row, at in singles:
        to[at][...] = sums[row : row + 1, :]
    for first, count, at in ((2, 3, 12), (8, s.nctx, 13)):
        for j in range(count):
            to[at][:, j * 128 : (j + 1) * 128] = sums[first + j : first + j + 1, :]


def finish(s, hidden, arrays):
    steps = max(1, s.R // 32)

    def part(shape):
        if len(shape) == 3:
            return pl.BlockSpec((shape[0], shape[1] // steps, shape[2]), lambda i: (0, i, 0))
        return pl.BlockSpec((shape[0] // steps, shape[1]), lambda i: (i, 0))

    def whole(shape):
        return pl.BlockSpec(shape, lambda i: (0, 0))

    D = s.D
    shapes = [(s.T, D), (s.T, D), (s.R, 3 * D), (s.R, D), (s.R, hidden), (hidden // s.F, D)]
    types = [BF, F32, F32, F32, F32, F32]
    small = [(1, 128)] * 6 + [(1, 3 * s.R), (1, hidden // s.F)]
    return pl.pallas_call(
        lambda *refs: finish_kernel(s, hidden, *refs),
        grid=(steps,),
        out_shape=tuple(jax.ShapeDtypeStruct(sh, dt) for sh, dt in zip(shapes + small, types + [F32] * 8)),
        in_specs=[part(a.shape) for a in arrays[:-1]] + [whole(arrays[-1].shape)],
        out_specs=tuple([part(sh) for sh in shapes] + [whole(sh) for sh in small]),
        compiler_params=pltpu.CompilerParams(vmem_limit_bytes=63 << 20),
        name="finish",
    )(*arrays)


def rope_tables(length):
    half = ROT // 2
    freq = np.power(np.float32(10000.0), np.float32(-2.0) * np.arange(half, dtype=np.float32) / np.float32(ROT))
    angle = np.arange(length, dtype=np.float32)[:, None] * freq[None, :].astype(np.float32)
    cos = np.ones((length, 128), np.float32)
    sin = np.zeros((length, 128), np.float32)
    for base in range(0, 128, HEAD_DIM):
        cos[:, base : base + half] = np.cos(angle)
        cos[:, base + half : base + ROT] = np.cos(angle)
        sin[:, base : base + half] = -np.sin(angle)
        sin[:, base + half : base + ROT] = np.sin(angle)
    return cos, sin


def body(
    hidden_in,
    positions,
    out_grad,
    attn_gain,
    attn_shift,
    in_weight,
    in_bias,
    proj_weight,
    proj_bias,
    mlp_gain,
    mlp_shift,
    up_weight,
    up_bias,
    down_weight,
    down_bias,
):
    nctx, nshard = lax.axis_size("ctx"), lax.axis_size("fsdp")
    T, D = hidden_in.shape[1:]
    hidden = up_weight.shape[1]
    s = Sizes(T, D, hidden, nctx, nshard)
    R, G, F = s.R, s.G, s.F
    hc = s.hc
    c, f = lax.axis_index("ctx"), lax.axis_index("fsdp")

    def pick_ctx(array, axis):
        return lax.dynamic_index_in_dim(array, c, axis, keepdims=False)

    small = [attn_gain, attn_shift, mlp_gain, mlp_shift, proj_bias, down_bias, up_bias, in_bias]
    if s.packed:
        w_u = up_weight
        flat, at = 0.0, 0
        for v in small:
            flat = flat + jnp.pad(v.astype(F32), (at, VROWS * 128 - at - v.shape[0]))
            at += v.shape[0]
        extra = dict(vpack=flat.reshape(VROWS, 128))
    else:
        w_u = pick_ctx(up_weight.reshape(R, F, nctx, hc), 2).reshape(R, s.H)
        lengths = [v.shape[0] for v in small]
        gathered = lax.all_gather(jnp.concatenate(small).astype(F32), "fsdp", axis=0)
        full, at = [], 0
        for length in lengths:
            full.append(gathered[:, at : at + length].reshape(-1))
            at += length
        full[6] = pick_ctx(full[6].reshape(F, nctx, hc), 1).reshape(-1)
        full[7] = jnp.pad(pick_ctx(full[7].reshape(3, nctx, G), 1).reshape(-1), (0, D - 3 * G))
        extra = dict(vecs=jnp.stack(full))
    cos, sin = rope_tables(s.N)

    plan = scratch_plan(s)
    any_ = pl.BlockSpec(memory_space=pl.ANY)
    vmem = pl.BlockSpec(memory_space=pltpu.VMEM)
    ins = dict(
        x=hidden_in[0],
        g=out_grad[0],
        places=positions,
        w_i=in_weight,
        w_p=proj_weight,
        w_u=w_u,
        w_d=down_weight,
        **extra,
        cos=jnp.asarray(cos),
        sin=jnp.asarray(sin),
    )
    in_vmem = {"vecs", "cos", "sin", "places"}
    outs = dict(
        out=jax.ShapeDtypeStruct((T, D), BF),
        input_grad=jax.ShapeDtypeStruct((T, D), F32),
        out_i=jax.ShapeDtypeStruct((nctx, R, 3 * G), BF),
        out_p=jax.ShapeDtypeStruct((R, D), BF),
        out_u=jax.ShapeDtypeStruct((nctx, R, s.H), BF),
        out_d=jax.ShapeDtypeStruct((nctx * hc, D), BF),
        sums=jax.ShapeDtypeStruct((VROWS, 128) if s.packed else (8, D), F32),
    )
    names = list(ins) + list(outs) + list(plan)
    out, input_grad, gi, gp, gu, gd, sums = pl.pallas_call(
        lambda *refs: kernel_body(s, names, *refs),
        out_shape=tuple(outs.values()),
        in_specs=[vmem if name in in_vmem else any_ for name in ins],
        out_specs=tuple(any_ for _ in outs),
        scratch_shapes=list(plan.values()),
        compiler_params=pltpu.CompilerParams(
            collective_id=0, has_side_effects=True, vmem_limit_bytes=63 << 20
        ),
        name="block",
    )(*ins.values())

    def own(full_vector):
        length = full_vector.shape[0] // F
        return lax.dynamic_slice_in_dim(full_vector, f * length, length)

    if s.packed:
        done = finish(s, hidden, (gi, gp, gu, gd, out, input_grad, sums))
        out, input_grad, in_total, proj_total, up_total, down_total = done[:6]
        gain1, shift1, g_sum, gain2, shift2, g_again, in_bias_sum, up_bias_sum = (v.reshape(-1) for v in done[6:])
    else:
        here = (jnp.arange(nctx) == c).astype(F32)
        in_b = (sums[2, : 3 * G].reshape(3, 1, G) * here[None, :, None]).reshape(-1)
        up_b = (sums[6].reshape(F, 1, hc) * here[None, :, None]).reshape(-1)
        total = lax.psum(
            jnp.concatenate([sums[0], sums[1], in_b, sums[3], sums[4], sums[5], up_b]), ("ctx", "fsdp")
        )
        parts, at = [], 0
        for length in (D, D, 3 * D, D, D, D, hidden):
            parts.append(own(total[at : at + length]))
            at += length
        gain1, shift1, in_bias_sum, g_sum, gain2, shift2, up_bias_sum = parts
        g_again = g_sum
        in_total = gi.astype(F32).reshape(nctx, R, 3, G).transpose(1, 2, 0, 3).reshape(R, 3 * D)
        proj_total, down_total = gp.astype(F32), gd.astype(F32)
        up_total = gu.astype(F32).reshape(nctx, R, F, hc).transpose(1, 2, 0, 3).reshape(R, hidden)
    return (
        out[None],
        input_grad[None],
        gain1,
        shift1,
        in_total,
        in_bias_sum,
        proj_total,
        g_sum,
        gain2,
        shift2,
        up_total,
        up_bias_sum,
        down_total,
        g_again,
    )


def solution(mesh):
    tok, vec, mat = P("fsdp", "ctx", None), P("fsdp"), P("fsdp", None)
    placed = (tok, P("fsdp", "ctx"), tok, vec, vec, mat, vec, mat, vec, vec, vec, mat, vec, mat, vec)
    return jax.shard_map(
        body,
        mesh=mesh,
        in_specs=placed,
        out_specs=(tok, tok, vec, vec, mat, vec, mat, vec, vec, vec, mat, vec, mat, vec),
        check_vma=False,
    )
```

```python
import math

import jax
import jax.numpy as jnp
import numpy as np
from jax import lax
from jax.experimental import pallas as pl
from jax.experimental.pallas import tpu as pltpu
from jax.sharding import PartitionSpec as P

HEADS = 16
HEAD_DIM = 64
ROT = 16
BLK = 128
EPS = 1e-05
MESH = pl.DeviceIdType.MESH
BF = jnp.bfloat16
F32 = jnp.float32
IN, PROJ, UP, DOWN, VEC, CROSS, PIECE = range(7)
PIECES = 2
NAMES = "ipudvefgh"
VROWS = 16
BOTH1 = (((1,), (1,)), ((), ()))
BOTH0 = (((0,), (0,)), ((), ()))


def dot(a, b):
    return jnp.dot(a, b, preferred_element_type=F32)


def dot11(a, b):
    return lax.dot_general(a, b, BOTH1, preferred_element_type=F32)


def dot00(a, b):
    return lax.dot_general(a, b, BOTH0, preferred_element_type=F32)


def mult(value, of):
    return pl.multiple_of(value, of)


def both(*conds):
    out = conds[0]
    for cond in conds[1:]:
        out = jnp.logical_and(out, cond)
    return out


class Sizes:
    def __init__(self, tokens, width, hidden, nctx, nshard):
        self.T = tokens
        self.N = tokens * nctx
        self.D = width
        self.H = hidden // nctx
        self.G = width // nctx
        self.nctx = nctx
        self.F = nshard
        self.A = nctx
        self.B = nshard // nctx
        self.R = width // nshard
        self.hc = hidden // nshard // nctx
        self.vector_rows = (1, 1, 1, 1, 1, 1, nctx, 3)
        self.packed = self.R % 128 == 0 and self.hc % 128 == 0
        half = self.hc // 2
        pieces = min(PIECES, self.R // 16)
        part = self.R // pieces
        more = pieces - 1
        self.pieces = (IN,) + tuple(range(PIECE, PIECE + more))
        self.buffer = ("i", "p", "u", "d", "v", "d") + ("i",) * more
        self.stride = (self.R, self.R, self.R, self.hc, VROWS, self.hc) + (self.R,) * more
        self.offset = (0, 0, 0, 0, 0, self.hc - half) + tuple(part * (i + 1) for i in range(more))
        self.rows = (part, self.R, self.R, self.hc - half, VROWS, half) + (part,) * more
        self.gather_rows = (self.R,) + self.rows[1:]
        self.cols = (3 * self.G, width, self.H, width, 128, width) + (3 * self.G,) * more
        self.units = (self.F, self.B, self.F, self.F, self.F, self.F) + (self.F,) * more
        self.types = (BF, BF, BF, BF, F32, BF) + (BF,) * more
        self.gathered = (IN, PROJ, UP, DOWN, CROSS) + ((VEC,) if self.packed else ())
        self.kinds = self.gathered + self.pieces[1:]
        self.NY = 1 if self.B == 2 else self.B + 1


def scratch_plan(s):
    N, D, G, H = s.N, s.D, s.G, s.H
    vm = pltpu.VMEM
    dma = pltpu.SemaphoreType.DMA
    plan = dict(
        Xs=vm((N, D), BF),
        Gs=vm((N, D), BF),
        Bs=vm((s.nctx * 8, D), jnp.int32),
        cos_st=vm((N, 128), F32),
        sin_st=vm((N, 128), F32),
        nb=vm((N, D), BF),
        A1=vm((N, D), BF),
        A2=vm((N, D), BF),
        S=vm((N, 4 * G), BF),
        dq=vm((N, G), F32),
        dk=vm((N, G), F32),
        dv=vm((N, G), F32),
        att_st=vm((N, G), BF),
        dj=vm((N, 3 * G), BF),
        act=vm((N, H), BF),
        gp=vm((N, H), BF),
        dl=vm((N, H), BF),
        Po=vm((N, D), BF),
        Pc=vm((N, D), BF),
        r1=vm((2, 2 * s.T, D), BF),
        r2=vm((2, s.T, D), BF),
        cs=vm((8, D), F32),
        xo=vm((s.T, D), BF),
        xg=vm((s.T, D), F32),
    )
    if s.packed:
        plan["vecs"] = vm((8, D), F32)
        plan["FV"] = vm((s.nctx * VROWS, 128), F32)
        plan["vtot"] = vm((VROWS, 128), F32)
        for i, count in enumerate(s.vector_rows):
            plan[f"vin{i}"] = vm((count * 128,), BF)
        plan["loc_v"] = dma((len(s.vector_rows),))
    A, B, F = s.A, s.B, s.F
    for kind in s.kinds:
        name = NAMES[kind]
        r, cl = s.rows[kind], s.cols[kind]
        dt = s.types[kind]
        if kind < CROSS:
            size = (s.units[kind] * s.stride[kind], cl)
            plan["W" + name] = vm(size, dt)
            plan["G" + name] = vm(size, dt)
        cross, proj = kind == CROSS, kind == PROJ
        per = 1 if cross or proj else A
        cols = B if cross else 1
        plan["Y" + name] = vm((s.NY * per * r, cl), dt)
        plan["Z" + name] = vm((A * B * r if kind == VEC else 3 * cols * r, cl), dt)
        along_y = per if B == 2 else 2 * per * B
        if kind in s.gathered:
            plan["az" + name] = dma(((2 if proj else A + 1) * cols,))
            plan["ay" + name] = dma((along_y,))
            plan["ar" + name] = dma((s.units[kind],))
        plan["ys" + name] = dma((along_y,))
        plan["yr" + name] = dma((along_y,))
        plan["zs" + name] = dma((A if kind == VEC else 3 * cols,))
        plan["zr" + name] = dma((A if kind == VEC else 3 * cols,))
    plan.update(
        xa_s=dma((3, 3)),
        xa_r=dma((3, s.nctx)),
        cr_s=dma((2, 3)),
        cr_r=dma((2, 3)),
        fa_s=dma((len(s.rows), 3)),
        fa_r=dma((len(s.rows), 3)),
        fa_l=dma((len(s.rows),)),
        loc=dma((16,)),
        loc_i=dma((3,)),
        loc_u=dma((s.F if s.packed else 1,)),
    )
    return plan


def kernel_body(s, names, *refs):
    n = dict(zip(names, refs))
    T, N, D, G, H, A, B, R = s.T, s.N, s.D, s.G, s.H, s.A, s.B, s.R
    c = lax.axis_index("ctx")
    f = lax.axis_index("fsdp")
    zi, yi = f // B, f % B
    sib_c = c + 1 - 2 * (c % 2)
    xn_c = (c + s.nctx // 2) % s.nctx
    xs_c = (sib_c + s.nctx // 2) % s.nctx
    sib, xn = (sib_c, f), (xn_c, f)
    edge = (zi < A - 1, zi > 0, yi < B - 1, yi > 0)
    hop = ((c, f + B), (c, f - B), (c, f + 1), (c, f - 1))

    def when(cond, fn):
        pl.when(cond)(fn)

    def rcopy(src, dst, ssem, rsem, dev):
        return pltpu.make_async_remote_copy(
            src_ref=src, dst_ref=dst, send_sem=ssem, recv_sem=rsem, device_id=dev, device_id_type=MESH
        )

    def rows(ref, start, size):
        return ref.at[pl.ds(mult(start, size), size)]

    W = [n.get("W" + x) for x in s.buffer]

    def has(kind, oz):
        return (oz == c) if kind == PROJ else (oz == oz)

    def wunit(ref, kind, oz, oy, sizes=s.rows):
        at = oy if kind == PROJ else oz * B + oy
        return rows(ref, at * s.stride[kind] + s.offset[kind], sizes[kind])

    def along_y(kind, oz, oy, d):
        per = 1 if kind in (PROJ, CROSS) else A
        at = 0 if per == 1 else oz
        return at if B == 2 else (d * per + at) * B + oy

    def ag_copy(kind, oz, oy, d):
        u = wunit(W[kind], kind, oz, oy, s.gather_rows)
        name = NAMES[kind]
        if d >= 2:
            send = n["ay" + name].at[along_y(kind, oz, oy, d - 2)]
        elif kind == PROJ:
            send = n["az" + name].at[d]
        else:
            at = oz if d == 0 else jnp.where(oz == zi, A, oz)
            send = n["az" + name].at[at + (oy * (A + 1) if kind == CROSS else 0)]
        return rcopy(u, u, send, n["ar" + name].at[oy if kind == PROJ else oz * B + oy], hop[d])

    def va_copy(source, oz):
        u = wunit(W[VEC], VEC, source, yi)
        return rcopy(
            u, u, n["azv"].at[oz], n["arv"].at[source * B + yi], (c, oz * B + yi)
        )

    def va_start():
        for oz in range(A):
            when(zi != oz, lambda oz=oz: va_copy(zi, oz).start())
        for d in (2, 3):
            when(edge[d], lambda d=d: ag_copy(VEC, zi, yi, d).start())

    def va_z():
        for i in range(1, A):
            oz = (zi + i) % A
            va_copy(oz, zi).wait_recv()
            for d in (2, 3):
                when(edge[d], lambda d=d, oz=oz: ag_copy(VEC, oz, yi, d).start())

    def va_drain():
        for oz in range(A):
            when(zi != oz, lambda oz=oz: va_copy(zi, oz).wait_send())
        for oz in range(A):
            for oy in range(B):
                when(both(oy <= yi, edge[2]), lambda oz=oz, oy=oy: ag_copy(VEC, oz, oy, 2).wait_send())
                when(both(oy >= yi, edge[3]), lambda oz=oz, oy=oy: ag_copy(VEC, oz, oy, 3).wait_send())

    def ag_start(kind):
        for d in range(4):
            when(both(has(kind, zi), edge[d]), lambda d=d: ag_copy(kind, zi, yi, d).start())

    def ag_z(kind, t):
        for i in range(B if kind == CROSS else 1):
            oy = (yi + i) % B if i else yi
            for sign, d in ((-1, 0), (1, 1)):
                oz = zi + sign * (1 + t)

                def go(oz=oz, d=d, oy=oy):
                    ag_copy(kind, oz, oy, d).wait_recv()
                    for dd in (d,) if kind == CROSS else (d, 2, 3):
                        when(edge[dd], lambda dd=dd: ag_copy(kind, oz, oy, dd).start())

                when(both(oz >= 0, oz < A, has(kind, oz)), go)

    def ag_y(kind):
        for t in range(B - 1):
            for zz in {PROJ: [c], CROSS: [zi]}.get(kind, list(range(A))):
                for sign, d in ((-1, 2), (1, 3)):
                    oy = yi + sign * (1 + t)

                    def go(oy=oy, d=d, zz=zz):
                        ag_copy(kind, zz, oy, d).wait_recv()
                        onward = ([d] if B > 2 else []) + ([0, 1] if kind == CROSS else [])
                        for dd in onward:
                            when(edge[dd], lambda dd=dd: ag_copy(kind, zz, oy, dd).start())

                    when(both(oy >= 0, oy < B), go)

    def ag_drain(kind):
        for oz in [c] if kind == PROJ else list(range(A)):
            for oy in range(B) if kind == CROSS else [yi]:
                when(both(oz <= zi, edge[0]), lambda oz=oz, oy=oy: ag_copy(kind, oz, oy, 0).wait_send())
                when(both(oz >= zi, edge[1]), lambda oz=oz, oy=oy: ag_copy(kind, oz, oy, 1).wait_send())
        for oz in {PROJ: [c], CROSS: [zi]}.get(kind, list(range(A))):
            for oy in range(B):
                when(both(oy <= yi, edge[2]), lambda oz=oz, oy=oy: ag_copy(kind, oz, oy, 2).wait_send())
                when(both(oy >= yi, edge[3]), lambda oz=oz, oy=oy: ag_copy(kind, oz, oy, 3).wait_send())

    XA = ((n["Xs"], T), (n["Gs"], T), (n["Bs"], 8))

    def xa_copy(arr, slot, which):
        ref, r = XA[arr]
        u = rows(ref, slot * r, r)
        return rcopy(u, u, n["xa_s"].at[arr, which], n["xa_r"].at[arr, slot], (xn, sib)[which != 0])

    def xa_start(arr):
        xa_copy(arr, c, 0).start()
        xa_copy(arr, c, 1).start()

    def xa_wait(arr, slot):
        xa_copy(arr, slot, 0).wait_recv()

    def xa_fwd(arr):
        xa_wait(arr, xn_c)
        xa_copy(arr, xn_c, 2).start()

    def xa_drain(arr):
        xa_copy(arr, c, 0).wait_send()
        xa_copy(arr, c, 1).wait_send()
        xa_copy(arr, xn_c, 2).wait_send()

    GR = [n.get("G" + x) for x in s.buffer]
    YB = [n.get("Y" + x) for x in NAMES]
    ZB = [n.get("Z" + x) for x in NAMES]

    def add_into(dst, src):
        dst[...] = (dst[...].astype(F32) + src[...].astype(F32)).astype(dst.dtype)

    def ry_slot(kind, zz, target, d, receiver):
        r = s.rows[kind]
        per = 1 if kind in (PROJ, CROSS) else A
        at = 0 if per == 1 else zz
        if B == 2:
            slot = 0
        elif d == 0:
            slot = target
        else:
            slot = jnp.where(receiver == target, B, target)
        return rows(YB[kind], (slot * per + at) * r, r)

    def ry_copy(kind, zz, target, d, receiver):
        at = along_y(kind, zz, target, d)
        return rcopy(
            wunit(GR[kind], kind, zz, target),
            ry_slot(kind, zz, target, d, receiver),
            n["ys" + NAMES[kind]].at[at],
            n["yr" + NAMES[kind]].at[at],
            hop[2 + d],
        )

    pair_z = zi + 1 - 2 * (zi % 2)
    far_z = (zi + A // 2) % A
    diag_z = (pair_z + A // 2) % A
    by_step = [diag_z, pair_z, far_z, zi]

    def ry_zz(kind):
        return {PROJ: [c], CROSS: [zi], VEC: [zi]}.get(kind, by_step)

    def ry_send(kind, t, zz):
        hi, lo = B - 1 - t, t
        when(yi == 0, lambda: ry_copy(kind, zz, hi, 0, yi + 1).start())
        when(yi == B - 1, lambda: ry_copy(kind, zz, lo, 1, yi - 1).start())

    def ry_recv(kind, t, zz):
        hi, lo = B - 1 - t, t
        for target, d, cond, onward in (
            (hi, 0, both(yi > 0, yi <= hi), both(yi > 0, yi < hi)),
            (lo, 1, both(yi < B - 1, yi >= lo), both(yi < B - 1, yi > lo)),
        ):

            def go(target=target, d=d):
                ry_copy(kind, zz, target, d, yi).wait_recv()
                add_into(wunit(GR[kind], kind, zz, target), ry_slot(kind, zz, target, d, yi))

            when(cond, go)
            if B > 2:
                when(
                    onward,
                    lambda target=target, d=d: ry_copy(
                        kind, zz, target, d, yi + 1 - 2 * d
                    ).start(),
                )

    def ry_drain(kind):
        for zz in {PROJ: [c], CROSS: [zi], VEC: [zi]}.get(kind, list(range(A))):
            for target in range(B):
                when(yi < target, lambda zz=zz, target=target: ry_copy(kind, zz, target, 0, yi + 1).wait_send())
                when(yi > target, lambda zz=zz, target=target: ry_copy(kind, zz, target, 1, yi - 1).wait_send())

    def rz_cols(kind):
        return [(yi + i) % B for i in range(B)] if kind == CROSS else [yi]

    def rz_slot(kind, which, col):
        r = s.rows[kind]
        return rows(ZB[kind], (which * B + col if kind == CROSS else which) * r, r)

    def rz_copy(kind, which, col):
        at = which * B + col if kind == CROSS else which
        return rcopy(
            wunit(GR[kind], kind, by_step[which], col),
            rz_slot(kind, which, col),
            n["zs" + NAMES[kind]].at[at],
            n["zr" + NAMES[kind]].at[at],
            (c, (pair_z, pair_z, far_z)[which] * B + yi),
        )

    def rz_take(kind, which, target, col):
        rz_copy(kind, which, col).wait_recv()
        add_into(wunit(GR[kind], kind, target, col), rz_slot(kind, which, col))

    def rz_pair(kind, which):
        def go():
            for col in rz_cols(kind):
                rz_copy(kind, which, col).start()

        when(has(kind, by_step[which]), go)

    def rz_far(kind):
        def go():
            for col in rz_cols(kind):
                rz_take(kind, 0, far_z, col)
                rz_copy(kind, 2, col).start()

        when(has(kind, far_z), go)

    def rz_sum(kind):
        def go():
            for col in rz_cols(kind):
                rz_take(kind, 1, zi, col)
                rz_take(kind, 2, zi, col)

        when(has(kind, zi), go)

    def rz_drain(kind):
        for which in range(3):

            def go(which=which):
                for col in rz_cols(kind):
                    rz_copy(kind, which, col).wait_send()

            when(has(kind, by_step[which]), go)

    def ry_first(kind):
        for t in range(B - 2):
            for zz in ry_zz(kind):
                if t:
                    ry_send(kind, t, zz)
                ry_recv(kind, t, zz)
        if B > 2:
            for zz in ry_zz(kind):
                ry_send(kind, B - 2, zz)

    def ry_start(kind):
        if kind in s.kinds:
            for zz in ry_zz(kind):
                ry_send(kind, 0, zz)

    def if_kind(kind, fn, *args):
        if kind in s.kinds:
            fn(kind, *args)

    def ry_unit(kind, i):
        if i == 0:
            ry_first(kind)
        ry_recv(kind, B - 2, by_step[i])
        if i < 2:
            rz_pair(kind, i)

    def vs_copy(source, target):
        return rcopy(
            rows(GR[VEC], target * B * VROWS, B * VROWS),
            rows(ZB[VEC], source * B * VROWS, B * VROWS),
            n["zsv"].at[target],
            n["zrv"].at[source],
            (c, target * B + yi),
        )

    def vs_start():
        for i in range(1, A):
            vs_copy(zi, (zi + i) % A).start()

    def vs_sum():
        mine = rows(GR[VEC], zi * B * VROWS, B * VROWS)
        for i in range(1, A):
            source = (zi + i) % A
            vs_copy(source, zi).wait_recv()
            add_into(mine, rows(ZB[VEC], source * B * VROWS, B * VROWS))

    def vs_drain():
        for i in range(1, A):
            vs_copy(zi, (zi + i) % A).wait_send()

    def ry_vec():
        ry_first(VEC)
        ry_recv(VEC, B - 2, zi)

    def ry_cross():
        ry_first(CROSS)
        ry_recv(CROSS, B - 2, zi)

    def ry_proj():
        ry_first(PROJ)
        ry_recv(PROJ, B - 2, c)
        rz_pair(PROJ, 0)
        rz_pair(PROJ, 1)

    def fa_has(kind, slot):
        return (zi == slot) if kind == PROJ else (c == c)

    def fa_dst(kind, slot):
        if kind == VEC:
            return rows(n["FV"], slot * VROWS, VROWS)
        if kind == PROJ:
            return n["out_p"]
        out = n["out_" + s.buffer[kind]]
        if s.buffer[kind] == "d":
            return rows(out, slot * s.hc + s.offset[kind], s.rows[kind])
        return out.at[slot, pl.ds(s.offset[kind], s.rows[kind])]

    def fa_copy(kind, slot, which):
        src = wunit(GR[kind], kind, zi, yi) if which < 2 else fa_dst(kind, slot)
        return rcopy(
            src, fa_dst(kind, slot), n["fa_s"].at[kind, which], n["fa_r"].at[kind, which], (sib, xn, sib)[which]
        )

    def fa_local(kind):
        return pltpu.make_async_copy(wunit(GR[kind], kind, zi, yi), fa_dst(kind, c), n["fa_l"].at[kind])

    def each(copies, what):
        for copy in copies:
            getattr(copy, what)()

    def fa_start(kind):
        def go():
            fa_copy(kind, c, 1).start()
            fa_copy(kind, c, 0).start()
            fa_local(kind).start()

        when(fa_has(kind, c), go)

    def fa_fwd(kind):
        def go():
            fa_copy(kind, xn_c, 1).wait_recv()
            fa_copy(kind, xn_c, 2).start()

        when(fa_has(kind, xn_c), go)

    def fa_end(kind):
        when(fa_has(kind, sib_c), lambda: fa_copy(kind, sib_c, 0).wait_recv())
        when(fa_has(kind, xs_c), lambda: fa_copy(kind, xs_c, 2).wait_recv())

        def own():
            fa_copy(kind, c, 1).wait_send()
            fa_copy(kind, c, 0).wait_send()
            fa_local(kind).wait()

        when(fa_has(kind, c), own)
        when(fa_has(kind, xn_c), lambda: fa_copy(kind, xn_c, 2).wait_send())

    PC = (n["Po"], n["Pc"])

    def cr_copy(arr, which, slot):
        if which < 2:
            return rcopy(
                rows(PC[arr], slot * T, T),
                n["r1"].at[arr, pl.ds(which * T, T)],
                n["cr_s"].at[arr, which],
                n["cr_r"].at[arr, which],
                sib,
            )
        return rcopy(rows(PC[arr], slot * T, T), n["r2"].at[arr], n["cr_s"].at[arr, 2], n["cr_r"].at[arr, 2], xn)

    def cr_start(arr):
        cr_copy(arr, 1, xs_c).start()
        cr_copy(arr, 0, sib_c).start()

    def cr_mid(arr):
        cr_copy(arr, 1, xs_c).wait_recv()
        add_into(rows(PC[arr], xn_c * T, T), n["r1"].at[arr, pl.ds(T, T)])
        cr_copy(arr, 2, xn_c).start()

    def cr_wait(arr):
        cr_copy(arr, 0, sib_c).wait_recv()
        cr_copy(arr, 2, xn_c).wait_recv()

    def cr_drain(arr):
        cr_copy(arr, 1, xs_c).wait_send()
        cr_copy(arr, 0, sib_c).wait_send()
        cr_copy(arr, 2, xn_c).wait_send()

    vecs, cos, sin = n["vecs"], n["cos"], n["sin"]

    def vec(row, width=D):
        return vecs[row : row + 1, 0:width]

    def loop(count, fn, first=0):
        def step(i, carry):
            fn(i)
            return carry

        lax.fori_loop(first, count, step, 0)

    def tile(ref, start, size, cols=slice(None)):
        return ref[pl.ds(mult(start, size), size), cols]

    def here(j, k, width):
        at = 8 * (j // 2) + j % 2
        return jnp.where(n["Bs"][at : at + 1, 0:width] == k, 1.0, 0.0)

    def to_order(dst, src):
        def one(k):
            total = None
            for j in range(2 * s.nctx):
                w = here(j, k, src.shape[1]).astype(src.dtype)
                term = src[j * BLK : (j + 1) * BLK, :] * w
                total = term if total is None else total + term
            dst[pl.ds(mult(k * BLK, BLK), BLK), :] = total

        loop(2 * s.nctx, one)

    def from_order(src, put):
        for j in range(2 * s.nctx):
            total = None
            for k in range(2 * s.nctx):
                w = here(j, k, src.shape[1]).astype(src.dtype)
                term = src[k * BLK : (k + 1) * BLK, :] * w
                total = term if total is None else total + term
            put(slice(j * BLK, (j + 1) * BLK), total)

    def norms(slot):
        def one(i):
            at = pl.ds(mult(slot * T + i * BLK, BLK), BLK)
            x = n["Xs"][at, :].astype(F32)
            center = x - jnp.mean(x, axis=-1, keepdims=True)
            nn = center * lax.rsqrt(jnp.mean(center * center, axis=-1, keepdims=True) + EPS)
            n["nb"][at, :] = nn.astype(BF)
            n["A1"][at, :] = (nn * vec(0) + vec(1)).astype(BF)
            n["A2"][at, :] = (nn * vec(2) + vec(3)).astype(BF)

        loop(T // BLK, one)

    lane64 = lax.broadcasted_iota(jnp.int32, (T, 128), 1) % HEAD_DIM
    first_half = lane64 < ROT // 2

    def rope(u, cs_, sn_, sign):
        partner = jnp.where(first_half, pltpu.roll(u, 128 - ROT // 2, 1), pltpu.roll(u, ROT // 2, 1))
        return u * cs_ + (partner * sn_) * sign

    def tables():
        def put(name):
            def store(at, value):
                n[name][at, :] = value

            return store

        from_order(cos, put("cos_st"))
        from_order(sin, put("sin_st"))

    raw, S = n["Pc"], n["S"]

    def qkv():
        def one(i):
            at = pl.ds(mult(i * T, T), T)
            j = dot(n["A1"][at, :], n["Wi"][...]) + vec(7, 3 * G)
            cs_, sn_ = n["cos_st"][at, :], n["sin_st"][at, :]
            for p in range(G // 128):
                lo = 128 * p
                q = rope(j[:, lo : lo + 128], cs_, sn_, 1.0).astype(BF)
                raw[at, lo : lo + 128] = (q.astype(F32) * HEAD_DIM**-0.5).astype(BF)
                raw[at, G + lo : G + lo + 128] = rope(j[:, G + lo : G + lo + 128], cs_, sn_, 1.0).astype(BF)
            raw[at, 2 * G : 3 * G] = j[:, 2 * G : 3 * G].astype(BF)

        loop(N // T, one)

    def dattended():
        def one(i):
            at = pl.ds(mult(i * T, T), T)
            raw[at, 3 * G : 4 * G] = dot11(n["Gs"][at, :], n["Wp"][...]).astype(BF)

        loop(N // T, one)

    def order():
        to_order(S, raw)

    def zero_dkv():
        n["dk"][...] = jnp.zeros((N, G), F32)
        n["dv"][...] = jnp.zeros((N, G), F32)

    def attention(p, i):
        L = (i + 1) * T
        cols = slice(128 * p, 128 * p + 128)
        at = slice(i * T, i * T + T)
        part = [slice(j * G + 128 * p, j * G + 128 * p + 128) for j in range(4)]
        kb, vb = S[0:L, part[1]], S[0:L, part[2]]
        qb, db = S[at, part[0]], S[at, part[3]]
        lane = lax.broadcasted_iota(jnp.int32, (T, 128), 1)
        key_at = lax.broadcasted_iota(jnp.int32, (T, T), 0)
        query_at = lax.broadcasted_iota(jnp.int32, (T, T), 1)
        keep = key_at <= query_at
        outs, dqs, ps, ds_, qs, dbs = [], [], [], [], [], []
        for h in range(2):
            mine = (lane >= HEAD_DIM) if h else (lane < HEAD_DIM)
            qh = jnp.where(mine, qb, jnp.zeros_like(qb))
            dh = jnp.where(mine, db, jnp.zeros_like(db))
            sc = dot11(kb, qh)
            last = jnp.where(keep, sc[L - T :], -1e30)
            sc = last if i == 0 else jnp.concatenate([sc[: L - T], last], axis=0)
            e = jnp.exp(sc - jnp.max(sc, axis=0, keepdims=True))
            pr = e * (1.0 / jnp.sum(e, axis=0, keepdims=True))
            dp = dot11(vb, dh)
            delta = jnp.sum(pr * dp, axis=0, keepdims=True)
            dsl = (pr * (dp - delta)).astype(BF)
            pb = pr.astype(BF)
            outs.append(dot00(vb, pb))
            dqs.append(dot00(kb, dsl))
            n["dv"][0:L, cols] += dot(pb, dh)
            n["dk"][0:L, cols] += dot(dsl, qh)
        feature = lax.broadcasted_iota(jnp.int32, (128, T), 0)
        raw[at, part[3]] = jnp.where(feature < HEAD_DIM, outs[0], outs[1]).T.astype(BF)
        n["dq"][at, cols] = jnp.where(feature < HEAD_DIM, dqs[0], dqs[1]).T * HEAD_DIM**-0.5

    def joined_back():
        n["cs"][2:3, :] = jnp.zeros((1, D), F32)

        def one(i):
            at = pl.ds(mult(i * T, T), T)
            cs_, sn_ = cos[at, :], sin[at, :]
            for p in range(G // 128):
                cols = slice(128 * p, 128 * p + 128)
                for j, (name, turn) in enumerate((("dq", True), ("dk", True), ("dv", False))):
                    u = n[name][at, cols]
                    if turn:
                        u = rope(u, cs_, sn_, -1.0)
                    u = u.astype(BF)
                    lo = j * G + 128 * p
                    raw[at, lo : lo + 128] = u
                    n["cs"][2:3, lo : lo + 128] += jnp.sum(u.astype(F32), axis=0, keepdims=True)

        loop(N // T, one)

        def put(at, value):
            n["dj"][at, :] = value[:, 0 : 3 * G]
            n["att_st"][at, :] = value[:, 3 * G : 4 * G]

        from_order(raw, put)

    def in_grad():
        def one(i):
            at = pl.ds(mult(i * 256, 256), 256)
            n["Gi"][at, :] = dot00(n["A1"][:, at], n["dj"][...]).astype(BF)

        loop(D // 256, one)

    def proj_grad():
        def one(i):
            at = pl.ds(mult(i * 256, 256), 256)
            n["Gp"][:, at] = dot00(n["att_st"][...], n["Gs"][:, at]).astype(BF)

        loop(D // 256, one)

    def mlp_up(part):
        def one(i):
            at = pl.ds(mult((i // 4) * T, T), T)
            cols = pl.ds(mult((i % 4) * 256, 256), 256)
            x = dot(n["A2"][at, :], n["Wu"][:, cols]) + vecs[6:7, cols]
            phi = 0.5 + 0.5 * lax.erf(x * math.sqrt(0.5))
            pdf = jnp.exp(-0.5 * x * x) * (1.0 / math.sqrt(2.0 * math.pi))
            n["act"][at, cols] = (x * phi).astype(BF)
            n["gp"][at, cols] = (phi + x * pdf).astype(BF)

        loop(4 * part + 4, one, 4 * part)

    def down_grad(part):
        def one(i):
            at = pl.ds(mult(i * 256, 256), 256)
            n["Gd"][at, :] = dot00(n["act"][:, at], n["Gs"][...]).astype(BF)

        loop(H // 512 * (part + 1), one, H // 512 * part)

    def mlp_back(part):
        if part == 0:
            n["cs"][6:7, :] = jnp.zeros((1, D), F32)

        def one(i):
            at = pl.ds(mult((i // 4) * T, T), T)
            cols = pl.ds(mult((i % 4) * 256, 256), 256)
            da = dot11(n["Gs"][at, :], n["Wd"][cols, :])
            dl = (da * n["gp"][at, cols].astype(F32)).astype(BF)
            n["dl"][at, cols] = dl
            n["cs"][6:7, cols] += jnp.sum(dl.astype(F32), axis=0, keepdims=True)

        loop(4 * part + 4, one, 4 * part)

    def up_grad(part):
        def one(i):
            at = pl.ds(mult(i * 256, 256), 256)
            n["Gu"][at, :] = dot00(n["A2"][:, at], n["dl"][...]).astype(BF)

        loop(D // 512 * (part + 1), one, D // 512 * part)

    def out_part():
        def one(i):
            at = pl.ds(mult(i * T, T), T)
            n["Po"][at, :] = (dot(n["att_st"][at, :], n["Wp"][...]) + dot(n["act"][at, :], n["Wd"][...])).astype(BF)

        loop(N // T, one)

    def input_part():
        for row in (0, 1, 4, 5):
            n["cs"][row : row + 1, :] = jnp.zeros((1, D), F32)

        def one(i):
            at = pl.ds(mult(i * T, T), T)
            nn = n["nb"][at, :].astype(F32)
            e1 = dot11(n["dj"][at, :], n["Wi"][...])
            n["cs"][0:1, :] += jnp.sum(e1 * nn, axis=0, keepdims=True)
            n["cs"][1:2, :] += jnp.sum(e1, axis=0, keepdims=True)
            e2 = dot11(n["dl"][at, :], n["Wu"][...])
            n["cs"][4:5, :] += jnp.sum(e2 * nn, axis=0, keepdims=True)
            n["cs"][5:6, :] += jnp.sum(e2, axis=0, keepdims=True)
            n["Pc"][at, :] = (e1 * vec(0) + e2 * vec(2)).astype(BF)

        loop(N // T, one)

    def own_g_sum():
        n["cs"][7:8, :] = jnp.zeros((1, D), F32)
        g = tile(n["Gs"], c * T, T).astype(F32)
        n["cs"][3:4, :] = jnp.sum(g, axis=0, keepdims=True)

    def finish_out():
        base = c * T
        x = tile(n["Xs"], base, T).astype(F32)
        total = tile(n["Po"], base, T).astype(F32) + n["r1"][0, 0:T].astype(F32) + n["r2"][0].astype(F32)
        n["xo"][...] = (x + total + vec(4) + vec(5)).astype(BF)

    def finish_input():
        base = c * T
        x = tile(n["Xs"], base, T).astype(F32)
        center = x - jnp.mean(x, axis=-1, keepdims=True)
        rstd = lax.rsqrt(jnp.mean(center * center, axis=-1, keepdims=True) + EPS)
        nn = center * rstd
        cc = tile(n["Pc"], base, T).astype(F32) + n["r1"][1, 0:T].astype(F32) + n["r2"][1].astype(F32)
        mean_c = jnp.mean(cc, axis=-1, keepdims=True)
        mean_cn = jnp.mean(cc * nn, axis=-1, keepdims=True)
        n["xg"][...] = tile(n["Gs"], base, T).astype(F32) + (cc - mean_c - nn * mean_cn) * rstd

    def unpack_vectors():
        for j in range(s.F):
            cols = slice(j * 128, (j + 1) * 128)
            n["vecs"][0:6, cols] = n["Wv"][j * VROWS : j * VROWS + 6, :]
            n["vecs"][6:7, cols] = n["Wv"][pl.ds(j * VROWS + 6 + c, 1), :]
        per = G // 128
        for j in range(3):
            for p in range(per):
                b = j * (D // 128) + c * per + p
                lo = (j * per + p) * 128
                n["vecs"][7:8, lo : lo + 128] = n["Wv"][pl.ds((b // 3) * VROWS + 6 + s.nctx + b % 3, 1), :]

    def pack_sums():
        n["Gv"][...] = jnp.zeros((s.F * VROWS, 128), F32)
        cs = n["cs"]
        for j in range(s.F):
            cols = slice(j * 128, (j + 1) * 128)
            base = j * VROWS
            for row, place in ((0, 0), (1, 1), (3, 5), (4, 6), (5, 7)):
                n["Gv"][base + place : base + place + 1, :] = cs[row : row + 1, cols]
            n["Gv"][pl.ds(base + 8 + c, 1), :] = cs[6:7, cols]
        per = G // 128
        for j in range(3):
            for p in range(per):
                b = j * (D // 128) + c * per + p
                lo = (j * per + p) * 128
                n["Gv"][pl.ds((b // 3) * VROWS + 2 + b % 3, 1), :] = cs[2:3, lo : lo + 128]

    def local(i, src, dst):
        return pltpu.make_async_copy(src, dst, n["loc"].at[i])

    own_i = rows(n["Wi"], (zi * B + yi) * R, R)
    own_u = wunit(W[UP], UP, zi, yi)
    hc = s.hc
    lc = {
        "x": [local(0, n["x"], rows(n["Xs"], c * T, T))],
        "i": [
            pltpu.make_async_copy(
                n["w_i"].at[:, pl.ds(mult(j * D + c * G, 128), G)], own_i.at[:, pl.ds(j * G, G)], n["loc_i"].at[j]
            )
            for j in range(3)
        ],
        "p": [local(3, n["w_p"], wunit(W[PROJ], PROJ, zi, yi))],
        "g": [local(4, n["g"], rows(n["Gs"], c * T, T))],
        "u": [local(5, n["w_u"], own_u)]
        if not s.packed
        else [
            pltpu.make_async_copy(
                n["w_u"].at[:, pl.ds(mult((j * s.nctx + c) * hc, 128), hc)],
                own_u.at[:, pl.ds(j * hc, hc)],
                n["loc_u"].at[j],
            )
            for j in range(s.F)
        ],
        "d": [local(6, rows(n["w_d"], c * hc, hc), rows(n["Wd"], (zi * B + yi) * hc, hc))],
    }
    if s.packed:
        lc["v"] = [
            pltpu.make_async_copy(n[f"vec{i}"], n[f"vin{i}"], n["loc_v"].at[i]) for i in range(len(s.vector_rows))
        ]

    def lstart(key):
        if key == "p":
            when(zi == c, lambda: each(lc[key], "start"))
        else:
            each(lc[key], "start")

    def lwait(key):
        if key == "p":
            when(zi == c, lambda: each(lc[key], "wait"))
        else:
            each(lc[key], "wait")

    for key in lc:
        lstart(key)
    bar = pltpu.get_barrier_semaphore()
    for dev in (sib, xn):
        pl.semaphore_signal(bar, inc=1, device_id=dev, device_id_type=MESH)
    for step in range(1, A):
        pl.semaphore_signal(bar, inc=1, device_id=(c, (zi + step) % A * B + yi), device_id_type=MESH)
    for d in (2, 3):
        when(
            edge[d],
            lambda d=d: pl.semaphore_signal(bar, inc=1, device_id=hop[d], device_id_type=MESH),
        )
    count = 2 + A - 1 + sum(jnp.where(e, 1, 0) for e in edge[2:])
    pl.semaphore_wait(bar, count)

    for key in lc:
        if key != "p":
            lwait(key)
    lwait("p")

    def blocks_start():
        for j in range(T // BLK):
            first = n["places"][0:1, j * BLK : j * BLK + 1] // BLK
            n["Bs"][pl.ds(c * 8 + j, 1), :] = jnp.broadcast_to(first, (1, D))
        xa_start(2)

    def vectors_start():
        if s.packed:
            at = (zi * B + yi) * VROWS
            for i, count in enumerate(s.vector_rows):
                for j in range(count):
                    n["Wv"][pl.ds(at, 1), :] = n[f"vin{i}"][j * 128 : (j + 1) * 128].astype(F32).reshape(1, 128)
                    at = at + 1
            va_start()

    def vectors_z():
        if s.packed:
            va_z()

    def vectors_y():
        if s.packed:
            ag_y(VEC)
            unpack_vectors()

    def sums_start():
        if s.packed:
            pack_sums()
            vs_start()

    def sums_y():
        if s.packed:
            vs_sum()
            ry_send(VEC, 0, zi)

    def sums_end():
        if s.packed:
            ry_vec()
            fa_start(VEC)

    def sums_fwd():
        if s.packed:
            fa_fwd(VEC)

    def cross_pair():
        rz_pair(CROSS, 0)
        rz_pair(CROSS, 1)

    def cross_y():
        rz_sum(CROSS)
        ry_send(CROSS, 0, zi)

    def cross_end():
        ry_cross()
        fa_start(CROSS)

    def done(kind):
        rz_sum(kind)
        fa_start(kind)

    put_out = local(12, n["xo"], n["out"])
    put_in = local(13, n["xg"], n["input_grad"])

    def store_out():
        cr_wait(0)
        finish_out()
        put_out.start()

    def store_input():
        cr_wait(1)
        finish_input()
        put_in.start()

    ag_start(IN)
    blocks_start()
    xa_start(0)
    own_g_sum()
    vectors_start()
    xa_wait(2, sib_c)
    xa_wait(0, sib_c)
    ag_start(PROJ)
    ag_z(IN, 0)
    zero_dkv()
    xa_start(1)
    vectors_z()
    xa_fwd(2)
    ag_z(PROJ, 0)
    xa_wait(2, xs_c)
    ag_z(IN, 1)
    xa_fwd(0)
    ag_start(UP)
    tables()
    ag_z(PROJ, 1)
    xa_wait(0, xs_c)
    xa_wait(1, sib_c)
    ag_z(IN, 2)
    ag_start(CROSS)
    vectors_y()
    norms(xs_c)
    norms(c)
    norms(sib_c)
    ag_z(PROJ, 2)
    ag_start(DOWN)
    xa_fwd(1)
    ag_z(UP, 0)
    norms(xn_c)
    xa_wait(1, xs_c)
    ag_y(IN)
    qkv()
    ag_y(PROJ)
    dattended()
    order()
    attention(0, 0)
    ag_z(UP, 1)
    ag_y(CROSS)
    attention(0, 1)
    ag_z(DOWN, 0)
    attention(0, 2)
    attention(0, 3)
    attention(1, 0)
    attention(1, 1)
    ag_z(UP, 2)
    attention(1, 2)
    attention(1, 3)
    ag_z(CROSS, 0)
    joined_back()
    ag_y(UP)
    mlp_up(0)
    ag_z(DOWN, 1)
    mlp_up(1)
    proj_grad()
    ag_z(CROSS, 1)
    ry_start(PROJ)
    mlp_up(2)
    ag_z(DOWN, 2)
    mlp_up(3)
    down_grad(0)
    down_grad(1)
    cross_pair()
    ag_z(CROSS, 2)
    in_grad()
    ag_y(DOWN)
    ry_start(DOWN)
    mlp_back(0)
    ry_proj()
    mlp_back(1)
    ry_start(PIECE)
    mlp_back(2)
    rz_far(CROSS)
    ry_unit(DOWN, 0)
    mlp_back(3)
    input_part()
    cr_start(1)
    if_kind(PIECE, ry_unit, 0)
    up_grad(0)
    if_kind(PIECE, ry_unit, 1)
    up_grad(1)
    ry_start(UP)
    rz_far(PROJ)
    cr_mid(1)
    ry_unit(DOWN, 1)
    sums_start()
    out_part()
    ry_unit(UP, 0)
    cr_start(0)
    ry_unit(DOWN, 2)
    done(PROJ)
    cross_y()
    rz_far(DOWN)
    cr_mid(0)
    ry_unit(UP, 1)
    ry_unit(UP, 2)
    rz_far(UP)
    ry_start(IN)
    ry_unit(DOWN, 3)
    sums_y()
    done(DOWN)
    if_kind(PIECE, ry_unit, 2)
    cross_end()
    ry_unit(UP, 3)
    ry_unit(IN, 0)
    if_kind(PIECE, rz_far)
    store_out()
    ry_unit(IN, 1)
    done(UP)
    ry_unit(IN, 2)
    rz_far(IN)
    sums_end()
    fa_fwd(PROJ)
    fa_fwd(DOWN)
    if_kind(PIECE, ry_unit, 3)
    fa_fwd(CROSS)
    if_kind(PIECE, done)
    ry_unit(IN, 3)
    done(IN)
    store_input()
    fa_fwd(UP)
    if_kind(PIECE, fa_fwd)
    fa_fwd(IN)
    sums_fwd()
    for kind in s.kinds:
        fa_end(kind)
    if s.packed:
        n["vtot"][...] = sum(n["FV"][j * VROWS : (j + 1) * VROWS, :] for j in range(s.nctx))
    put_cs = local(14, n["vtot"] if s.packed else n["cs"], n["sums"])
    put_cs.start()
    for kind in s.kinds:
        ry_drain(kind)
        if kind == VEC:
            va_drain()
            vs_drain()
        else:
            if kind in s.gathered:
                ag_drain(kind)
            rz_drain(kind)
    for arr in range(3):
        xa_drain(arr)
    for arr in range(2):
        cr_drain(arr)
    put_out.wait()
    put_in.wait()
    put_cs.wait()


def finish_kernel(s, hidden, *refs):
    gi, gp, gu, gd, out, input_grad, sums = refs[:7]
    to = refs[7:]
    to[0][...] = out[...]
    to[1][...] = input_grad[...]
    for slot in range(s.nctx):
        for j in range(3):
            lo = j * s.D + slot * s.G
            to[2][:, lo : lo + s.G] = gi[slot, :, j * s.G : (j + 1) * s.G].astype(F32)
        for j in range(s.F):
            lo = (j * s.nctx + slot) * s.hc
            to[4][:, lo : lo + s.hc] = gu[slot, :, j * s.hc : (j + 1) * s.hc].astype(F32)
    to[3][...] = gp[...].astype(F32)
    to[5][...] = gd[...].astype(F32)
    singles = ((0, 6), (1, 7), (5, 8), (6, 9), (7, 10), (5, 11))
    for row, at in singles:
        to[at][...] = sums[row, :]
    for first, count, at in ((2, 3, 12), (8, s.nctx, 13)):
        for j in range(count):
            to[at][j * 128 : (j + 1) * 128] = sums[first + j, :]


def finish(s, hidden, arrays):
    steps = max(1, s.R // 64)

    def part(shape):
        if len(shape) == 3:
            return pl.BlockSpec((shape[0], shape[1] // steps, shape[2]), lambda i: (0, i, 0))
        return pl.BlockSpec((shape[0] // steps, shape[1]), lambda i: (i, 0))

    def whole(shape):
        return pl.BlockSpec(shape, lambda i: (0,) * len(shape))

    D = s.D
    shapes = [(s.T, D), (s.T, D), (s.R, 3 * D), (s.R, D), (s.R, hidden), (hidden // s.F, D)]
    types = [BF, F32, F32, F32, F32, F32]
    small = [(128,)] * 6 + [(3 * s.R,), (hidden // s.F,)]
    return pl.pallas_call(
        lambda *refs: finish_kernel(s, hidden, *refs),
        grid=(steps,),
        out_shape=tuple(jax.ShapeDtypeStruct(sh, dt) for sh, dt in zip(shapes + small, types + [F32] * 8)),
        in_specs=[part(a.shape) for a in arrays[:-1]] + [whole(arrays[-1].shape)],
        out_specs=tuple([part(sh) for sh in shapes] + [whole(sh) for sh in small]),
        compiler_params=pltpu.CompilerParams(vmem_limit_bytes=63 << 20),
        name="finish",
    )(*arrays)


def rope_tables(length):
    half = ROT // 2
    freq = np.power(np.float32(10000.0), np.float32(-2.0) * np.arange(half, dtype=np.float32) / np.float32(ROT))
    angle = np.arange(length, dtype=np.float32)[:, None] * freq[None, :].astype(np.float32)
    cos = np.ones((length, 128), np.float32)
    sin = np.zeros((length, 128), np.float32)
    for base in range(0, 128, HEAD_DIM):
        cos[:, base : base + half] = np.cos(angle)
        cos[:, base + half : base + ROT] = np.cos(angle)
        sin[:, base : base + half] = -np.sin(angle)
        sin[:, base + half : base + ROT] = np.sin(angle)
    return cos, sin


def body(
    hidden_in,
    positions,
    out_grad,
    attn_gain,
    attn_shift,
    in_weight,
    in_bias,
    proj_weight,
    proj_bias,
    mlp_gain,
    mlp_shift,
    up_weight,
    up_bias,
    down_weight,
    down_bias,
):
    nctx, nshard = lax.axis_size("ctx"), lax.axis_size("fsdp")
    T, D = hidden_in.shape[1:]
    hidden = up_weight.shape[1]
    s = Sizes(T, D, hidden, nctx, nshard)
    R, G, F = s.R, s.G, s.F
    hc = s.hc
    c, f = lax.axis_index("ctx"), lax.axis_index("fsdp")

    def pick_ctx(array, axis):
        return lax.dynamic_index_in_dim(array, c, axis, keepdims=False)

    small = [attn_gain, attn_shift, mlp_gain, mlp_shift, proj_bias, down_bias, up_bias, in_bias]
    if s.packed:
        w_u = up_weight
        extra = {f"vec{i}": v for i, v in enumerate(small)}
    else:
        w_u = pick_ctx(up_weight.reshape(R, F, nctx, hc), 2).reshape(R, s.H)
        lengths = [v.shape[0] for v in small]
        gathered = lax.all_gather(jnp.concatenate(small).astype(F32), "fsdp", axis=0)
        full, at = [], 0
        for length in lengths:
            full.append(gathered[:, at : at + length].reshape(-1))
            at += length
        full[6] = pick_ctx(full[6].reshape(F, nctx, hc), 1).reshape(-1)
        full[7] = jnp.pad(pick_ctx(full[7].reshape(3, nctx, G), 1).reshape(-1), (0, D - 3 * G))
        extra = dict(vecs=jnp.stack(full))
    cos, sin = rope_tables(s.N)

    plan = scratch_plan(s)
    any_ = pl.BlockSpec(memory_space=pl.ANY)
    vmem = pl.BlockSpec(memory_space=pltpu.VMEM)
    ins = dict(
        x=hidden_in[0],
        g=out_grad[0],
        places=positions,
        w_i=in_weight,
        w_p=proj_weight,
        w_u=w_u,
        w_d=down_weight,
        **extra,
        cos=jnp.asarray(cos),
        sin=jnp.asarray(sin),
    )
    in_vmem = {"vecs", "cos", "sin", "places"}
    outs = dict(
        out=jax.ShapeDtypeStruct((T, D), BF),
        input_grad=jax.ShapeDtypeStruct((T, D), F32),
        out_i=jax.ShapeDtypeStruct((nctx, R, 3 * G), BF),
        out_p=jax.ShapeDtypeStruct((R, D), BF),
        out_u=jax.ShapeDtypeStruct((nctx, R, s.H), BF),
        out_d=jax.ShapeDtypeStruct((nctx * hc, D), BF),
        sums=jax.ShapeDtypeStruct((VROWS, 128) if s.packed else (8, D), F32),
    )
    names = list(ins) + list(outs) + list(plan)
    out, input_grad, gi, gp, gu, gd, sums = pl.pallas_call(
        lambda *refs: kernel_body(s, names, *refs),
        out_shape=tuple(outs.values()),
        in_specs=[vmem if name in in_vmem else any_ for name in ins],
        out_specs=tuple(any_ for _ in outs),
        scratch_shapes=list(plan.values()),
        compiler_params=pltpu.CompilerParams(
            collective_id=0, has_side_effects=True, vmem_limit_bytes=63 << 20
        ),
        name="block",
    )(*ins.values())

    def own(full_vector):
        length = full_vector.shape[0] // F
        return lax.dynamic_slice_in_dim(full_vector, f * length, length)

    if s.packed:
        done = finish(s, hidden, (gi, gp, gu, gd, out, input_grad, sums))
        out, input_grad, in_total, proj_total, up_total, down_total = done[:6]
        gain1, shift1, g_sum, gain2, shift2, g_again, in_bias_sum, up_bias_sum = done[6:]
    else:
        here = (jnp.arange(nctx) == c).astype(F32)
        in_b = (sums[2, : 3 * G].reshape(3, 1, G) * here[None, :, None]).reshape(-1)
        up_b = (sums[6].reshape(F, 1, hc) * here[None, :, None]).reshape(-1)
        total = lax.psum(
            jnp.concatenate([sums[0], sums[1], in_b, sums[3], sums[4], sums[5], up_b]), ("ctx", "fsdp")
        )
        parts, at = [], 0
        for length in (D, D, 3 * D, D, D, D, hidden):
            parts.append(own(total[at : at + length]))
            at += length
        gain1, shift1, in_bias_sum, g_sum, gain2, shift2, up_bias_sum = parts
        g_again = g_sum
        in_total = gi.astype(F32).reshape(nctx, R, 3, G).transpose(1, 2, 0, 3).reshape(R, 3 * D)
        proj_total, down_total = gp.astype(F32), gd.astype(F32)
        up_total = gu.astype(F32).reshape(nctx, R, F, hc).transpose(1, 2, 0, 3).reshape(R, hidden)
    return (
        out[None],
        input_grad[None],
        gain1,
        shift1,
        in_total,
        in_bias_sum,
        proj_total,
        g_sum,
        gain2,
        shift2,
        up_total,
        up_bias_sum,
        down_total,
        g_again,
    )


def solution(mesh):
    tok, vec, mat = P("fsdp", "ctx", None), P("fsdp"), P("fsdp", None)
    placed = (tok, P("fsdp", "ctx"), tok, vec, vec, mat, vec, mat, vec, vec, vec, mat, vec, mat, vec)
    return jax.shard_map(
        body,
        mesh=mesh,
        in_specs=placed,
        out_specs=(tok, tok, vec, vec, mat, vec, mat, vec, vec, vec, mat, vec, mat, vec),
        check_vma=False,
    )
```

```python
import math

import jax
import jax.numpy as jnp
import numpy as np
from jax import lax
from jax.experimental import pallas as pl
from jax.experimental.pallas import tpu as pltpu
from jax.sharding import PartitionSpec as P

HEADS = 16
HEAD_DIM = 64
ROT = 16
BLK = 128
EPS = 1e-05
MESH = pl.DeviceIdType.MESH
BF = jnp.bfloat16
F32 = jnp.float32
IN, PROJ, UP, DOWN, VEC, CROSS, PIECE = range(7)
PIECES = 2
NAMES = "ipudvefgh"
VROWS = 16
BOTH1 = (((1,), (1,)), ((), ()))
BOTH0 = (((0,), (0,)), ((), ()))


def dot(a, b):
    return jnp.dot(a, b, preferred_element_type=F32)


def dot11(a, b):
    return lax.dot_general(a, b, BOTH1, preferred_element_type=F32)


def dot00(a, b):
    return lax.dot_general(a, b, BOTH0, preferred_element_type=F32)


def mult(value, of):
    return pl.multiple_of(value, of)


def both(*conds):
    out = conds[0]
    for cond in conds[1:]:
        out = jnp.logical_and(out, cond)
    return out


class Sizes:
    def __init__(self, tokens, width, hidden, nctx, nshard):
        self.T = tokens
        self.N = tokens * nctx
        self.D = width
        self.H = hidden // nctx
        self.G = width // nctx
        self.nctx = nctx
        self.F = nshard
        self.A = nctx
        self.B = nshard // nctx
        self.R = width // nshard
        self.hc = hidden // nshard // nctx
        self.vector_rows = (1, 1, 1, 1, 1, 1, nctx, 3)
        self.packed = self.R % 128 == 0 and self.hc % 128 == 0
        half = self.hc // 2
        pieces = min(PIECES, self.R // 16)
        part = self.R // pieces
        more = pieces - 1
        self.pieces = (IN,) + tuple(range(PIECE, PIECE + more))
        self.buffer = ("i", "p", "u", "d", "v", "d") + ("i",) * more
        self.stride = (self.R, self.R, self.R, self.hc, VROWS, self.hc) + (self.R,) * more
        self.offset = (0, 0, 0, 0, 0, self.hc - half) + tuple(part * (i + 1) for i in range(more))
        self.rows = (part, self.R, self.R, self.hc - half, VROWS, half) + (part,) * more
        self.gather_rows = (self.R,) + self.rows[1:]
        self.cols = (3 * self.G, width, self.H, width, 128, width) + (3 * self.G,) * more
        self.units = (self.F, self.B, self.F, self.F, self.F, self.F) + (self.F,) * more
        self.types = (BF, BF, BF, BF, F32, BF) + (BF,) * more
        self.gathered = (IN, PROJ, UP, DOWN, CROSS) + ((VEC,) if self.packed else ())
        self.kinds = self.gathered + self.pieces[1:]
        self.NY = 1 if self.B == 2 else self.B + 1


def scratch_plan(s):
    N, D, G, H = s.N, s.D, s.G, s.H
    vm = pltpu.VMEM
    dma = pltpu.SemaphoreType.DMA
    plan = dict(
        Xs=vm((N, D), BF),
        Gs=vm((N, D), BF),
        Bs=vm((s.nctx * 8, D), jnp.int32),
        cos_st=vm((N, 128), F32),
        sin_st=vm((N, 128), F32),
        nb=vm((N, D), BF),
        A1=vm((N, D), BF),
        A2=vm((N, D), BF),
        S=vm((N, 4 * G), BF),
        dq=vm((N, G), F32),
        dk=vm((N, G), F32),
        dv=vm((N, G), F32),
        att_st=vm((N, G), BF),
        dj=vm((N, 3 * G), BF),
        act=vm((N, H), BF),
        gp=vm((N, H), BF),
        dl=vm((N, H), BF),
        Po=vm((N, D), BF),
        Pc=vm((N, D), BF),
        r1=vm((2, 2 * s.T, D), BF),
        r2=vm((2, s.T, D), BF),
        cs=vm((8, D), F32),
        xo=vm((s.T, D), BF),
        xg=vm((s.T, D), F32),
    )
    if s.packed:
        plan["vecs"] = vm((8, D), F32)
        plan["FV"] = vm((s.nctx * VROWS, 128), F32)
        plan["vtot"] = vm((VROWS, 128), F32)
        for i, count in enumerate(s.vector_rows):
            plan[f"vin{i}"] = vm((count * 128,), BF)
        plan["loc_v"] = dma((len(s.vector_rows),))
    A, B, F = s.A, s.B, s.F
    for kind in s.kinds:
        name = NAMES[kind]
        r, cl = s.rows[kind], s.cols[kind]
        dt = s.types[kind]
        if kind < CROSS:
            size = (s.units[kind] * s.stride[kind], cl)
            plan["W" + name] = vm(size, dt)
            plan["G" + name] = vm(size, dt)
        cross, proj = kind == CROSS, kind == PROJ
        per = 1 if cross or proj else A
        cols = B if cross else 1
        plan["Y" + name] = vm((s.NY * per * r, cl), dt)
        plan["Z" + name] = vm((A * B * r if kind == VEC else 3 * cols * r, cl), dt)
        along_y = per if B == 2 else 2 * per * B
        if kind in s.gathered:
            plan["az" + name] = dma(((2 if proj else A + 1) * cols,))
            plan["ay" + name] = dma((along_y,))
            plan["ar" + name] = dma((s.units[kind],))
        plan["ys" + name] = dma((along_y,))
        plan["yr" + name] = dma((along_y,))
        plan["zs" + name] = dma((A if kind == VEC else 3 * cols,))
        plan["zr" + name] = dma((A if kind == VEC else 3 * cols,))
    plan.update(
        xa_s=dma((3, 3)),
        xa_r=dma((3, s.nctx)),
        cr_s=dma((2, 3)),
        cr_r=dma((2, 3)),
        fa_s=dma((len(s.rows), 3)),
        fa_r=dma((len(s.rows), 3)),
        fa_l=dma((len(s.rows),)),
        loc=dma((16,)),
        loc_i=dma((3,)),
        loc_u=dma((s.F if s.packed else 1,)),
    )
    return plan


def kernel_body(s, names, *refs):
    n = dict(zip(names, refs))
    T, N, D, G, H, A, B, R = s.T, s.N, s.D, s.G, s.H, s.A, s.B, s.R
    c = lax.axis_index("ctx")
    f = lax.axis_index("fsdp")
    zi, yi = f // B, f % B
    sib_c = c + 1 - 2 * (c % 2)
    xn_c = (c + s.nctx // 2) % s.nctx
    xs_c = (sib_c + s.nctx // 2) % s.nctx
    sib, xn = (sib_c, f), (xn_c, f)
    edge = (zi < A - 1, zi > 0, yi < B - 1, yi > 0)
    hop = ((c, f + B), (c, f - B), (c, f + 1), (c, f - 1))

    def when(cond, fn):
        pl.when(cond)(fn)

    def rcopy(src, dst, ssem, rsem, dev):
        return pltpu.make_async_remote_copy(
            src_ref=src, dst_ref=dst, send_sem=ssem, recv_sem=rsem, device_id=dev, device_id_type=MESH
        )

    def rows(ref, start, size):
        return ref.at[pl.ds(mult(start, math.gcd(size, 64)), size)]

    W = [n.get("W" + x) for x in s.buffer]

    def has(kind, oz):
        return (oz == c) if kind == PROJ else (oz == oz)

    def wunit(ref, kind, oz, oy, sizes=s.rows):
        at = oy if kind == PROJ else oz * B + oy
        return rows(ref, at * s.stride[kind] + s.offset[kind], sizes[kind])

    def along_y(kind, oz, oy, d):
        per = 1 if kind in (PROJ, CROSS) else A
        at = 0 if per == 1 else oz
        return at if B == 2 else (d * per + at) * B + oy

    def ag_copy(kind, oz, oy, d):
        u = wunit(W[kind], kind, oz, oy, s.gather_rows)
        name = NAMES[kind]
        if d >= 2:
            send = n["ay" + name].at[along_y(kind, oz, oy, d - 2)]
        elif kind == PROJ:
            send = n["az" + name].at[d]
        else:
            at = oz if d == 0 else jnp.where(oz == zi, A, oz)
            send = n["az" + name].at[at + (oy * (A + 1) if kind == CROSS else 0)]
        return rcopy(u, u, send, n["ar" + name].at[oy if kind == PROJ else oz * B + oy], hop[d])

    def va_copy(source, oz):
        u = wunit(W[VEC], VEC, source, yi)
        return rcopy(
            u, u, n["azv"].at[oz], n["arv"].at[source * B + yi], (c, oz * B + yi)
        )

    def va_start():
        for oz in range(A):
            when(zi != oz, lambda oz=oz: va_copy(zi, oz).start())
        for d in (2, 3):
            when(edge[d], lambda d=d: ag_copy(VEC, zi, yi, d).start())

    def va_z():
        for i in range(1, A):
            oz = (zi + i) % A
            va_copy(oz, zi).wait_recv()
            for d in (2, 3):
                when(edge[d], lambda d=d, oz=oz: ag_copy(VEC, oz, yi, d).start())

    def va_drain():
        for oz in range(A):
            when(zi != oz, lambda oz=oz: va_copy(zi, oz).wait_send())
        for oz in range(A):
            for oy in range(B):
                when(both(oy <= yi, edge[2]), lambda oz=oz, oy=oy: ag_copy(VEC, oz, oy, 2).wait_send())
                when(both(oy >= yi, edge[3]), lambda oz=oz, oy=oy: ag_copy(VEC, oz, oy, 3).wait_send())

    def ag_start(kind):
        for d in range(4):
            when(both(has(kind, zi), edge[d]), lambda d=d: ag_copy(kind, zi, yi, d).start())

    def ag_z(kind, t):
        for i in range(B if kind == CROSS else 1):
            oy = (yi + i) % B if i else yi
            for sign, d in ((-1, 0), (1, 1)):
                oz = zi + sign * (1 + t)

                def go(oz=oz, d=d, oy=oy):
                    ag_copy(kind, oz, oy, d).wait_recv()
                    for dd in (d,) if kind == CROSS else (d, 2, 3):
                        when(edge[dd], lambda dd=dd: ag_copy(kind, oz, oy, dd).start())

                when(both(oz >= 0, oz < A, has(kind, oz)), go)

    def ag_y(kind):
        for t in range(B - 1):
            for zz in {PROJ: [c], CROSS: [zi]}.get(kind, list(range(A))):
                for sign, d in ((-1, 2), (1, 3)):
                    oy = yi + sign * (1 + t)

                    def go(oy=oy, d=d, zz=zz):
                        ag_copy(kind, zz, oy, d).wait_recv()
                        onward = ([d] if B > 2 else []) + ([0, 1] if kind == CROSS else [])
                        for dd in onward:
                            when(edge[dd], lambda dd=dd: ag_copy(kind, zz, oy, dd).start())

                    when(both(oy >= 0, oy < B), go)

    def ag_drain(kind):
        for oz in [c] if kind == PROJ else list(range(A)):
            for oy in range(B) if kind == CROSS else [yi]:
                when(both(oz <= zi, edge[0]), lambda oz=oz, oy=oy: ag_copy(kind, oz, oy, 0).wait_send())
                when(both(oz >= zi, edge[1]), lambda oz=oz, oy=oy: ag_copy(kind, oz, oy, 1).wait_send())
        for oz in {PROJ: [c], CROSS: [zi]}.get(kind, list(range(A))):
            for oy in range(B):
                when(both(oy <= yi, edge[2]), lambda oz=oz, oy=oy: ag_copy(kind, oz, oy, 2).wait_send())
                when(both(oy >= yi, edge[3]), lambda oz=oz, oy=oy: ag_copy(kind, oz, oy, 3).wait_send())

    XA = ((n["Xs"], T), (n["Gs"], T), (n["Bs"], 8))

    def xa_copy(arr, slot, which):
        ref, r = XA[arr]
        u = rows(ref, slot * r, r)
        return rcopy(u, u, n["xa_s"].at[arr, which], n["xa_r"].at[arr, slot], (xn, sib)[which != 0])

    def xa_start(arr):
        xa_copy(arr, c, 0).start()
        xa_copy(arr, c, 1).start()

    def xa_wait(arr, slot):
        xa_copy(arr, slot, 0).wait_recv()

    def xa_fwd(arr):
        xa_wait(arr, xn_c)
        xa_copy(arr, xn_c, 2).start()

    def xa_drain(arr):
        xa_copy(arr, c, 0).wait_send()
        xa_copy(arr, c, 1).wait_send()
        xa_copy(arr, xn_c, 2).wait_send()

    GR = [n.get("G" + x) for x in s.buffer]
    YB = [n.get("Y" + x) for x in NAMES]
    ZB = [n.get("Z" + x) for x in NAMES]

    def add_into(dst, src):
        dst[...] = (dst[...].astype(F32) + src[...].astype(F32)).astype(dst.dtype)

    def ry_slot(kind, zz, target, d, receiver):
        r = s.rows[kind]
        per = 1 if kind in (PROJ, CROSS) else A
        at = 0 if per == 1 else zz
        if B == 2:
            slot = 0
        elif d == 0:
            slot = target
        else:
            slot = jnp.where(receiver == target, B, target)
        return rows(YB[kind], (slot * per + at) * r, r)

    def ry_copy(kind, zz, target, d, receiver):
        at = along_y(kind, zz, target, d)
        return rcopy(
            wunit(GR[kind], kind, zz, target),
            ry_slot(kind, zz, target, d, receiver),
            n["ys" + NAMES[kind]].at[at],
            n["yr" + NAMES[kind]].at[at],
            hop[2 + d],
        )

    pair_z = zi + 1 - 2 * (zi % 2)
    far_z = (zi + A // 2) % A
    diag_z = (pair_z + A // 2) % A
    by_step = [diag_z, pair_z, far_z, zi]

    def ry_zz(kind):
        return {PROJ: [c], CROSS: [zi], VEC: [zi]}.get(kind, by_step)

    def ry_send(kind, t, zz):
        hi, lo = B - 1 - t, t
        when(yi == 0, lambda: ry_copy(kind, zz, hi, 0, yi + 1).start())
        when(yi == B - 1, lambda: ry_copy(kind, zz, lo, 1, yi - 1).start())

    def ry_recv(kind, t, zz):
        hi, lo = B - 1 - t, t
        for target, d, cond, onward in (
            (hi, 0, both(yi > 0, yi <= hi), both(yi > 0, yi < hi)),
            (lo, 1, both(yi < B - 1, yi >= lo), both(yi < B - 1, yi > lo)),
        ):

            def go(target=target, d=d):
                ry_copy(kind, zz, target, d, yi).wait_recv()
                add_into(wunit(GR[kind], kind, zz, target), ry_slot(kind, zz, target, d, yi))

            when(cond, go)
            if B > 2:
                when(
                    onward,
                    lambda target=target, d=d: ry_copy(
                        kind, zz, target, d, yi + 1 - 2 * d
                    ).start(),
                )

    def ry_drain(kind):
        for zz in {PROJ: [c], CROSS: [zi], VEC: [zi]}.get(kind, list(range(A))):
            for target in range(B):
                when(yi < target, lambda zz=zz, target=target: ry_copy(kind, zz, target, 0, yi + 1).wait_send())
                when(yi > target, lambda zz=zz, target=target: ry_copy(kind, zz, target, 1, yi - 1).wait_send())

    def rz_cols(kind):
        return [(yi + i) % B for i in range(B)] if kind == CROSS else [yi]

    def rz_slot(kind, which, col):
        r = s.rows[kind]
        return rows(ZB[kind], (which * B + col if kind == CROSS else which) * r, r)

    def rz_copy(kind, which, col):
        at = which * B + col if kind == CROSS else which
        return rcopy(
            wunit(GR[kind], kind, by_step[which], col),
            rz_slot(kind, which, col),
            n["zs" + NAMES[kind]].at[at],
            n["zr" + NAMES[kind]].at[at],
            (c, (pair_z, pair_z, far_z)[which] * B + yi),
        )

    def rz_take(kind, which, target, col):
        rz_copy(kind, which, col).wait_recv()
        add_into(wunit(GR[kind], kind, target, col), rz_slot(kind, which, col))

    def rz_pair(kind, which):
        def go():
            for col in rz_cols(kind):
                rz_copy(kind, which, col).start()

        when(has(kind, by_step[which]), go)

    def rz_far(kind):
        def go():
            for col in rz_cols(kind):
                rz_take(kind, 0, far_z, col)
                rz_copy(kind, 2, col).start()

        when(has(kind, far_z), go)

    def rz_sum(kind):
        def go():
            for col in rz_cols(kind):
                rz_take(kind, 1, zi, col)
                rz_take(kind, 2, zi, col)

        when(has(kind, zi), go)

    def rz_drain(kind):
        for which in range(3):

            def go(which=which):
                for col in rz_cols(kind):
                    rz_copy(kind, which, col).wait_send()

            when(has(kind, by_step[which]), go)

    def ry_first(kind):
        for t in range(B - 2):
            for zz in ry_zz(kind):
                if t:
                    ry_send(kind, t, zz)
                ry_recv(kind, t, zz)
        if B > 2:
            for zz in ry_zz(kind):
                ry_send(kind, B - 2, zz)

    def ry_start(kind):
        if kind in s.kinds:
            for zz in ry_zz(kind):
                ry_send(kind, 0, zz)

    def if_kind(kind, fn, *args):
        if kind in s.kinds:
            fn(kind, *args)

    def ry_unit(kind, i):
        if i == 0:
            ry_first(kind)
        ry_recv(kind, B - 2, by_step[i])
        if i < 2:
            rz_pair(kind, i)

    def vs_copy(source, target):
        return rcopy(
            rows(GR[VEC], target * B * VROWS, B * VROWS),
            rows(ZB[VEC], source * B * VROWS, B * VROWS),
            n["zsv"].at[target],
            n["zrv"].at[source],
            (c, target * B + yi),
        )

    def vs_start():
        for i in range(1, A):
            vs_copy(zi, (zi + i) % A).start()

    def vs_sum():
        mine = rows(GR[VEC], zi * B * VROWS, B * VROWS)
        for i in range(1, A):
            source = (zi + i) % A
            vs_copy(source, zi).wait_recv()
            add_into(mine, rows(ZB[VEC], source * B * VROWS, B * VROWS))

    def vs_drain():
        for i in range(1, A):
            vs_copy(zi, (zi + i) % A).wait_send()

    def ry_vec():
        ry_first(VEC)
        ry_recv(VEC, B - 2, zi)

    def ry_cross():
        ry_first(CROSS)
        ry_recv(CROSS, B - 2, zi)

    def ry_proj():
        ry_first(PROJ)
        ry_recv(PROJ, B - 2, c)
        rz_pair(PROJ, 0)
        rz_pair(PROJ, 1)

    def fa_has(kind, slot):
        return (zi == slot) if kind == PROJ else (c == c)

    def fa_dst(kind, slot):
        if kind == VEC:
            return rows(n["FV"], slot * VROWS, VROWS)
        if kind == PROJ:
            return n["out_p"]
        out = n["out_" + s.buffer[kind]]
        if s.buffer[kind] == "d":
            return rows(out, slot * s.hc + s.offset[kind], s.rows[kind])
        return out.at[slot, pl.ds(s.offset[kind], s.rows[kind])]

    def fa_copy(kind, slot, which):
        src = wunit(GR[kind], kind, zi, yi) if which < 2 else fa_dst(kind, slot)
        return rcopy(
            src, fa_dst(kind, slot), n["fa_s"].at[kind, which], n["fa_r"].at[kind, which], (sib, xn, sib)[which]
        )

    def fa_local(kind):
        return pltpu.make_async_copy(wunit(GR[kind], kind, zi, yi), fa_dst(kind, c), n["fa_l"].at[kind])

    def each(copies, what):
        for copy in copies:
            getattr(copy, what)()

    def fa_start(kind):
        def go():
            fa_copy(kind, c, 1).start()
            fa_copy(kind, c, 0).start()
            fa_local(kind).start()

        when(fa_has(kind, c), go)

    def fa_fwd(kind):
        def go():
            fa_copy(kind, xn_c, 1).wait_recv()
            fa_copy(kind, xn_c, 2).start()

        when(fa_has(kind, xn_c), go)

    def fa_end(kind):
        when(fa_has(kind, sib_c), lambda: fa_copy(kind, sib_c, 0).wait_recv())
        when(fa_has(kind, xs_c), lambda: fa_copy(kind, xs_c, 2).wait_recv())

        def own():
            fa_copy(kind, c, 1).wait_send()
            fa_copy(kind, c, 0).wait_send()
            fa_local(kind).wait()

        when(fa_has(kind, c), own)
        when(fa_has(kind, xn_c), lambda: fa_copy(kind, xn_c, 2).wait_send())

    PC = (n["Po"], n["Pc"])

    def cr_copy(arr, which, slot):
        if which < 2:
            return rcopy(
                rows(PC[arr], slot * T, T),
                n["r1"].at[arr, pl.ds(which * T, T)],
                n["cr_s"].at[arr, which],
                n["cr_r"].at[arr, which],
                sib,
            )
        return rcopy(rows(PC[arr], slot * T, T), n["r2"].at[arr], n["cr_s"].at[arr, 2], n["cr_r"].at[arr, 2], xn)

    def cr_start(arr):
        cr_copy(arr, 1, xs_c).start()
        cr_copy(arr, 0, sib_c).start()

    def cr_mid(arr):
        cr_copy(arr, 1, xs_c).wait_recv()
        add_into(rows(PC[arr], xn_c * T, T), n["r1"].at[arr, pl.ds(T, T)])
        cr_copy(arr, 2, xn_c).start()

    def cr_wait(arr):
        cr_copy(arr, 0, sib_c).wait_recv()
        cr_copy(arr, 2, xn_c).wait_recv()

    def cr_drain(arr):
        cr_copy(arr, 1, xs_c).wait_send()
        cr_copy(arr, 0, sib_c).wait_send()
        cr_copy(arr, 2, xn_c).wait_send()

    vecs, cos, sin = n["vecs"], n["cos"], n["sin"]

    def vec(row, width=D):
        return vecs[row : row + 1, 0:width]

    def loop(count, fn, first=0):
        def step(i, carry):
            fn(i)
            return carry

        lax.fori_loop(first, count, step, 0)

    def tile(ref, start, size, cols=slice(None)):
        return ref[pl.ds(mult(start, size), size), cols]

    def here(j, k, width):
        at = 8 * (j // 2) + j % 2
        return jnp.where(n["Bs"][at : at + 1, 0:width] == k, 1.0, 0.0)

    def to_order(dst, src):
        def one(k):
            total = None
            for j in range(2 * s.nctx):
                w = here(j, k, src.shape[1]).astype(src.dtype)
                term = src[j * BLK : (j + 1) * BLK, :] * w
                total = term if total is None else total + term
            dst[pl.ds(mult(k * BLK, BLK), BLK), :] = total

        loop(2 * s.nctx, one)

    def from_order(src, put):
        for j in range(2 * s.nctx):
            total = None
            for k in range(2 * s.nctx):
                w = here(j, k, src.shape[1]).astype(src.dtype)
                term = src[k * BLK : (k + 1) * BLK, :] * w
                total = term if total is None else total + term
            put(slice(j * BLK, (j + 1) * BLK), total)

    def norms(slot):
        def one(i):
            at = pl.ds(mult(slot * T + i * BLK, BLK), BLK)
            x = n["Xs"][at, :].astype(F32)
            center = x - jnp.mean(x, axis=-1, keepdims=True)
            nn = center * lax.rsqrt(jnp.mean(center * center, axis=-1, keepdims=True) + EPS)
            n["nb"][at, :] = nn.astype(BF)
            n["A1"][at, :] = (nn * vec(0) + vec(1)).astype(BF)
            n["A2"][at, :] = (nn * vec(2) + vec(3)).astype(BF)

        loop(T // BLK, one)

    lane64 = lax.broadcasted_iota(jnp.int32, (T, 128), 1) % HEAD_DIM
    first_half = lane64 < ROT // 2

    def rope(u, cs_, sn_, sign):
        partner = jnp.where(first_half, pltpu.roll(u, 128 - ROT // 2, 1), pltpu.roll(u, ROT // 2, 1))
        return u * cs_ + (partner * sn_) * sign

    def tables():
        def put(name):
            def store(at, value):
                n[name][at, :] = value

            return store

        from_order(cos, put("cos_st"))
        from_order(sin, put("sin_st"))

    raw, S = n["Pc"], n["S"]

    def qkv():
        def one(i):
            at = pl.ds(mult(i * T, T), T)
            j = dot(n["A1"][at, :], n["Wi"][...]) + vec(7, 3 * G)
            cs_, sn_ = n["cos_st"][at, :], n["sin_st"][at, :]
            for p in range(G // 128):
                lo = 128 * p
                q = rope(j[:, lo : lo + 128], cs_, sn_, 1.0).astype(BF)
                raw[at, lo : lo + 128] = (q.astype(F32) * HEAD_DIM**-0.5).astype(BF)
                raw[at, G + lo : G + lo + 128] = rope(j[:, G + lo : G + lo + 128], cs_, sn_, 1.0).astype(BF)
            raw[at, 2 * G : 3 * G] = j[:, 2 * G : 3 * G].astype(BF)

        loop(N // T, one)

    def dattended():
        def one(i):
            at = pl.ds(mult(i * T, T), T)
            raw[at, 3 * G : 4 * G] = dot11(n["Gs"][at, :], n["Wp"][...]).astype(BF)

        loop(N // T, one)

    def order():
        to_order(S, raw)

    def zero_dkv():
        n["dk"][...] = jnp.zeros((N, G), F32)
        n["dv"][...] = jnp.zeros((N, G), F32)

    def attention(p, i):
        L = (i + 1) * T
        cols = slice(128 * p, 128 * p + 128)
        at = slice(i * T, i * T + T)
        part = [slice(j * G + 128 * p, j * G + 128 * p + 128) for j in range(4)]
        kb, vb = S[0:L, part[1]], S[0:L, part[2]]
        qb, db = S[at, part[0]], S[at, part[3]]
        lane = lax.broadcasted_iota(jnp.int32, (T, 128), 1)
        key_at = lax.broadcasted_iota(jnp.int32, (T, T), 0)
        query_at = lax.broadcasted_iota(jnp.int32, (T, T), 1)
        keep = key_at <= query_at
        outs, dqs, ps, ds_, qs, dbs = [], [], [], [], [], []
        for h in range(2):
            mine = (lane >= HEAD_DIM) if h else (lane < HEAD_DIM)
            qh = jnp.where(mine, qb, jnp.zeros_like(qb))
            dh = jnp.where(mine, db, jnp.zeros_like(db))
            sc = dot11(kb, qh)
            last = jnp.where(keep, sc[L - T :], -1e30)
            sc = last if i == 0 else jnp.concatenate([sc[: L - T], last], axis=0)
            e = jnp.exp(sc - jnp.max(sc, axis=0, keepdims=True))
            pr = e * (1.0 / jnp.sum(e, axis=0, keepdims=True))
            dp = dot11(vb, dh)
            delta = jnp.sum(pr * dp, axis=0, keepdims=True)
            dsl = (pr * (dp - delta)).astype(BF)
            pb = pr.astype(BF)
            outs.append(dot00(vb, pb))
            dqs.append(dot00(kb, dsl))
            n["dv"][0:L, cols] += dot(pb, dh)
            n["dk"][0:L, cols] += dot(dsl, qh)
        feature = lax.broadcasted_iota(jnp.int32, (128, T), 0)
        raw[at, part[3]] = jnp.where(feature < HEAD_DIM, outs[0], outs[1]).T.astype(BF)
        n["dq"][at, cols] = jnp.where(feature < HEAD_DIM, dqs[0], dqs[1]).T * HEAD_DIM**-0.5

    def joined_back():
        n["cs"][2:3, :] = jnp.zeros((1, D), F32)

        def one(i):
            at = pl.ds(mult(i * T, T), T)
            cs_, sn_ = cos[at, :], sin[at, :]
            for p in range(G // 128):
                cols = slice(128 * p, 128 * p + 128)
                for j, (name, turn) in enumerate((("dq", True), ("dk", True), ("dv", False))):
                    u = n[name][at, cols]
                    if turn:
                        u = rope(u, cs_, sn_, -1.0)
                    u = u.astype(BF)
                    lo = j * G + 128 * p
                    raw[at, lo : lo + 128] = u
                    n["cs"][2:3, lo : lo + 128] += jnp.sum(u.astype(F32), axis=0, keepdims=True)

        loop(N // T, one)

        def put(at, value):
            n["dj"][at, :] = value[:, 0 : 3 * G]
            n["att_st"][at, :] = value[:, 3 * G : 4 * G]

        from_order(raw, put)

    def in_grad():
        def one(i):
            at = pl.ds(mult(i * 256, 256), 256)
            n["Gi"][at, :] = dot00(n["A1"][:, at], n["dj"][...]).astype(BF)

        loop(D // 256, one)

    def proj_grad():
        def one(i):
            at = pl.ds(mult(i * 256, 256), 256)
            n["Gp"][:, at] = dot00(n["att_st"][...], n["Gs"][:, at]).astype(BF)

        loop(D // 256, one)

    def mlp_up(part):
        def one(i):
            at = pl.ds(mult((i // 4) * T, T), T)
            cols = pl.ds(mult((i % 4) * 256, 256), 256)
            x = dot(n["A2"][at, :], n["Wu"][:, cols]) + vecs[6:7, cols]
            phi = 0.5 + 0.5 * lax.erf(x * math.sqrt(0.5))
            pdf = jnp.exp(-0.5 * x * x) * (1.0 / math.sqrt(2.0 * math.pi))
            n["act"][at, cols] = (x * phi).astype(BF)
            n["gp"][at, cols] = (phi + x * pdf).astype(BF)

        loop(4 * part + 4, one, 4 * part)

    def down_grad(part):
        def one(i):
            at = pl.ds(mult(i * 256, 256), 256)
            n["Gd"][at, :] = dot00(n["act"][:, at], n["Gs"][...]).astype(BF)

        loop(H // 512 * (part + 1), one, H // 512 * part)

    def mlp_back(part):
        if part == 0:
            n["cs"][6:7, :] = jnp.zeros((1, D), F32)

        def one(i):
            at = pl.ds(mult((i // 4) * T, T), T)
            cols = pl.ds(mult((i % 4) * 256, 256), 256)
            da = dot11(n["Gs"][at, :], n["Wd"][cols, :])
            dl = (da * n["gp"][at, cols].astype(F32)).astype(BF)
            n["dl"][at, cols] = dl
            n["cs"][6:7, cols] += jnp.sum(dl.astype(F32), axis=0, keepdims=True)

        loop(4 * part + 4, one, 4 * part)

    def up_grad(part):
        def one(i):
            at = pl.ds(mult(i * 256, 256), 256)
            n["Gu"][at, :] = dot00(n["A2"][:, at], n["dl"][...]).astype(BF)

        loop(D // 512 * (part + 1), one, D // 512 * part)

    def out_part():
        def one(i):
            at = pl.ds(mult(i * T, T), T)
            n["Po"][at, :] = (dot(n["att_st"][at, :], n["Wp"][...]) + dot(n["act"][at, :], n["Wd"][...])).astype(BF)

        loop(N // T, one)

    def input_part():
        for row in (0, 1, 4, 5):
            n["cs"][row : row + 1, :] = jnp.zeros((1, D), F32)

        def one(i):
            at = pl.ds(mult(i * T, T), T)
            nn = n["nb"][at, :].astype(F32)
            e1 = dot11(n["dj"][at, :], n["Wi"][...])
            n["cs"][0:1, :] += jnp.sum(e1 * nn, axis=0, keepdims=True)
            n["cs"][1:2, :] += jnp.sum(e1, axis=0, keepdims=True)
            e2 = dot11(n["dl"][at, :], n["Wu"][...])
            n["cs"][4:5, :] += jnp.sum(e2 * nn, axis=0, keepdims=True)
            n["cs"][5:6, :] += jnp.sum(e2, axis=0, keepdims=True)
            n["Pc"][at, :] = (e1 * vec(0) + e2 * vec(2)).astype(BF)

        loop(N // T, one)

    def own_g_sum():
        n["cs"][7:8, :] = jnp.zeros((1, D), F32)
        g = tile(n["Gs"], c * T, T).astype(F32)
        n["cs"][3:4, :] = jnp.sum(g, axis=0, keepdims=True)

    def finish_out():
        base = c * T
        x = tile(n["Xs"], base, T).astype(F32)
        total = tile(n["Po"], base, T).astype(F32) + n["r1"][0, 0:T].astype(F32) + n["r2"][0].astype(F32)
        n["xo"][...] = (x + total + vec(4) + vec(5)).astype(BF)

    def finish_input():
        base = c * T
        x = tile(n["Xs"], base, T).astype(F32)
        center = x - jnp.mean(x, axis=-1, keepdims=True)
        rstd = lax.rsqrt(jnp.mean(center * center, axis=-1, keepdims=True) + EPS)
        nn = center * rstd
        cc = tile(n["Pc"], base, T).astype(F32) + n["r1"][1, 0:T].astype(F32) + n["r2"][1].astype(F32)
        mean_c = jnp.mean(cc, axis=-1, keepdims=True)
        mean_cn = jnp.mean(cc * nn, axis=-1, keepdims=True)
        n["xg"][...] = tile(n["Gs"], base, T).astype(F32) + (cc - mean_c - nn * mean_cn) * rstd

    def unpack_vectors():
        for j in range(s.F):
            cols = slice(j * 128, (j + 1) * 128)
            n["vecs"][0:6, cols] = n["Wv"][j * VROWS : j * VROWS + 6, :]
            n["vecs"][6:7, cols] = n["Wv"][pl.ds(j * VROWS + 6 + c, 1), :]
        per = G // 128
        for j in range(3):
            for p in range(per):
                b = j * (D // 128) + c * per + p
                lo = (j * per + p) * 128
                n["vecs"][7:8, lo : lo + 128] = n["Wv"][pl.ds((b // 3) * VROWS + 6 + s.nctx + b % 3, 1), :]

    def pack_sums():
        n["Gv"][...] = jnp.zeros((s.F * VROWS, 128), F32)
        cs = n["cs"]
        for j in range(s.F):
            cols = slice(j * 128, (j + 1) * 128)
            base = j * VROWS
            for row, place in ((0, 0), (1, 1), (3, 5), (4, 6), (5, 7)):
                n["Gv"][base + place : base + place + 1, :] = cs[row : row + 1, cols]
            n["Gv"][pl.ds(base + 8 + c, 1), :] = cs[6:7, cols]
        per = G // 128
        for j in range(3):
            for p in range(per):
                b = j * (D // 128) + c * per + p
                lo = (j * per + p) * 128
                n["Gv"][pl.ds((b // 3) * VROWS + 2 + b % 3, 1), :] = cs[2:3, lo : lo + 128]

    def local(i, src, dst):
        return pltpu.make_async_copy(src, dst, n["loc"].at[i])

    own_i = rows(n["Wi"], (zi * B + yi) * R, R)
    own_u = wunit(W[UP], UP, zi, yi)
    hc = s.hc
    lc = {
        "x": [local(0, n["x"], rows(n["Xs"], c * T, T))],
        "i": [
            pltpu.make_async_copy(
                n["w_i"].at[:, pl.ds(mult(j * D + c * G, 128), G)], own_i.at[:, pl.ds(j * G, G)], n["loc_i"].at[j]
            )
            for j in range(3)
        ],
        "p": [local(3, n["w_p"], wunit(W[PROJ], PROJ, zi, yi))],
        "g": [local(4, n["g"], rows(n["Gs"], c * T, T))],
        "u": [local(5, n["w_u"], own_u)]
        if not s.packed
        else [
            pltpu.make_async_copy(
                n["w_u"].at[:, pl.ds(mult((j * s.nctx + c) * hc, 128), hc)],
                own_u.at[:, pl.ds(j * hc, hc)],
                n["loc_u"].at[j],
            )
            for j in range(s.F)
        ],
        "d": [local(6, rows(n["w_d"], c * hc, hc), rows(n["Wd"], (zi * B + yi) * hc, hc))],
    }
    if s.packed:
        lc["v"] = [
            pltpu.make_async_copy(n[f"vec{i}"], n[f"vin{i}"], n["loc_v"].at[i]) for i in range(len(s.vector_rows))
        ]

    def lstart(key):
        if key == "p":
            when(zi == c, lambda: each(lc[key], "start"))
        else:
            each(lc[key], "start")

    def lwait(key):
        if key == "p":
            when(zi == c, lambda: each(lc[key], "wait"))
        else:
            each(lc[key], "wait")

    for key in lc:
        lstart(key)
    bar = pltpu.get_barrier_semaphore()
    for dev in (sib, xn):
        pl.semaphore_signal(bar, inc=1, device_id=dev, device_id_type=MESH)
    for step in range(1, A):
        pl.semaphore_signal(bar, inc=1, device_id=(c, (zi + step) % A * B + yi), device_id_type=MESH)
    for d in (2, 3):
        when(
            edge[d],
            lambda d=d: pl.semaphore_signal(bar, inc=1, device_id=hop[d], device_id_type=MESH),
        )
    count = 2 + A - 1 + sum(jnp.where(e, 1, 0) for e in edge[2:])
    pl.semaphore_wait(bar, count)

    for key in lc:
        if key != "p":
            lwait(key)
    lwait("p")

    def blocks_start():
        for j in range(T // BLK):
            first = n["places"][0:1, j * BLK : j * BLK + 1] // BLK
            n["Bs"][pl.ds(c * 8 + j, 1), :] = jnp.broadcast_to(first, (1, D))
        xa_start(2)

    def vectors_start():
        if s.packed:
            at = (zi * B + yi) * VROWS
            for i, count in enumerate(s.vector_rows):
                for j in range(count):
                    n["Wv"][pl.ds(at, 1), :] = n[f"vin{i}"][j * 128 : (j + 1) * 128].astype(F32).reshape(1, 128)
                    at = at + 1
            va_start()

    def vectors_z():
        if s.packed:
            va_z()

    def vectors_y():
        if s.packed:
            ag_y(VEC)
            unpack_vectors()

    def sums_start():
        if s.packed:
            pack_sums()
            vs_start()

    def sums_y():
        if s.packed:
            vs_sum()
            ry_send(VEC, 0, zi)

    def sums_end():
        if s.packed:
            ry_vec()
            fa_start(VEC)

    def sums_fwd():
        if s.packed:
            fa_fwd(VEC)

    def cross_pair():
        rz_pair(CROSS, 0)
        rz_pair(CROSS, 1)

    def cross_y():
        rz_sum(CROSS)
        ry_send(CROSS, 0, zi)

    def cross_end():
        ry_cross()
        fa_start(CROSS)

    def done(kind):
        rz_sum(kind)
        fa_start(kind)

    put_out = local(12, n["xo"], n["out"])
    put_in = local(13, n["xg"], n["input_grad"])

    def store_out():
        cr_wait(0)
        finish_out()
        put_out.start()

    def store_input():
        cr_wait(1)
        finish_input()
        put_in.start()

    vectors_start()
    own_g_sum()
    ag_start(IN)
    xa_start(0)
    ag_start(PROJ)
    vectors_z()
    blocks_start()
    ag_z(IN, 0)
    ag_z(PROJ, 0)
    xa_start(1)
    xa_fwd(0)
    ag_z(IN, 1)
    xa_wait(0, sib_c)
    vectors_y()
    norms(xn_c)
    xa_fwd(2)
    xa_wait(1, sib_c)
    ag_z(PROJ, 1)
    ag_z(IN, 2)
    ag_start(CROSS)
    xa_wait(2, xs_c)
    zero_dkv()
    xa_wait(0, xs_c)
    norms(c)
    xa_wait(2, sib_c)
    ag_z(PROJ, 2)
    ag_start(UP)
    tables()
    norms(sib_c)
    norms(xs_c)
    xa_fwd(1)
    ag_start(DOWN)
    ag_y(IN)
    qkv()
    xa_wait(1, xs_c)
    ag_y(PROJ)
    dattended()
    order()
    ag_z(UP, 0)
    attention(0, 0)
    attention(0, 1)
    attention(0, 2)
    ag_y(CROSS)
    attention(0, 3)
    ag_z(UP, 1)
    attention(1, 0)
    attention(1, 1)
    attention(1, 2)
    ag_z(CROSS, 0)
    ag_z(UP, 2)
    attention(1, 3)
    joined_back()
    proj_grad()
    ag_z(CROSS, 1)
    ry_start(PROJ)
    ag_y(UP)
    ag_z(DOWN, 0)
    mlp_up(0)
    mlp_up(1)
    mlp_up(2)
    mlp_up(3)
    ag_z(DOWN, 1)
    down_grad(0)
    ry_proj()
    ag_z(DOWN, 2)
    down_grad(1)
    cross_pair()
    ag_z(CROSS, 2)
    ry_start(DOWN)
    ag_y(DOWN)
    in_grad()
    out_part()
    rz_far(PROJ)
    mlp_back(0)
    ry_unit(DOWN, 0)
    mlp_back(1)
    mlp_back(2)
    ry_start(PIECE)
    cr_start(0)
    mlp_back(3)
    rz_far(CROSS)
    up_grad(0)
    cr_mid(0)
    up_grad(1)
    ry_unit(DOWN, 1)
    ry_start(UP)
    if_kind(PIECE, ry_unit, 0)
    if_kind(PIECE, ry_unit, 1)
    ry_unit(DOWN, 2)
    rz_far(DOWN)
    input_part()
    ry_unit(UP, 0)
    cr_start(1)
    done(PROJ)
    if_kind(PIECE, ry_unit, 2)
    if_kind(PIECE, rz_far)
    cr_mid(1)
    ry_unit(DOWN, 3)
    ry_unit(UP, 1)
    ry_unit(UP, 2)
    rz_far(UP)
    cross_y()
    ry_start(IN)
    done(DOWN)
    if_kind(PIECE, ry_unit, 3)
    ry_unit(UP, 3)
    cross_end()
    sums_start()
    ry_unit(IN, 0)
    if_kind(PIECE, done)
    ry_unit(IN, 1)
    done(UP)
    fa_fwd(DOWN)
    ry_unit(IN, 2)
    rz_far(IN)
    sums_y()
    ry_unit(IN, 3)
    fa_fwd(PROJ)
    store_input()
    done(IN)
    store_out()
    sums_end()
    fa_fwd(CROSS)
    if_kind(PIECE, fa_fwd)
    fa_fwd(UP)
    fa_fwd(IN)
    sums_fwd()
    for kind in s.kinds:
        fa_end(kind)
    if s.packed:
        n["vtot"][...] = sum(n["FV"][j * VROWS : (j + 1) * VROWS, :] for j in range(s.nctx))
    put_cs = local(14, n["vtot"] if s.packed else n["cs"], n["sums"])
    put_cs.start()
    for kind in s.kinds:
        ry_drain(kind)
        if kind == VEC:
            va_drain()
            vs_drain()
        else:
            if kind in s.gathered:
                ag_drain(kind)
            rz_drain(kind)
    for arr in range(3):
        xa_drain(arr)
    for arr in range(2):
        cr_drain(arr)
    put_out.wait()
    put_in.wait()
    put_cs.wait()


def finish_kernel(s, hidden, *refs):
    gi, gp, gu, gd, out, input_grad, sums = refs[:7]
    to = refs[7:]
    to[0][...] = out[...]
    to[1][...] = input_grad[...]
    for slot in range(s.nctx):
        for j in range(3):
            lo = j * s.D + slot * s.G
            to[2][:, lo : lo + s.G] = gi[slot, :, j * s.G : (j + 1) * s.G].astype(F32)
        for j in range(s.F):
            lo = (j * s.nctx + slot) * s.hc
            to[4][:, lo : lo + s.hc] = gu[slot, :, j * s.hc : (j + 1) * s.hc].astype(F32)
    to[3][...] = gp[...].astype(F32)
    to[5][...] = gd[...].astype(F32)
    singles = ((0, 6), (1, 7), (5, 8), (6, 9), (7, 10), (5, 11))
    for row, at in singles:
        to[at][...] = sums[row, :]
    for first, count, at in ((2, 3, 12), (8, s.nctx, 13)):
        for j in range(count):
            to[at][j * 128 : (j + 1) * 128] = sums[first + j, :]


def finish(s, hidden, arrays):
    steps = max(1, s.R // 64)

    def part(shape):
        if len(shape) == 3:
            return pl.BlockSpec((shape[0], shape[1] // steps, shape[2]), lambda i: (0, i, 0))
        return pl.BlockSpec((shape[0] // steps, shape[1]), lambda i: (i, 0))

    def whole(shape):
        return pl.BlockSpec(shape, lambda i: (0,) * len(shape))

    D = s.D
    shapes = [(s.T, D), (s.T, D), (s.R, 3 * D), (s.R, D), (s.R, hidden), (hidden // s.F, D)]
    types = [BF, F32, F32, F32, F32, F32]
    small = [(128,)] * 6 + [(3 * s.R,), (hidden // s.F,)]
    return pl.pallas_call(
        lambda *refs: finish_kernel(s, hidden, *refs),
        grid=(steps,),
        out_shape=tuple(jax.ShapeDtypeStruct(sh, dt) for sh, dt in zip(shapes + small, types + [F32] * 8)),
        in_specs=[part(a.shape) for a in arrays[:-1]] + [whole(arrays[-1].shape)],
        out_specs=tuple([part(sh) for sh in shapes] + [whole(sh) for sh in small]),
        compiler_params=pltpu.CompilerParams(vmem_limit_bytes=63 << 20),
        name="finish",
    )(*arrays)


def rope_tables(length):
    half = ROT // 2
    freq = np.power(np.float32(10000.0), np.float32(-2.0) * np.arange(half, dtype=np.float32) / np.float32(ROT))
    angle = np.arange(length, dtype=np.float32)[:, None] * freq[None, :].astype(np.float32)
    cos = np.ones((length, 128), np.float32)
    sin = np.zeros((length, 128), np.float32)
    for base in range(0, 128, HEAD_DIM):
        cos[:, base : base + half] = np.cos(angle)
        cos[:, base + half : base + ROT] = np.cos(angle)
        sin[:, base : base + half] = -np.sin(angle)
        sin[:, base + half : base + ROT] = np.sin(angle)
    return cos, sin


def body(
    hidden_in,
    positions,
    out_grad,
    attn_gain,
    attn_shift,
    in_weight,
    in_bias,
    proj_weight,
    proj_bias,
    mlp_gain,
    mlp_shift,
    up_weight,
    up_bias,
    down_weight,
    down_bias,
):
    nctx, nshard = lax.axis_size("ctx"), lax.axis_size("fsdp")
    T, D = hidden_in.shape[1:]
    hidden = up_weight.shape[1]
    s = Sizes(T, D, hidden, nctx, nshard)
    R, G, F = s.R, s.G, s.F
    hc = s.hc
    c, f = lax.axis_index("ctx"), lax.axis_index("fsdp")

    def pick_ctx(array, axis):
        return lax.dynamic_index_in_dim(array, c, axis, keepdims=False)

    small = [attn_gain, attn_shift, mlp_gain, mlp_shift, proj_bias, down_bias, up_bias, in_bias]
    if s.packed:
        w_u = up_weight
        extra = {f"vec{i}": v for i, v in enumerate(small)}
    else:
        w_u = pick_ctx(up_weight.reshape(R, F, nctx, hc), 2).reshape(R, s.H)
        lengths = [v.shape[0] for v in small]
        gathered = lax.all_gather(jnp.concatenate(small).astype(F32), "fsdp", axis=0)
        full, at = [], 0
        for length in lengths:
            full.append(gathered[:, at : at + length].reshape(-1))
            at += length
        full[6] = pick_ctx(full[6].reshape(F, nctx, hc), 1).reshape(-1)
        full[7] = jnp.pad(pick_ctx(full[7].reshape(3, nctx, G), 1).reshape(-1), (0, D - 3 * G))
        extra = dict(vecs=jnp.stack(full))
    cos, sin = rope_tables(s.N)

    plan = scratch_plan(s)
    any_ = pl.BlockSpec(memory_space=pl.ANY)
    vmem = pl.BlockSpec(memory_space=pltpu.VMEM)
    ins = dict(
        x=hidden_in[0],
        g=out_grad[0],
        places=positions,
        w_i=in_weight,
        w_p=proj_weight,
        w_u=w_u,
        w_d=down_weight,
        **extra,
        cos=jnp.asarray(cos),
        sin=jnp.asarray(sin),
    )
    in_vmem = {"vecs", "cos", "sin", "places"}
    outs = dict(
        out=jax.ShapeDtypeStruct((T, D), BF),
        input_grad=jax.ShapeDtypeStruct((T, D), F32),
        out_i=jax.ShapeDtypeStruct((nctx, R, 3 * G), BF),
        out_p=jax.ShapeDtypeStruct((R, D), BF),
        out_u=jax.ShapeDtypeStruct((nctx, R, s.H), BF),
        out_d=jax.ShapeDtypeStruct((nctx * hc, D), BF),
        sums=jax.ShapeDtypeStruct((VROWS, 128) if s.packed else (8, D), F32),
    )
    names = list(ins) + list(outs) + list(plan)
    out, input_grad, gi, gp, gu, gd, sums = pl.pallas_call(
        lambda *refs: kernel_body(s, names, *refs),
        out_shape=tuple(outs.values()),
        in_specs=[vmem if name in in_vmem else any_ for name in ins],
        out_specs=tuple(any_ for _ in outs),
        scratch_shapes=list(plan.values()),
        compiler_params=pltpu.CompilerParams(
            collective_id=0, has_side_effects=True, vmem_limit_bytes=63 << 20
        ),
        name="block",
    )(*ins.values())

    def own(full_vector):
        length = full_vector.shape[0] // F
        return lax.dynamic_slice_in_dim(full_vector, f * length, length)

    if s.packed:
        done = finish(s, hidden, (gi, gp, gu, gd, out, input_grad, sums))
        out, input_grad, in_total, proj_total, up_total, down_total = done[:6]
        gain1, shift1, g_sum, gain2, shift2, g_again, in_bias_sum, up_bias_sum = done[6:]
    else:
        here = (jnp.arange(nctx) == c).astype(F32)
        in_b = (sums[2, : 3 * G].reshape(3, 1, G) * here[None, :, None]).reshape(-1)
        up_b = (sums[6].reshape(F, 1, hc) * here[None, :, None]).reshape(-1)
        total = lax.psum(
            jnp.concatenate([sums[0], sums[1], in_b, sums[3], sums[4], sums[5], up_b]), ("ctx", "fsdp")
        )
        parts, at = [], 0
        for length in (D, D, 3 * D, D, D, D, hidden):
            parts.append(own(total[at : at + length]))
            at += length
        gain1, shift1, in_bias_sum, g_sum, gain2, shift2, up_bias_sum = parts
        g_again = g_sum
        in_total = gi.astype(F32).reshape(nctx, R, 3, G).transpose(1, 2, 0, 3).reshape(R, 3 * D)
        proj_total, down_total = gp.astype(F32), gd.astype(F32)
        up_total = gu.astype(F32).reshape(nctx, R, F, hc).transpose(1, 2, 0, 3).reshape(R, hidden)
    return (
        out[None],
        input_grad[None],
        gain1,
        shift1,
        in_total,
        in_bias_sum,
        proj_total,
        g_sum,
        gain2,
        shift2,
        up_total,
        up_bias_sum,
        down_total,
        g_again,
    )


def solution(mesh):
    tok, vec, mat = P("fsdp", "ctx", None), P("fsdp"), P("fsdp", None)
    placed = (tok, P("fsdp", "ctx"), tok, vec, vec, mat, vec, mat, vec, vec, vec, mat, vec, mat, vec)
    return jax.shard_map(
        body,
        mesh=mesh,
        in_specs=placed,
        out_specs=(tok, tok, vec, vec, mat, vec, mat, vec, vec, vec, mat, vec, mat, vec),
        check_vma=False,
    )
```

```python
import math

import jax
import jax.numpy as jnp
import numpy as np
from jax import lax
from jax.experimental import pallas as pl
from jax.experimental.pallas import tpu as pltpu
from jax.sharding import PartitionSpec as P

HEADS = 16
HEAD_DIM = 64
ROT = 16
BLK = 128
EPS = 1e-05
MESH = pl.DeviceIdType.MESH
BF = jnp.bfloat16
F32 = jnp.float32
IN, PROJ, UP, DOWN, VEC, CROSS, PIECE = range(7)
PIECES = 2
NAMES = "ipudvefgh"
VROWS = 16
BOTH1 = (((1,), (1,)), ((), ()))
BOTH0 = (((0,), (0,)), ((), ()))


def dot(a, b):
    return jnp.dot(a, b, preferred_element_type=F32)


def dot11(a, b):
    return lax.dot_general(a, b, BOTH1, preferred_element_type=F32)


def dot00(a, b):
    return lax.dot_general(a, b, BOTH0, preferred_element_type=F32)


def mult(value, of):
    return pl.multiple_of(value, of)


def both(*conds):
    out = conds[0]
    for cond in conds[1:]:
        out = jnp.logical_and(out, cond)
    return out


class Sizes:
    def __init__(self, tokens, width, hidden, nctx, nshard):
        self.T = tokens
        self.N = tokens * nctx
        self.D = width
        self.H = hidden // nctx
        self.G = width // nctx
        self.nctx = nctx
        self.F = nshard
        self.A = nctx
        self.B = nshard // nctx
        self.R = width // nshard
        self.hc = hidden // nshard // nctx
        self.vector_rows = (1, 1, 1, 1, 1, 1, nctx, 3)
        self.packed = self.R % 128 == 0 and self.hc % 128 == 0
        half = self.hc // 2
        pieces = min(PIECES, self.R // 16)
        part = self.R // pieces
        more = pieces - 1
        self.pieces = (IN,) + tuple(range(PIECE, PIECE + more))
        self.buffer = ("i", "p", "u", "d", "v", "d") + ("i",) * more
        self.stride = (self.R, self.R, self.R, self.hc, VROWS, self.hc) + (self.R,) * more
        self.offset = (0, 0, 0, 0, 0, self.hc - half) + tuple(part * (i + 1) for i in range(more))
        self.rows = (part, self.R, self.R, self.hc - half, VROWS, half) + (part,) * more
        self.gather_rows = (self.R,) + self.rows[1:]
        self.cols = (3 * self.G, width, self.H, width, 128, width) + (3 * self.G,) * more
        self.units = (self.F, self.B, self.F, self.F, self.F, self.F) + (self.F,) * more
        self.types = (BF, BF, BF, BF, F32, BF) + (BF,) * more
        self.gathered = (IN, PROJ, UP, DOWN, CROSS) + ((VEC,) if self.packed else ())
        self.kinds = self.gathered + self.pieces[1:]
        self.NY = 1 if self.B == 2 else self.B + 1


def scratch_plan(s):
    N, D, G, H = s.N, s.D, s.G, s.H
    vm = pltpu.VMEM
    dma = pltpu.SemaphoreType.DMA
    plan = dict(
        Xs=vm((N, D), BF),
        Gs=vm((N, D), BF),
        Bs=vm((s.nctx * 8, D), jnp.int32),
        cos_st=vm((N, 128), F32),
        sin_st=vm((N, 128), F32),
        nb=vm((N, D), BF),
        A1=vm((N, D), BF),
        A2=vm((N, D), BF),
        S=vm((N, 4 * G), BF),
        dq=vm((N, G), F32),
        dk=vm((N, G), F32),
        dv=vm((N, G), F32),
        att_st=vm((N, G), BF),
        dj=vm((N, 3 * G), BF),
        act=vm((N, H), BF),
        gp=vm((N, H), BF),
        dl=vm((N, H), BF),
        Po=vm((N, D), BF),
        Pc=vm((N, D), BF),
        r1=vm((2, 2 * s.T, D), BF),
        r2=vm((2, s.T, D), BF),
        cs=vm((8, D), F32),
        xo=vm((s.T, D), BF),
        xg=vm((s.T, D), F32),
    )
    if s.packed:
        plan["vecs"] = vm((8, D), F32)
        plan["FV"] = vm((s.nctx * VROWS, 128), F32)
        plan["vtot"] = vm((VROWS, 128), F32)
        for i, count in enumerate(s.vector_rows):
            plan[f"vin{i}"] = vm((count * 128,), BF)
        plan["loc_v"] = dma((len(s.vector_rows),))
    A, B, F = s.A, s.B, s.F
    for kind in s.kinds:
        name = NAMES[kind]
        r, cl = s.rows[kind], s.cols[kind]
        dt = s.types[kind]
        if kind < CROSS:
            size = (s.units[kind] * s.stride[kind], cl)
            plan["W" + name] = vm(size, dt)
            plan["G" + name] = vm(size, dt)
        cross, proj = kind == CROSS, kind == PROJ
        per = 1 if cross or proj else A
        cols = B if cross else 1
        plan["Y" + name] = vm((s.NY * per * r, cl), dt)
        plan["Z" + name] = vm((A * B * r if kind == VEC else 3 * cols * r, cl), dt)
        along_y = per if B == 2 else 2 * per * B
        if kind in s.gathered:
            plan["az" + name] = dma(((2 if proj else A + 1) * cols,))
            plan["ay" + name] = dma((along_y,))
            plan["ar" + name] = dma((s.units[kind],))
        plan["ys" + name] = dma((along_y,))
        plan["yr" + name] = dma((along_y,))
        plan["zs" + name] = dma((A if kind == VEC else 3 * cols,))
        plan["zr" + name] = dma((A if kind == VEC else 3 * cols,))
    plan.update(
        xa_s=dma((3, 3)),
        xa_r=dma((3, s.nctx)),
        cr_s=dma((2, 3)),
        cr_r=dma((2, 3)),
        fa_s=dma((len(s.rows), 3)),
        fa_r=dma((len(s.rows), 3)),
        fa_l=dma((len(s.rows),)),
        loc=dma((16,)),
        loc_i=dma((3,)),
        loc_u=dma((s.F if s.packed else 1,)),
    )
    return plan


def kernel_body(s, names, *refs):
    n = dict(zip(names, refs))
    T, N, D, G, H, A, B, R = s.T, s.N, s.D, s.G, s.H, s.A, s.B, s.R
    c = lax.axis_index("ctx")
    f = lax.axis_index("fsdp")
    zi, yi = f // B, f % B
    sib_c = c + 1 - 2 * (c % 2)
    xn_c = (c + s.nctx // 2) % s.nctx
    xs_c = (sib_c + s.nctx // 2) % s.nctx
    sib, xn = (sib_c, f), (xn_c, f)
    edge = (zi < A - 1, zi > 0, yi < B - 1, yi > 0)
    hop = ((c, f + B), (c, f - B), (c, f + 1), (c, f - 1))

    def when(cond, fn):
        pl.when(cond)(fn)

    def rcopy(src, dst, ssem, rsem, dev):
        return pltpu.make_async_remote_copy(
            src_ref=src, dst_ref=dst, send_sem=ssem, recv_sem=rsem, device_id=dev, device_id_type=MESH
        )

    def rows(ref, start, size):
        return ref.at[pl.ds(mult(start, math.gcd(size, 64)), size)]

    W = [n.get("W" + x) for x in s.buffer]

    def has(kind, oz):
        return (oz == c) if kind == PROJ else (oz == oz)

    def wunit(ref, kind, oz, oy, sizes=s.rows):
        at = oy if kind == PROJ else oz * B + oy
        return rows(ref, at * s.stride[kind] + s.offset[kind], sizes[kind])

    def along_y(kind, oz, oy, d):
        per = 1 if kind in (PROJ, CROSS) else A
        at = 0 if per == 1 else oz
        return at if B == 2 else (d * per + at) * B + oy

    def ag_copy(kind, oz, oy, d):
        u = wunit(W[kind], kind, oz, oy, s.gather_rows)
        name = NAMES[kind]
        if d >= 2:
            send = n["ay" + name].at[along_y(kind, oz, oy, d - 2)]
        elif kind == PROJ:
            send = n["az" + name].at[d]
        else:
            at = oz if d == 0 else jnp.where(oz == zi, A, oz)
            send = n["az" + name].at[at + (oy * (A + 1) if kind == CROSS else 0)]
        return rcopy(u, u, send, n["ar" + name].at[oy if kind == PROJ else oz * B + oy], hop[d])

    def va_copy(source, oz):
        u = wunit(W[VEC], VEC, source, yi)
        return rcopy(
            u, u, n["azv"].at[oz], n["arv"].at[source * B + yi], (c, oz * B + yi)
        )

    def va_start():
        for oz in range(A):
            when(zi != oz, lambda oz=oz: va_copy(zi, oz).start())
        for d in (2, 3):
            when(edge[d], lambda d=d: ag_copy(VEC, zi, yi, d).start())

    def va_z():
        for i in range(1, A):
            oz = (zi + i) % A
            va_copy(oz, zi).wait_recv()
            for d in (2, 3):
                when(edge[d], lambda d=d, oz=oz: ag_copy(VEC, oz, yi, d).start())

    def va_drain():
        for oz in range(A):
            when(zi != oz, lambda oz=oz: va_copy(zi, oz).wait_send())
        for oz in range(A):
            for oy in range(B):
                when(both(oy <= yi, edge[2]), lambda oz=oz, oy=oy: ag_copy(VEC, oz, oy, 2).wait_send())
                when(both(oy >= yi, edge[3]), lambda oz=oz, oy=oy: ag_copy(VEC, oz, oy, 3).wait_send())

    def ag_start(kind):
        for d in range(4):
            when(both(has(kind, zi), edge[d]), lambda d=d: ag_copy(kind, zi, yi, d).start())

    def ag_z(kind, t):
        for i in range(B if kind == CROSS else 1):
            oy = (yi + i) % B if i else yi
            for sign, d in ((-1, 0), (1, 1)):
                oz = zi + sign * (1 + t)

                def go(oz=oz, d=d, oy=oy):
                    ag_copy(kind, oz, oy, d).wait_recv()
                    for dd in (d,) if kind == CROSS else (d, 2, 3):
                        when(edge[dd], lambda dd=dd: ag_copy(kind, oz, oy, dd).start())

                when(both(oz >= 0, oz < A, has(kind, oz)), go)

    def ag_y(kind):
        for t in range(B - 1):
            for zz in {PROJ: [c], CROSS: [zi]}.get(kind, list(range(A))):
                for sign, d in ((-1, 2), (1, 3)):
                    oy = yi + sign * (1 + t)

                    def go(oy=oy, d=d, zz=zz):
                        ag_copy(kind, zz, oy, d).wait_recv()
                        onward = ([d] if B > 2 else []) + ([0, 1] if kind == CROSS else [])
                        for dd in onward:
                            when(edge[dd], lambda dd=dd: ag_copy(kind, zz, oy, dd).start())

                    when(both(oy >= 0, oy < B), go)

    def ag_drain(kind):
        for oz in [c] if kind == PROJ else list(range(A)):
            for oy in range(B) if kind == CROSS else [yi]:
                when(both(oz <= zi, edge[0]), lambda oz=oz, oy=oy: ag_copy(kind, oz, oy, 0).wait_send())
                when(both(oz >= zi, edge[1]), lambda oz=oz, oy=oy: ag_copy(kind, oz, oy, 1).wait_send())
        for oz in {PROJ: [c], CROSS: [zi]}.get(kind, list(range(A))):
            for oy in range(B):
                when(both(oy <= yi, edge[2]), lambda oz=oz, oy=oy: ag_copy(kind, oz, oy, 2).wait_send())
                when(both(oy >= yi, edge[3]), lambda oz=oz, oy=oy: ag_copy(kind, oz, oy, 3).wait_send())

    XA = ((n["Xs"], T), (n["Gs"], T), (n["Bs"], 8))

    def xa_copy(arr, slot, which):
        ref, r = XA[arr]
        u = rows(ref, slot * r, r)
        return rcopy(u, u, n["xa_s"].at[arr, which], n["xa_r"].at[arr, slot], (xn, sib)[which != 0])

    def xa_start(arr):
        xa_copy(arr, c, 0).start()
        xa_copy(arr, c, 1).start()

    def xa_wait(arr, slot):
        xa_copy(arr, slot, 0).wait_recv()

    def xa_fwd(arr):
        xa_wait(arr, xn_c)
        xa_copy(arr, xn_c, 2).start()

    def xa_drain(arr):
        xa_copy(arr, c, 0).wait_send()
        xa_copy(arr, c, 1).wait_send()
        xa_copy(arr, xn_c, 2).wait_send()

    GR = [n.get("G" + x) for x in s.buffer]
    YB = [n.get("Y" + x) for x in NAMES]
    ZB = [n.get("Z" + x) for x in NAMES]

    def add_into(dst, src):
        dst[...] = (dst[...].astype(F32) + src[...].astype(F32)).astype(dst.dtype)

    def ry_slot(kind, zz, target, d, receiver):
        r = s.rows[kind]
        per = 1 if kind in (PROJ, CROSS) else A
        at = 0 if per == 1 else zz
        if B == 2:
            slot = 0
        elif d == 0:
            slot = target
        else:
            slot = jnp.where(receiver == target, B, target)
        return rows(YB[kind], (slot * per + at) * r, r)

    def ry_copy(kind, zz, target, d, receiver):
        at = along_y(kind, zz, target, d)
        return rcopy(
            wunit(GR[kind], kind, zz, target),
            ry_slot(kind, zz, target, d, receiver),
            n["ys" + NAMES[kind]].at[at],
            n["yr" + NAMES[kind]].at[at],
            hop[2 + d],
        )

    pair_z = zi + 1 - 2 * (zi % 2)
    far_z = (zi + A // 2) % A
    diag_z = (pair_z + A // 2) % A
    by_step = [diag_z, pair_z, far_z, zi]

    def ry_zz(kind):
        return {PROJ: [c], CROSS: [zi], VEC: [zi]}.get(kind, by_step)

    def ry_send(kind, t, zz):
        hi, lo = B - 1 - t, t
        when(yi == 0, lambda: ry_copy(kind, zz, hi, 0, yi + 1).start())
        when(yi == B - 1, lambda: ry_copy(kind, zz, lo, 1, yi - 1).start())

    def ry_recv(kind, t, zz):
        hi, lo = B - 1 - t, t
        for target, d, cond, onward in (
            (hi, 0, both(yi > 0, yi <= hi), both(yi > 0, yi < hi)),
            (lo, 1, both(yi < B - 1, yi >= lo), both(yi < B - 1, yi > lo)),
        ):

            def go(target=target, d=d):
                ry_copy(kind, zz, target, d, yi).wait_recv()
                add_into(wunit(GR[kind], kind, zz, target), ry_slot(kind, zz, target, d, yi))

            when(cond, go)
            if B > 2:
                when(
                    onward,
                    lambda target=target, d=d: ry_copy(
                        kind, zz, target, d, yi + 1 - 2 * d
                    ).start(),
                )

    def ry_drain(kind):
        for zz in {PROJ: [c], CROSS: [zi], VEC: [zi]}.get(kind, list(range(A))):
            for target in range(B):
                when(yi < target, lambda zz=zz, target=target: ry_copy(kind, zz, target, 0, yi + 1).wait_send())
                when(yi > target, lambda zz=zz, target=target: ry_copy(kind, zz, target, 1, yi - 1).wait_send())

    def rz_cols(kind):
        return [(yi + i) % B for i in range(B)] if kind == CROSS else [yi]

    def rz_slot(kind, which, col):
        r = s.rows[kind]
        return rows(ZB[kind], (which * B + col if kind == CROSS else which) * r, r)

    def rz_copy(kind, which, col):
        at = which * B + col if kind == CROSS else which
        return rcopy(
            wunit(GR[kind], kind, by_step[which], col),
            rz_slot(kind, which, col),
            n["zs" + NAMES[kind]].at[at],
            n["zr" + NAMES[kind]].at[at],
            (c, (pair_z, pair_z, far_z)[which] * B + yi),
        )

    def rz_take(kind, which, target, col):
        rz_copy(kind, which, col).wait_recv()
        add_into(wunit(GR[kind], kind, target, col), rz_slot(kind, which, col))

    def rz_pair(kind, which):
        def go():
            for col in rz_cols(kind):
                rz_copy(kind, which, col).start()

        when(has(kind, by_step[which]), go)

    def rz_far(kind):
        def go():
            for col in rz_cols(kind):
                rz_take(kind, 0, far_z, col)
                rz_copy(kind, 2, col).start()

        when(has(kind, far_z), go)

    def rz_sum(kind):
        def go():
            for col in rz_cols(kind):
                rz_take(kind, 1, zi, col)
                rz_take(kind, 2, zi, col)

        when(has(kind, zi), go)

    def rz_drain(kind):
        for which in range(3):

            def go(which=which):
                for col in rz_cols(kind):
                    rz_copy(kind, which, col).wait_send()

            when(has(kind, by_step[which]), go)

    def ry_first(kind):
        for t in range(B - 2):
            for zz in ry_zz(kind):
                if t:
                    ry_send(kind, t, zz)
                ry_recv(kind, t, zz)
        if B > 2:
            for zz in ry_zz(kind):
                ry_send(kind, B - 2, zz)

    def ry_start(kind):
        if kind in s.kinds:
            for zz in ry_zz(kind):
                ry_send(kind, 0, zz)

    def if_kind(kind, fn, *args):
        if kind in s.kinds:
            fn(kind, *args)

    def ry_unit(kind, i):
        if i == 0:
            ry_first(kind)
        ry_recv(kind, B - 2, by_step[i])
        if i < 2:
            rz_pair(kind, i)

    def vs_copy(source, target):
        return rcopy(
            rows(GR[VEC], target * B * VROWS, B * VROWS),
            rows(ZB[VEC], source * B * VROWS, B * VROWS),
            n["zsv"].at[target],
            n["zrv"].at[source],
            (c, target * B + yi),
        )

    def vs_start():
        for i in range(1, A):
            vs_copy(zi, (zi + i) % A).start()

    def vs_sum():
        mine = rows(GR[VEC], zi * B * VROWS, B * VROWS)
        for i in range(1, A):
            source = (zi + i) % A
            vs_copy(source, zi).wait_recv()
            add_into(mine, rows(ZB[VEC], source * B * VROWS, B * VROWS))

    def vs_drain():
        for i in range(1, A):
            vs_copy(zi, (zi + i) % A).wait_send()

    def ry_vec():
        ry_first(VEC)
        ry_recv(VEC, B - 2, zi)

    def ry_cross():
        ry_first(CROSS)
        ry_recv(CROSS, B - 2, zi)

    def ry_proj():
        ry_first(PROJ)
        ry_recv(PROJ, B - 2, c)
        rz_pair(PROJ, 0)
        rz_pair(PROJ, 1)

    def fa_has(kind, slot):
        return (zi == slot) if kind == PROJ else (c == c)

    def fa_dst(kind, slot):
        if kind == VEC:
            return rows(n["FV"], slot * VROWS, VROWS)
        if kind == PROJ:
            return n["out_p"]
        out = n["out_" + s.buffer[kind]]
        if s.buffer[kind] == "d":
            return rows(out, slot * s.hc + s.offset[kind], s.rows[kind])
        return out.at[slot, pl.ds(s.offset[kind], s.rows[kind])]

    def fa_copy(kind, slot, which):
        src = wunit(GR[kind], kind, zi, yi) if which < 2 else fa_dst(kind, slot)
        return rcopy(
            src, fa_dst(kind, slot), n["fa_s"].at[kind, which], n["fa_r"].at[kind, which], (sib, xn, sib)[which]
        )

    def fa_local(kind):
        return pltpu.make_async_copy(wunit(GR[kind], kind, zi, yi), fa_dst(kind, c), n["fa_l"].at[kind])

    def each(copies, what):
        for copy in copies:
            getattr(copy, what)()

    def fa_start(kind):
        def go():
            fa_copy(kind, c, 1).start()
            fa_copy(kind, c, 0).start()
            fa_local(kind).start()

        when(fa_has(kind, c), go)

    def fa_fwd(kind):
        def go():
            fa_copy(kind, xn_c, 1).wait_recv()
            fa_copy(kind, xn_c, 2).start()

        when(fa_has(kind, xn_c), go)

    def fa_end(kind):
        when(fa_has(kind, sib_c), lambda: fa_copy(kind, sib_c, 0).wait_recv())
        when(fa_has(kind, xs_c), lambda: fa_copy(kind, xs_c, 2).wait_recv())

        def own():
            fa_copy(kind, c, 1).wait_send()
            fa_copy(kind, c, 0).wait_send()
            fa_local(kind).wait()

        when(fa_has(kind, c), own)
        when(fa_has(kind, xn_c), lambda: fa_copy(kind, xn_c, 2).wait_send())

    PC = (n["Po"], n["Pc"])

    def cr_copy(arr, which, slot):
        if which < 2:
            return rcopy(
                rows(PC[arr], slot * T, T),
                n["r1"].at[arr, pl.ds(which * T, T)],
                n["cr_s"].at[arr, which],
                n["cr_r"].at[arr, which],
                sib,
            )
        return rcopy(rows(PC[arr], slot * T, T), n["r2"].at[arr], n["cr_s"].at[arr, 2], n["cr_r"].at[arr, 2], xn)

    def cr_start(arr):
        cr_copy(arr, 1, xs_c).start()
        cr_copy(arr, 0, sib_c).start()

    def cr_mid(arr):
        cr_copy(arr, 1, xs_c).wait_recv()
        add_into(rows(PC[arr], xn_c * T, T), n["r1"].at[arr, pl.ds(T, T)])
        cr_copy(arr, 2, xn_c).start()

    def cr_wait(arr):
        cr_copy(arr, 0, sib_c).wait_recv()
        cr_copy(arr, 2, xn_c).wait_recv()

    def cr_drain(arr):
        cr_copy(arr, 1, xs_c).wait_send()
        cr_copy(arr, 0, sib_c).wait_send()
        cr_copy(arr, 2, xn_c).wait_send()

    vecs, cos, sin = n["vecs"], n["cos"], n["sin"]

    def vec(row, width=D):
        return vecs[row : row + 1, 0:width]

    def loop(count, fn, first=0):
        def step(i, carry):
            fn(i)
            return carry

        lax.fori_loop(first, count, step, 0)

    def tile(ref, start, size, cols=slice(None)):
        return ref[pl.ds(mult(start, size), size), cols]

    def here(j, k, width):
        at = 8 * (j // 2) + j % 2
        return jnp.where(n["Bs"][at : at + 1, 0:width] == k, 1.0, 0.0)

    def to_order(dst, src):
        def one(k):
            total = None
            for j in range(2 * s.nctx):
                w = here(j, k, src.shape[1]).astype(src.dtype)
                term = src[j * BLK : (j + 1) * BLK, :] * w
                total = term if total is None else total + term
            dst[pl.ds(mult(k * BLK, BLK), BLK), :] = total

        loop(2 * s.nctx, one)

    def from_order(src, put):
        for j in range(2 * s.nctx):
            total = None
            for k in range(2 * s.nctx):
                w = here(j, k, src.shape[1]).astype(src.dtype)
                term = src[k * BLK : (k + 1) * BLK, :] * w
                total = term if total is None else total + term
            put(slice(j * BLK, (j + 1) * BLK), total)

    def norms(slot):
        def one(i):
            at = pl.ds(mult(slot * T + i * BLK, BLK), BLK)
            x = n["Xs"][at, :].astype(F32)
            center = x - jnp.mean(x, axis=-1, keepdims=True)
            nn = center * lax.rsqrt(jnp.mean(center * center, axis=-1, keepdims=True) + EPS)
            n["nb"][at, :] = nn.astype(BF)
            n["A1"][at, :] = (nn * vec(0) + vec(1)).astype(BF)
            n["A2"][at, :] = (nn * vec(2) + vec(3)).astype(BF)

        loop(T // BLK, one)

    lane64 = lax.broadcasted_iota(jnp.int32, (T, 128), 1) % HEAD_DIM
    first_half = lane64 < ROT // 2

    def rope(u, cs_, sn_, sign):
        partner = jnp.where(first_half, pltpu.roll(u, 128 - ROT // 2, 1), pltpu.roll(u, ROT // 2, 1))
        return u * cs_ + (partner * sn_) * sign

    def tables():
        def put(name):
            def store(at, value):
                n[name][at, :] = value

            return store

        from_order(cos, put("cos_st"))
        from_order(sin, put("sin_st"))

    raw, S = n["Pc"], n["S"]

    def qkv():
        def one(i):
            at = pl.ds(mult(i * T, T), T)
            j = dot(n["A1"][at, :], n["Wi"][...]) + vec(7, 3 * G)
            cs_, sn_ = n["cos_st"][at, :], n["sin_st"][at, :]
            for p in range(G // 128):
                lo = 128 * p
                q = rope(j[:, lo : lo + 128], cs_, sn_, 1.0).astype(BF)
                raw[at, lo : lo + 128] = (q.astype(F32) * HEAD_DIM**-0.5).astype(BF)
                raw[at, G + lo : G + lo + 128] = rope(j[:, G + lo : G + lo + 128], cs_, sn_, 1.0).astype(BF)
            raw[at, 2 * G : 3 * G] = j[:, 2 * G : 3 * G].astype(BF)

        loop(N // T, one)

    def dattended():
        def one(i):
            at = pl.ds(mult(i * T, T), T)
            raw[at, 3 * G : 4 * G] = dot11(n["Gs"][at, :], n["Wp"][...]).astype(BF)

        loop(N // T, one)

    def order():
        to_order(S, raw)

    def zero_dkv():
        n["dk"][...] = jnp.zeros((N, G), F32)
        n["dv"][...] = jnp.zeros((N, G), F32)

    def attention(p, i):
        L = (i + 1) * T
        cols = slice(128 * p, 128 * p + 128)
        at = slice(i * T, i * T + T)
        part = [slice(j * G + 128 * p, j * G + 128 * p + 128) for j in range(4)]
        kb, vb = S[0:L, part[1]], S[0:L, part[2]]
        qb, db = S[at, part[0]], S[at, part[3]]
        lane = lax.broadcasted_iota(jnp.int32, (T, 128), 1)
        key_at = lax.broadcasted_iota(jnp.int32, (T, T), 0)
        query_at = lax.broadcasted_iota(jnp.int32, (T, T), 1)
        keep = key_at <= query_at
        outs, dqs, ps, ds_, qs, dbs = [], [], [], [], [], []
        for h in range(2):
            mine = (lane >= HEAD_DIM) if h else (lane < HEAD_DIM)
            qh = jnp.where(mine, qb, jnp.zeros_like(qb))
            dh = jnp.where(mine, db, jnp.zeros_like(db))
            sc = dot11(kb, qh)
            last = jnp.where(keep, sc[L - T :], -1e30)
            sc = last if i == 0 else jnp.concatenate([sc[: L - T], last], axis=0)
            e = jnp.exp(sc - jnp.max(sc, axis=0, keepdims=True))
            pr = e * (1.0 / jnp.sum(e, axis=0, keepdims=True))
            dp = dot11(vb, dh)
            delta = jnp.sum(pr * dp, axis=0, keepdims=True)
            dsl = (pr * (dp - delta)).astype(BF)
            pb = pr.astype(BF)
            outs.append(dot00(vb, pb))
            dqs.append(dot00(kb, dsl))
            n["dv"][0:L, cols] += dot(pb, dh)
            n["dk"][0:L, cols] += dot(dsl, qh)
        feature = lax.broadcasted_iota(jnp.int32, (128, T), 0)
        raw[at, part[3]] = jnp.where(feature < HEAD_DIM, outs[0], outs[1]).T.astype(BF)
        n["dq"][at, cols] = jnp.where(feature < HEAD_DIM, dqs[0], dqs[1]).T * HEAD_DIM**-0.5

    def joined_back():
        n["cs"][2:3, :] = jnp.zeros((1, D), F32)

        def one(i):
            at = pl.ds(mult(i * T, T), T)
            cs_, sn_ = cos[at, :], sin[at, :]
            for p in range(G // 128):
                cols = slice(128 * p, 128 * p + 128)
                for j, (name, turn) in enumerate((("dq", True), ("dk", True), ("dv", False))):
                    u = n[name][at, cols]
                    if turn:
                        u = rope(u, cs_, sn_, -1.0)
                    u = u.astype(BF)
                    lo = j * G + 128 * p
                    raw[at, lo : lo + 128] = u
                    n["cs"][2:3, lo : lo + 128] += jnp.sum(u.astype(F32), axis=0, keepdims=True)

        loop(N // T, one)

        def put(at, value):
            n["dj"][at, :] = value[:, 0 : 3 * G]
            n["att_st"][at, :] = value[:, 3 * G : 4 * G]

        from_order(raw, put)

    def in_grad():
        def one(i):
            at = pl.ds(mult(i * 256, 256), 256)
            n["Gi"][at, :] = dot00(n["A1"][:, at], n["dj"][...]).astype(BF)

        loop(D // 256, one)

    def proj_grad():
        def one(i):
            at = pl.ds(mult(i * 256, 256), 256)
            n["Gp"][:, at] = dot00(n["att_st"][...], n["Gs"][:, at]).astype(BF)

        loop(D // 256, one)

    def mlp_up(part):
        def one(i):
            at = pl.ds(mult((i // 4) * T, T), T)
            cols = pl.ds(mult((i % 4) * 256, 256), 256)
            x = dot(n["A2"][at, :], n["Wu"][:, cols]) + vecs[6:7, cols]
            phi = 0.5 + 0.5 * lax.erf(x * math.sqrt(0.5))
            pdf = jnp.exp(-0.5 * x * x) * (1.0 / math.sqrt(2.0 * math.pi))
            n["act"][at, cols] = (x * phi).astype(BF)
            n["gp"][at, cols] = (phi + x * pdf).astype(BF)

        loop(4 * part + 4, one, 4 * part)

    def down_grad(part):
        def one(i):
            at = pl.ds(mult(i * 256, 256), 256)
            n["Gd"][at, :] = dot00(n["act"][:, at], n["Gs"][...]).astype(BF)

        loop(H // 512 * (part + 1), one, H // 512 * part)

    def mlp_back(part):
        if part == 0:
            n["cs"][6:7, :] = jnp.zeros((1, D), F32)

        def one(i):
            at = pl.ds(mult((i // 4) * T, T), T)
            cols = pl.ds(mult((i % 4) * 256, 256), 256)
            da = dot11(n["Gs"][at, :], n["Wd"][cols, :])
            dl = (da * n["gp"][at, cols].astype(F32)).astype(BF)
            n["dl"][at, cols] = dl
            n["cs"][6:7, cols] += jnp.sum(dl.astype(F32), axis=0, keepdims=True)

        loop(4 * part + 4, one, 4 * part)

    def up_grad(part):
        def one(i):
            at = pl.ds(mult(i * 256, 256), 256)
            n["Gu"][at, :] = dot00(n["A2"][:, at], n["dl"][...]).astype(BF)

        loop(D // 512 * (part + 1), one, D // 512 * part)

    def out_part():
        def one(i):
            at = pl.ds(mult(i * T, T), T)
            n["Po"][at, :] = (dot(n["att_st"][at, :], n["Wp"][...]) + dot(n["act"][at, :], n["Wd"][...])).astype(BF)

        loop(N // T, one)

    def input_part():
        for row in (0, 1, 4, 5):
            n["cs"][row : row + 1, :] = jnp.zeros((1, D), F32)

        def one(i):
            at = pl.ds(mult(i * T, T), T)
            nn = n["nb"][at, :].astype(F32)
            e1 = dot11(n["dj"][at, :], n["Wi"][...])
            n["cs"][0:1, :] += jnp.sum(e1 * nn, axis=0, keepdims=True)
            n["cs"][1:2, :] += jnp.sum(e1, axis=0, keepdims=True)
            e2 = dot11(n["dl"][at, :], n["Wu"][...])
            n["cs"][4:5, :] += jnp.sum(e2 * nn, axis=0, keepdims=True)
            n["cs"][5:6, :] += jnp.sum(e2, axis=0, keepdims=True)
            n["Pc"][at, :] = (e1 * vec(0) + e2 * vec(2)).astype(BF)

        loop(N // T, one)

    def own_g_sum():
        n["cs"][7:8, :] = jnp.zeros((1, D), F32)
        g = tile(n["Gs"], c * T, T).astype(F32)
        n["cs"][3:4, :] = jnp.sum(g, axis=0, keepdims=True)

    def finish_out():
        base = c * T
        x = tile(n["Xs"], base, T).astype(F32)
        total = tile(n["Po"], base, T).astype(F32) + n["r1"][0, 0:T].astype(F32) + n["r2"][0].astype(F32)
        n["xo"][...] = (x + total + vec(4) + vec(5)).astype(BF)

    def finish_input():
        base = c * T
        x = tile(n["Xs"], base, T).astype(F32)
        center = x - jnp.mean(x, axis=-1, keepdims=True)
        rstd = lax.rsqrt(jnp.mean(center * center, axis=-1, keepdims=True) + EPS)
        nn = center * rstd
        cc = tile(n["Pc"], base, T).astype(F32) + n["r1"][1, 0:T].astype(F32) + n["r2"][1].astype(F32)
        mean_c = jnp.mean(cc, axis=-1, keepdims=True)
        mean_cn = jnp.mean(cc * nn, axis=-1, keepdims=True)
        n["xg"][...] = tile(n["Gs"], base, T).astype(F32) + (cc - mean_c - nn * mean_cn) * rstd

    def unpack_vectors():
        for j in range(s.F):
            cols = slice(j * 128, (j + 1) * 128)
            n["vecs"][0:6, cols] = n["Wv"][j * VROWS : j * VROWS + 6, :]
            n["vecs"][6:7, cols] = n["Wv"][pl.ds(j * VROWS + 6 + c, 1), :]
        per = G // 128
        for j in range(3):
            for p in range(per):
                b = j * (D // 128) + c * per + p
                lo = (j * per + p) * 128
                n["vecs"][7:8, lo : lo + 128] = n["Wv"][pl.ds((b // 3) * VROWS + 6 + s.nctx + b % 3, 1), :]

    def pack_sums():
        n["Gv"][...] = jnp.zeros((s.F * VROWS, 128), F32)
        cs = n["cs"]
        for j in range(s.F):
            cols = slice(j * 128, (j + 1) * 128)
            base = j * VROWS
            for row, place in ((0, 0), (1, 1), (3, 5), (4, 6), (5, 7)):
                n["Gv"][base + place : base + place + 1, :] = cs[row : row + 1, cols]
            n["Gv"][pl.ds(base + 8 + c, 1), :] = cs[6:7, cols]
        per = G // 128
        for j in range(3):
            for p in range(per):
                b = j * (D // 128) + c * per + p
                lo = (j * per + p) * 128
                n["Gv"][pl.ds((b // 3) * VROWS + 2 + b % 3, 1), :] = cs[2:3, lo : lo + 128]

    def local(i, src, dst):
        return pltpu.make_async_copy(src, dst, n["loc"].at[i])

    own_i = rows(n["Wi"], (zi * B + yi) * R, R)
    own_u = wunit(W[UP], UP, zi, yi)
    hc = s.hc
    lc = {
        "x": [local(0, n["x"], rows(n["Xs"], c * T, T))],
        "i": [
            pltpu.make_async_copy(
                n["w_i"].at[:, pl.ds(mult(j * D + c * G, 128), G)], own_i.at[:, pl.ds(j * G, G)], n["loc_i"].at[j]
            )
            for j in range(3)
        ],
        "p": [local(3, n["w_p"], wunit(W[PROJ], PROJ, zi, yi))],
        "g": [local(4, n["g"], rows(n["Gs"], c * T, T))],
        "u": [local(5, n["w_u"], own_u)]
        if not s.packed
        else [
            pltpu.make_async_copy(
                n["w_u"].at[:, pl.ds(mult((j * s.nctx + c) * hc, 128), hc)],
                own_u.at[:, pl.ds(j * hc, hc)],
                n["loc_u"].at[j],
            )
            for j in range(s.F)
        ],
        "d": [local(6, rows(n["w_d"], c * hc, hc), rows(n["Wd"], (zi * B + yi) * hc, hc))],
    }
    if s.packed:
        lc["v"] = [
            pltpu.make_async_copy(n[f"vec{i}"], n[f"vin{i}"], n["loc_v"].at[i]) for i in range(len(s.vector_rows))
        ]

    def lstart(key):
        if key == "p":
            when(zi == c, lambda: each(lc[key], "start"))
        else:
            each(lc[key], "start")

    def lwait(key):
        if key == "p":
            when(zi == c, lambda: each(lc[key], "wait"))
        else:
            each(lc[key], "wait")

    for key in lc:
        lstart(key)
    bar = pltpu.get_barrier_semaphore()
    for dev in (sib, xn):
        pl.semaphore_signal(bar, inc=1, device_id=dev, device_id_type=MESH)
    for step in range(1, A):
        pl.semaphore_signal(bar, inc=1, device_id=(c, (zi + step) % A * B + yi), device_id_type=MESH)
    for d in (2, 3):
        when(
            edge[d],
            lambda d=d: pl.semaphore_signal(bar, inc=1, device_id=hop[d], device_id_type=MESH),
        )
    count = 2 + A - 1 + sum(jnp.where(e, 1, 0) for e in edge[2:])
    pl.semaphore_wait(bar, count)

    for key in lc:
        if key != "p":
            lwait(key)
    lwait("p")

    def blocks_start():
        for j in range(T // BLK):
            first = n["places"][0:1, j * BLK : j * BLK + 1] // BLK
            n["Bs"][pl.ds(c * 8 + j, 1), :] = jnp.broadcast_to(first, (1, D))
        xa_start(2)

    def vectors_start():
        if s.packed:
            at = (zi * B + yi) * VROWS
            for i, count in enumerate(s.vector_rows):
                for j in range(count):
                    n["Wv"][pl.ds(at, 1), :] = n[f"vin{i}"][j * 128 : (j + 1) * 128].astype(F32).reshape(1, 128)
                    at = at + 1
            va_start()

    def vectors_z():
        if s.packed:
            va_z()

    def vectors_y():
        if s.packed:
            ag_y(VEC)
            unpack_vectors()

    def sums_start():
        if s.packed:
            pack_sums()
            vs_start()

    def sums_y():
        if s.packed:
            vs_sum()
            ry_send(VEC, 0, zi)

    def sums_end():
        if s.packed:
            ry_vec()
            fa_start(VEC)

    def sums_fwd():
        if s.packed:
            fa_fwd(VEC)

    def cross_pair():
        rz_pair(CROSS, 0)
        rz_pair(CROSS, 1)

    def cross_y():
        rz_sum(CROSS)
        ry_send(CROSS, 0, zi)

    def cross_end():
        ry_cross()
        fa_start(CROSS)

    def done(kind):
        rz_sum(kind)
        fa_start(kind)

    put_out = local(12, n["xo"], n["out"])
    put_in = local(13, n["xg"], n["input_grad"])

    def store_out():
        cr_wait(0)
        finish_out()
        put_out.start()

    def store_input():
        cr_wait(1)
        finish_input()
        put_in.start()

    vectors_start()
    own_g_sum()
    ag_start(IN)
    xa_start(0)
    ag_start(PROJ)
    vectors_z()
    blocks_start()
    ag_z(IN, 0)
    ag_z(PROJ, 0)
    xa_start(1)
    xa_fwd(0)
    ag_z(IN, 1)
    xa_wait(0, sib_c)
    vectors_y()
    norms(xn_c)
    xa_fwd(2)
    xa_wait(1, sib_c)
    ag_z(PROJ, 1)
    ag_z(IN, 2)
    xa_wait(2, xs_c)
    ag_start(CROSS)
    zero_dkv()
    xa_wait(0, xs_c)
    norms(c)
    xa_wait(2, sib_c)
    ag_z(PROJ, 2)
    ag_start(UP)
    norms(sib_c)
    tables()
    norms(xs_c)
    xa_fwd(1)
    ag_start(DOWN)
    ag_y(IN)
    qkv()
    xa_wait(1, xs_c)
    ag_y(PROJ)
    dattended()
    order()
    ag_z(UP, 0)
    attention(0, 0)
    attention(0, 1)
    attention(0, 2)
    ag_y(CROSS)
    attention(0, 3)
    ag_z(UP, 1)
    attention(1, 0)
    attention(1, 1)
    attention(1, 2)
    ag_z(CROSS, 0)
    ag_z(UP, 2)
    attention(1, 3)
    joined_back()
    proj_grad()
    ag_z(CROSS, 1)
    ry_start(PROJ)
    ag_z(DOWN, 0)
    ag_y(UP)
    mlp_up(0)
    mlp_up(1)
    mlp_up(2)
    mlp_up(3)
    ag_z(DOWN, 1)
    down_grad(0)
    ry_proj()
    ag_z(DOWN, 2)
    down_grad(1)
    cross_pair()
    ag_z(CROSS, 2)
    ry_start(DOWN)
    ag_y(DOWN)
    in_grad()
    out_part()
    rz_far(PROJ)
    mlp_back(0)
    ry_unit(DOWN, 0)
    mlp_back(1)
    mlp_back(2)
    ry_start(PIECE)
    cr_start(0)
    mlp_back(3)
    rz_far(CROSS)
    up_grad(0)
    cr_mid(0)
    up_grad(1)
    ry_unit(DOWN, 1)
    ry_start(UP)
    if_kind(PIECE, ry_unit, 0)
    if_kind(PIECE, ry_unit, 1)
    ry_unit(DOWN, 2)
    rz_far(DOWN)
    input_part()
    ry_unit(UP, 0)
    cr_start(1)
    done(PROJ)
    if_kind(PIECE, ry_unit, 2)
    if_kind(PIECE, rz_far)
    ry_unit(DOWN, 3)
    cr_mid(1)
    ry_unit(UP, 1)
    ry_unit(UP, 2)
    rz_far(UP)
    cross_y()
    ry_start(IN)
    done(DOWN)
    if_kind(PIECE, ry_unit, 3)
    ry_unit(UP, 3)
    cross_end()
    sums_start()
    ry_unit(IN, 0)
    if_kind(PIECE, done)
    ry_unit(IN, 1)
    done(UP)
    ry_unit(IN, 2)
    fa_fwd(DOWN)
    rz_far(IN)
    sums_y()
    ry_unit(IN, 3)
    fa_fwd(PROJ)
    store_input()
    done(IN)
    store_out()
    sums_end()
    fa_fwd(CROSS)
    if_kind(PIECE, fa_fwd)
    fa_fwd(UP)
    fa_fwd(IN)
    sums_fwd()
    for kind in s.kinds:
        fa_end(kind)
    if s.packed:
        n["vtot"][...] = sum(n["FV"][j * VROWS : (j + 1) * VROWS, :] for j in range(s.nctx))
    put_cs = local(14, n["vtot"] if s.packed else n["cs"], n["sums"])
    put_cs.start()
    for kind in s.kinds:
        ry_drain(kind)
        if kind == VEC:
            va_drain()
            vs_drain()
        else:
            if kind in s.gathered:
                ag_drain(kind)
            rz_drain(kind)
    for arr in range(3):
        xa_drain(arr)
    for arr in range(2):
        cr_drain(arr)
    put_out.wait()
    put_in.wait()
    put_cs.wait()


def finish_kernel(s, hidden, *refs):
    gi, gp, gu, gd, out, input_grad, sums = refs[:7]
    to = refs[7:]
    to[0][...] = out[...]
    to[1][...] = input_grad[...]
    for slot in range(s.nctx):
        for j in range(3):
            lo = j * s.D + slot * s.G
            to[2][:, lo : lo + s.G] = gi[slot, :, j * s.G : (j + 1) * s.G].astype(F32)
        for j in range(s.F):
            lo = (j * s.nctx + slot) * s.hc
            to[4][:, lo : lo + s.hc] = gu[slot, :, j * s.hc : (j + 1) * s.hc].astype(F32)
    to[3][...] = gp[...].astype(F32)
    to[5][...] = gd[...].astype(F32)
    singles = ((0, 6), (1, 7), (5, 8), (6, 9), (7, 10), (5, 11))
    for row, at in singles:
        to[at][...] = sums[row, :]
    for first, count, at in ((2, 3, 12), (8, s.nctx, 13)):
        for j in range(count):
            to[at][j * 128 : (j + 1) * 128] = sums[first + j, :]


def finish(s, hidden, arrays):
    steps = max(1, s.R // 64)

    def part(shape):
        if len(shape) == 3:
            return pl.BlockSpec((shape[0], shape[1] // steps, shape[2]), lambda i: (0, i, 0))
        return pl.BlockSpec((shape[0] // steps, shape[1]), lambda i: (i, 0))

    def whole(shape):
        return pl.BlockSpec(shape, lambda i: (0,) * len(shape))

    D = s.D
    shapes = [(s.T, D), (s.T, D), (s.R, 3 * D), (s.R, D), (s.R, hidden), (hidden // s.F, D)]
    types = [BF, F32, F32, F32, F32, F32]
    small = [(128,)] * 6 + [(3 * s.R,), (hidden // s.F,)]
    return pl.pallas_call(
        lambda *refs: finish_kernel(s, hidden, *refs),
        grid=(steps,),
        out_shape=tuple(jax.ShapeDtypeStruct(sh, dt) for sh, dt in zip(shapes + small, types + [F32] * 8)),
        in_specs=[part(a.shape) for a in arrays[:-1]] + [whole(arrays[-1].shape)],
        out_specs=tuple([part(sh) for sh in shapes] + [whole(sh) for sh in small]),
        compiler_params=pltpu.CompilerParams(vmem_limit_bytes=63 << 20),
        name="finish",
    )(*arrays)


def rope_tables(length):
    half = ROT // 2
    freq = np.power(np.float32(10000.0), np.float32(-2.0) * np.arange(half, dtype=np.float32) / np.float32(ROT))
    angle = np.arange(length, dtype=np.float32)[:, None] * freq[None, :].astype(np.float32)
    cos = np.ones((length, 128), np.float32)
    sin = np.zeros((length, 128), np.float32)
    for base in range(0, 128, HEAD_DIM):
        cos[:, base : base + half] = np.cos(angle)
        cos[:, base + half : base + ROT] = np.cos(angle)
        sin[:, base : base + half] = -np.sin(angle)
        sin[:, base + half : base + ROT] = np.sin(angle)
    return cos, sin


def body(
    hidden_in,
    positions,
    out_grad,
    attn_gain,
    attn_shift,
    in_weight,
    in_bias,
    proj_weight,
    proj_bias,
    mlp_gain,
    mlp_shift,
    up_weight,
    up_bias,
    down_weight,
    down_bias,
):
    nctx, nshard = lax.axis_size("ctx"), lax.axis_size("fsdp")
    T, D = hidden_in.shape[1:]
    hidden = up_weight.shape[1]
    s = Sizes(T, D, hidden, nctx, nshard)
    R, G, F = s.R, s.G, s.F
    hc = s.hc
    c, f = lax.axis_index("ctx"), lax.axis_index("fsdp")

    def pick_ctx(array, axis):
        return lax.dynamic_index_in_dim(array, c, axis, keepdims=False)

    small = [attn_gain, attn_shift, mlp_gain, mlp_shift, proj_bias, down_bias, up_bias, in_bias]
    if s.packed:
        w_u = up_weight
        extra = {f"vec{i}": v for i, v in enumerate(small)}
    else:
        w_u = pick_ctx(up_weight.reshape(R, F, nctx, hc), 2).reshape(R, s.H)
        lengths = [v.shape[0] for v in small]
        gathered = lax.all_gather(jnp.concatenate(small).astype(F32), "fsdp", axis=0)
        full, at = [], 0
        for length in lengths:
            full.append(gathered[:, at : at + length].reshape(-1))
            at += length
        full[6] = pick_ctx(full[6].reshape(F, nctx, hc), 1).reshape(-1)
        full[7] = jnp.pad(pick_ctx(full[7].reshape(3, nctx, G), 1).reshape(-1), (0, D - 3 * G))
        extra = dict(vecs=jnp.stack(full))
    cos, sin = rope_tables(s.N)

    plan = scratch_plan(s)
    any_ = pl.BlockSpec(memory_space=pl.ANY)
    vmem = pl.BlockSpec(memory_space=pltpu.VMEM)
    ins = dict(
        x=hidden_in[0],
        g=out_grad[0],
        places=positions,
        w_i=in_weight,
        w_p=proj_weight,
        w_u=w_u,
        w_d=down_weight,
        **extra,
        cos=jnp.asarray(cos),
        sin=jnp.asarray(sin),
    )
    in_vmem = {"vecs", "cos", "sin", "places"}
    outs = dict(
        out=jax.ShapeDtypeStruct((T, D), BF),
        input_grad=jax.ShapeDtypeStruct((T, D), F32),
        out_i=jax.ShapeDtypeStruct((nctx, R, 3 * G), BF),
        out_p=jax.ShapeDtypeStruct((R, D), BF),
        out_u=jax.ShapeDtypeStruct((nctx, R, s.H), BF),
        out_d=jax.ShapeDtypeStruct((nctx * hc, D), BF),
        sums=jax.ShapeDtypeStruct((VROWS, 128) if s.packed else (8, D), F32),
    )
    names = list(ins) + list(outs) + list(plan)
    out, input_grad, gi, gp, gu, gd, sums = pl.pallas_call(
        lambda *refs: kernel_body(s, names, *refs),
        out_shape=tuple(outs.values()),
        in_specs=[vmem if name in in_vmem else any_ for name in ins],
        out_specs=tuple(any_ for _ in outs),
        scratch_shapes=list(plan.values()),
        compiler_params=pltpu.CompilerParams(
            collective_id=0, has_side_effects=True, vmem_limit_bytes=63 << 20
        ),
        name="block",
    )(*ins.values())

    def own(full_vector):
        length = full_vector.shape[0] // F
        return lax.dynamic_slice_in_dim(full_vector, f * length, length)

    if s.packed:
        done = finish(s, hidden, (gi, gp, gu, gd, out, input_grad, sums))
        out, input_grad, in_total, proj_total, up_total, down_total = done[:6]
        gain1, shift1, g_sum, gain2, shift2, g_again, in_bias_sum, up_bias_sum = done[6:]
    else:
        here = (jnp.arange(nctx) == c).astype(F32)
        in_b = (sums[2, : 3 * G].reshape(3, 1, G) * here[None, :, None]).reshape(-1)
        up_b = (sums[6].reshape(F, 1, hc) * here[None, :, None]).reshape(-1)
        total = lax.psum(
            jnp.concatenate([sums[0], sums[1], in_b, sums[3], sums[4], sums[5], up_b]), ("ctx", "fsdp")
        )
        parts, at = [], 0
        for length in (D, D, 3 * D, D, D, D, hidden):
            parts.append(own(total[at : at + length]))
            at += length
        gain1, shift1, in_bias_sum, g_sum, gain2, shift2, up_bias_sum = parts
        g_again = g_sum
        in_total = gi.astype(F32).reshape(nctx, R, 3, G).transpose(1, 2, 0, 3).reshape(R, 3 * D)
        proj_total, down_total = gp.astype(F32), gd.astype(F32)
        up_total = gu.astype(F32).reshape(nctx, R, F, hc).transpose(1, 2, 0, 3).reshape(R, hidden)
    return (
        out[None],
        input_grad[None],
        gain1,
        shift1,
        in_total,
        in_bias_sum,
        proj_total,
        g_sum,
        gain2,
        shift2,
        up_total,
        up_bias_sum,
        down_total,
        g_again,
    )


def solution(mesh):
    tok, vec, mat = P("fsdp", "ctx", None), P("fsdp"), P("fsdp", None)
    placed = (tok, P("fsdp", "ctx"), tok, vec, vec, mat, vec, mat, vec, vec, vec, mat, vec, mat, vec)
    return jax.shard_map(
        body,
        mesh=mesh,
        in_specs=placed,
        out_specs=(tok, tok, vec, vec, mat, vec, mat, vec, vec, vec, mat, vec, mat, vec),
        check_vma=False,
    )
```
